32 devices in a mesh: fsdp: 2 (over x), ctx: 8 (over z, core), tensor: 2 (over y).
Axes of the slice: x: 2, y: 2, z: 4, core: 2. Of those that a mesh axis runs over, the one named last changes fastest.
Arguments:
- inputs: bfloat16 [2, 8, 1024, 768], P(None, 'fsdp', 'ctx'), may hold values from -6 to 6
- out_grad: bfloat16 [2, 8, 1024, 768], P(None, 'fsdp', 'ctx'), may hold values from -6 to 6
- lengths: int32 [2, 8], P(None, 'fsdp'), may hold values from 256 to 1024, as said below
- routes: int32 [2, 8, 1024], P(None, 'fsdp', 'ctx'), may hold values from 0 to 15
- slots: int32 [2, 8, 1024], P(None, 'fsdp', 'ctx'), may hold values from -1 to 24, as said below
- norm_gains: bfloat16 [2, 768], P(None, ('fsdp', 'ctx')), may hold values from 0.5 to 1.5
- router_matrix: bfloat16 [768, 16], P(('fsdp', 'ctx')), may hold values from -0.109375 to 0.109375
- input_projection: bfloat16 [2, 1536, 768], P(None, ('fsdp', 'ctx', 'tensor')), may hold values from -0.21875 to 0.21875
- inner_projection: bfloat16 [1536, 80], P(('fsdp', 'ctx', 'tensor')), may hold values from -0.15625 to 0.15625
- step_projection: bfloat16 [1536, 48], P(('fsdp', 'ctx', 'tensor')), may hold values from -1.5 to 1.5
- step_bias: bfloat16 [1536], P(('fsdp', 'ctx', 'tensor')), may hold values from -12 to 4
- channel_params: bfloat16 [1536, 22], P(('fsdp', 'ctx', 'tensor')), may hold values from -12 to 4
- output_projection: bfloat16 [1536, 768], P(('fsdp', 'ctx', 'tensor')), may hold values from -1.5 to 1.5
- expert_up: bfloat16 [16, 768, 3072], P(('fsdp', 'ctx'), None, 'tensor'), may hold values from -0.21875 to 0.21875
- expert_down: bfloat16 [16, 3072, 768], P(('fsdp', 'ctx'), 'tensor'), may hold values from -6 to 6
Outputs:
- activations: bfloat16 [2, 8, 1024, 768], P(None, 'fsdp', 'ctx')
- input_grad: float32 [2, 8, 1024, 768], P(None, 'fsdp', 'ctx')
- grad_norm_gains: float32 [2, 768], P(None, ('fsdp', 'ctx'))
- grad_router: float32 [768, 16], P(('fsdp', 'ctx'))
- grad_in_proj: float32 [2, 1536, 768], P(None, ('fsdp', 'ctx', 'tensor'))
- grad_x_proj: float32 [1536, 80], P(('fsdp', 'ctx', 'tensor'))
- grad_dt_proj: float32 [1536, 48], P(('fsdp', 'ctx', 'tensor'))
- grad_step_bias: float32 [1536], P(('fsdp', 'ctx', 'tensor'))
- grad_channel: float32 [1536, 22], P(('fsdp', 'ctx', 'tensor'))
- grad_out_proj: float32 [1536, 768], P(('fsdp', 'ctx', 'tensor'))
- grad_expert_up: float32 [16, 768, 3072], P(('fsdp', 'ctx'), None, 'tensor')
- grad_expert_down: float32 [16, 3072, 768], P(('fsdp', 'ctx'), 'tensor')
The draws below stay inside these ranges and needn't reach their ends.
Inputs may be any that keep to these rules, and one draw needn't show every extreme that they name: `lengths`: in every micro-batch and every fsdp index, one of its 4 sequences has length 1024. Padded positions have -1. Among the tokens of one micro-batch on one fsdp index and one ctx index, kept tokens with the same route have distinct slots; in every micro-batch some expert gets all 25 slots from every such group.
All inputs are finite; a program needn't handle non-finite values.
Results may differ from the reference program's by a relative error of at most 0.017.
Values may be sent and summed in bfloat16 or wider, within the bound.
A program may use at most 256 MiB of HBM per device.

```python
import math
import jax
import jax.numpy as jnp
from jax import lax

D = 768
DI = 1536
N = 16
CONV_TAPS = 4
R = 48
FF = 3072
MICRO = 2
SEQ_DEV = 4
LEN = 1024
DEV_LEN = 128
SEQS = 8
EXPERTS = 16
CAP = 25
XW = 80
N_FSDP = 2
N_CTX = 8


def routing_tables(key):
    keys = jax.random.split(jax.random.fold_in(key, 7), 8)
    groups = SEQS // SEQ_DEV
    ranges = LEN // DEV_LEN
    lengths = jax.random.randint(keys[0], (MICRO, groups, SEQ_DEV), LEN // 4, LEN + 1)
    chosen = jax.random.randint(keys[1], (MICRO, groups, 1), 0, SEQ_DEV)
    is_full = jnp.arange(SEQ_DEV)[None, None, :] == chosen
    lengths = jnp.where(is_full, LEN, lengths).reshape(MICRO, SEQS).astype(jnp.int32)
    is_full = is_full.reshape(MICRO, SEQS)
    drawn = jax.random.randint(keys[2], (MICRO, SEQS, LEN), 0, EXPERTS)
    popular = jax.random.randint(keys[3], (MICRO, SEQS, LEN), 0, max(1, EXPERTS // 8))
    picker = jax.random.randint(keys[4], (MICRO, SEQS, LEN), 0, 4) == 0
    order = jax.random.permutation(keys[5], EXPERTS)
    routes = order[jnp.where(picker, popular, drawn)]
    hottest = jax.random.randint(keys[6], (MICRO,), 0, EXPERTS)
    scores = jax.random.randint(keys[7], (MICRO, SEQS, ranges, DEV_LEN), 0, 1 << 20) * DEV_LEN + jnp.arange(DEV_LEN)
    ranking = jnp.argsort(jnp.argsort(scores, axis=-1), axis=-1).reshape(MICRO, SEQS, LEN)
    forced = is_full[:, :, None] & (ranking < CAP + 1)
    routes = jnp.where(forced, hottest[:, None, None], routes).astype(jnp.int32)
    valid = jnp.arange(LEN)[None, None, :] < lengths[:, :, None]

    def blocked(value):
        return value.reshape(MICRO, groups, SEQ_DEV, ranges, DEV_LEN).transpose(0, 1, 3, 2, 4).reshape(MICRO, groups, ranges, SEQ_DEV * DEV_LEN)
    route_blocks = blocked(routes)
    valid_blocks = blocked(valid)
    onehot = (route_blocks[..., None] == jnp.arange(EXPERTS)) & valid_blocks[..., None]
    counts = jnp.cumsum(onehot.astype(jnp.int32), axis=3)
    ranks = jnp.sum(jnp.where(onehot, counts - 1, 0), axis=-1)
    slot_blocks = jnp.where(valid_blocks & (ranks < CAP), ranks, -1)
    slots = slot_blocks.reshape(MICRO, groups, ranges, SEQ_DEV, DEV_LEN).transpose(0, 1, 3, 2, 4).reshape(MICRO, SEQS, LEN)
    return (lengths, routes, slots.astype(jnp.int32))


def draw_lengths(key, part):
    return routing_tables(key)[0]


def draw_routes(key, part):
    return routing_tables(key)[1]


def draw_slots(key, part):
    return routing_tables(key)[2]


def draw_step_bias(key, part):
    sample_key = jax.random.fold_in(key, 5)
    step = jnp.exp(jax.random.uniform(sample_key, (DI,), minval=math.log(0.5), maxval=math.log(48.0))) / LEN
    return jnp.log(jnp.expm1(step)).astype(jnp.float32).astype(jnp.bfloat16)


def draw_channel_params(key, part):
    keys = jax.random.split(jax.random.fold_in(key, 3), 6)
    taps = jax.random.uniform(keys[0], (DI, CONV_TAPS), minval=-1.0, maxval=1.0)
    conv_bias = jax.random.uniform(keys[1], (DI, 1), minval=-0.3, maxval=0.3)
    decay = (jnp.arange(N)[None, :] + 1.0) * jax.random.uniform(keys[5], (DI, N), minval=0.7, maxval=1.4)
    skip = jax.random.uniform(keys[3], (DI, 1), minval=0.5, maxval=1.5)
    table = jnp.concatenate([taps, conv_bias, skip, jnp.log(decay)], axis=1)
    return table.astype(jnp.float32).astype(jnp.bfloat16)


def block_scale(stream_key, shape, pieces, low, largest):
    def one(position, parts):
        draws = jax.random.uniform(jax.random.fold_in(jax.random.fold_in(stream_key, 6), position), (parts,), jnp.float32, low / len(pieces), largest / len(pieces))
        return jnp.repeat(jnp.exp(draws), shape[position] // parts).reshape((-1,) + (1,) * (len(shape) - position - 1))

    factor_of = one(*pieces[0])
    for cut in pieces[1:]:
        factor_of = factor_of * one(*cut)
    return factor_of


def gaussian(own_key, dims, deviation, reach, pieces=(), held_as=jnp.bfloat16):
    array = deviation * jax.random.normal(own_key, dims, jnp.float32)
    if pieces:
        array = array * block_scale(own_key, dims, pieces, -0.22, 0.18)
    return jnp.clip(array, -reach, reach).astype(held_as)


def setup_inputs(seed: int = 0) -> dict:
    streams_of = jax.random.split(jax.random.key(seed), 16)
    return {
        "inputs": gaussian(streams_of[0], (MICRO, SEQS, LEN, D), 1.0, 6.0, ((1, 2), (2, 8))),
        "out_grad": gaussian(streams_of[1], (MICRO, SEQS, LEN, D), 1.0, 6.0, ((1, 2), (2, 8))),
        "lengths": draw_lengths(jax.random.fold_in(streams_of[15], 71), 0),
        "routes": draw_routes(jax.random.fold_in(streams_of[15], 71), 0),
        "slots": draw_slots(jax.random.fold_in(streams_of[15], 71), 0),
        "norm_gains": jnp.clip(1.0 + 0.1 * jax.random.normal(streams_of[5], (2, D), jnp.float32), 0.5, 1.5).astype(jnp.bfloat16),
        "router_matrix": gaussian(streams_of[6], (D, EXPERTS), (4 * D) ** -0.5, 0.109375, ((0, 16),)),
        "input_projection": gaussian(streams_of[7], (2, DI, D), D ** -0.5, 0.21875, ((1, 32),)),
        "inner_projection": gaussian(streams_of[8], (DI, XW), DI ** -0.5, 0.15625, ((0, 32),)),
        "step_projection": gaussian(streams_of[9], (DI, R), 0.1, 1.5, ((0, 32),)),
        "step_bias": draw_step_bias(jax.random.fold_in(streams_of[15], 71), 0),
        "channel_params": draw_channel_params(jax.random.fold_in(streams_of[15], 71), 0),
        "output_projection": gaussian(streams_of[12], (DI, D), 0.1, 1.5, ((0, 32),)),
        "expert_up": gaussian(streams_of[13], (EXPERTS, D, FF), D ** -0.5, 0.21875, ((0, 16), (2, 2))),
        "expert_down": gaussian(streams_of[14], (EXPERTS, FF, D), 1.5, 6.0, ((0, 16), (1, 2))),
    }


@jax.custom_vjp
def low(v):
    return lax.optimization_barrier(v.astype(jnp.bfloat16)).astype(jnp.float32)

@jax.custom_vjp
def low_back(v):
    return v

def low_keep(v):
    return (low(v), None)

def low_pass(kept, grad):
    return (grad,)

def back_keep(v):
    return (v, None)

def back_low(kept, grad):
    return (low(grad),)
low.defvjp(low_keep, low_pass)
low_back.defvjp(back_keep, back_low)
EPS = 1e-05
PRECISION_TOP = lax.Precision.HIGHEST

def gelu_fn(value):
    return jax.nn.gelu(value, approximate=True)

def selective(delta, b_vals, c_vals, conv_activations, rates):
    group, length, chans = delta.shape
    span = math.gcd(length, 8)
    blocks = length // span

    def split(value):
        return jnp.moveaxis(value.reshape(group, blocks, span, value.shape[-1]), 1, 0)

    def block(state, items):
        step, b_blk, c_blk, u_blk = items
        outputs = []
        for pos in range(span):
            state = jnp.exp(step[:, pos, None, :] * rates) * state + (step[:, pos] * u_blk[:, pos])[:, None, :] * b_blk[:, pos, :, None]
            outputs.append(lax.optimization_barrier(jnp.sum(state * c_blk[:, pos, :, None], axis=1)))
        return (state, jnp.stack(outputs, 1))
    start = jnp.zeros((group, rates.shape[0], chans), jnp.float32)
    _, ys = lax.scan(jax.checkpoint(block), start, (split(delta), split(b_vals), split(c_vals), split(conv_activations)))
    return jnp.moveaxis(ys, 0, 1).reshape(group, length, chans)

def mamba_group(x_group, gain, input_projection, inner_projection, step_projection, step_bias, channel_slice, output_projection):
    length = x_group.shape[1]
    scale = lax.rsqrt(lax.optimization_barrier(jnp.mean(x_group * x_group, -1, keepdims=True)) + EPS)
    normed_input = low(x_group * scale * gain)
    inner_channels = low(low_back(jnp.einsum('fzq,sq->fzs', normed_input, input_projection[0], precision=PRECISION_TOP)))
    gate_branch = low_back(jnp.einsum('fzq,sq->fzs', normed_input, input_projection[1], precision=PRECISION_TOP))
    padded = jnp.pad(inner_channels, ((0, 0), (CONV_TAPS - 1, 0), (0, 0)))
    conv = channel_slice[:, CONV_TAPS] + jnp.zeros_like(inner_channels)
    for tap in range(CONV_TAPS):
        conv = conv + channel_slice[:, tap] * padded[:, tap:tap + length]
    conv_activations = low(jax.nn.silu(conv))
    projected_rows = low_back(jnp.einsum('hox,xr->hor', conv_activations, inner_projection, precision=PRECISION_TOP))
    step_rank = low(projected_rows[..., :R])
    b_vals = projected_rows[..., R:R + N]
    c_vals = projected_rows[..., R + N:]
    step_preactivation = low_back(jnp.einsum('oex,bx->oeb', step_rank, step_projection, precision=PRECISION_TOP) + step_bias)
    delta = jax.nn.softplus(step_preactivation)
    rates = -jnp.exp(channel_slice[:, CONV_TAPS + 2:]).T
    y_vals = selective(delta, b_vals, c_vals, conv_activations, rates) + channel_slice[:, CONV_TAPS + 1] * conv_activations
    gated_output = low(y_vals * jax.nn.silu(gate_branch))
    return low_back(jnp.einsum('uit,ts->uis', gated_output, output_projection, precision=PRECISION_TOP))

def block_forward(x_micro, params, len_micro, route_micro, slot_micro):
    gain_vectors, router_matrix, input_projection, inner_projection, step_projection, step_bias, channel_slice, output_projection, expert_up, expert_down = params
    seqs = x_micro.shape[0]
    group = math.gcd(seqs, max(1, 4096 // LEN))
    x_groups = x_micro.reshape(seqs // group, group, LEN, D)
    mixed = lax.map(lambda xs: mamba_group(xs, gain_vectors[0], input_projection, inner_projection, step_projection, step_bias, channel_slice, output_projection), x_groups)
    residual_input = x_micro + mixed.reshape(seqs, LEN, D)
    scale = lax.rsqrt(lax.optimization_barrier(jnp.mean(residual_input * residual_input, -1, keepdims=True)) + EPS)
    normed_input = low(residual_input * scale * gain_vectors[1])
    router_scores = low_back(jnp.einsum('xgo,op->xgp', normed_input, router_matrix, precision=PRECISION_TOP))
    probs = jax.nn.softmax(router_scores, -1)
    onehot = (route_micro[..., None] == jnp.arange(EXPERTS)[None, None, :]).astype(jnp.float32)
    gate = lax.optimization_barrier(jnp.sum(probs * onehot, -1))
    kept = slot_micro >= 0
    sources = N_FSDP * N_CTX
    anchor = (jnp.arange(seqs) // SEQ_DEV)[:, None] * N_CTX + (jnp.arange(LEN) // DEV_LEN)[None, :]
    per_expert = sources * CAP
    index = jnp.where(kept, route_micro * per_expert + anchor * CAP + slot_micro, EXPERTS * per_expert).astype(jnp.int32)
    sent = low_back(normed_input)
    buffer = jnp.zeros((EXPERTS * per_expert, D), jnp.float32).at[index.reshape(-1)].set(sent.reshape(-1, D), mode='drop')
    buffer = buffer.reshape(EXPERTS, per_expert, D)

    def expert(items):
        rows, up_w, down_w = items
        hidden = low_back(jnp.einsum('rd,df->rf', rows, up_w, precision=PRECISION_TOP))
        act = low(gelu_fn(hidden))
        return jnp.einsum('rf,fd->rd', act, down_w, precision=PRECISION_TOP)
    returned = lax.map(jax.checkpoint(expert), (buffer, expert_up, expert_down))
    returned = low_back(low(returned)).reshape(EXPERTS * per_expert, D)
    picked = returned[jnp.where(kept, index, 0)]
    moe = jnp.where(kept, gate, 0.0)[..., None] * picked
    valid = jnp.arange(LEN)[None, :] < len_micro[:, None]
    return jnp.where(valid[..., None], residual_input + moe, 0.0)

def reference(inputs, out_grad, lengths, routes, slots, norm_gains, router_matrix, input_projection, inner_projection, step_projection, step_bias, channel_params, output_projection, expert_up, expert_down):
    params = tuple((value.astype(jnp.float32) for value in (norm_gains, router_matrix, input_projection, inner_projection, step_projection, step_bias, channel_params, output_projection, expert_up, expert_down)))
    outputs = []
    input_grads = []
    totals = None
    for micro in range(MICRO):

        def forward(x_micro, weights):
            return block_forward(x_micro, weights, lengths[micro], routes[micro], slots[micro])
        value, pull = jax.vjp(forward, inputs[micro].astype(jnp.float32), params)
        x_grad, weight_grads = pull(out_grad[micro].astype(jnp.float32))
        outputs.append(value.astype(jnp.bfloat16))
        input_grads.append(x_grad)
        totals = weight_grads if totals is None else tuple((a + b for a, b in zip(totals, weight_grads)))
    return (jnp.stack(outputs), jnp.stack(input_grads), totals[0], totals[1], totals[2], totals[3], totals[4], totals[5], totals[6], totals[7], totals[8], totals[9])
```

```python
import functools

import jax
import jax.numpy as jnp
from jax import lax
from jax.experimental import pallas as pl
from jax.experimental.pallas import tpu as pltpu
from jax.sharding import PartitionSpec as P

N = 16
CONV_TAPS = 4
R = 48
EPS = 1e-05
BLK = 8
LANES = 128
F32 = jnp.float32
BF16 = jnp.bfloat16
OWNERS = ("fsdp", "ctx")


def silu_parts(value):
    sig = jax.nn.sigmoid(value)
    return value * sig, sig * (1.0 + value * (1.0 - sig))


def swapped(value):
    return lax.ppermute(value, "tensor", [(0, 1), (1, 0)])


def tensor_total(value, dtype):
    sent = value.astype(dtype)
    if lax.axis_size("tensor") == 2:
        return sent.astype(F32) + swapped(sent).astype(F32)
    return jnp.sum(lax.all_gather(sent, "tensor").astype(F32), axis=0)


def tensor_share(value):
    peers, here = lax.axis_size("tensor"), lax.axis_index("tensor")
    share = value.shape[-1] // peers
    if peers == 2:
        own = jnp.where(here == 0, value[..., :share], value[..., share:])
        other = jnp.where(here == 0, value[..., share:], value[..., :share])
        return own + swapped(other.astype(BF16)).astype(F32)
    return lax.psum_scatter(value, "tensor", scatter_dimension=value.ndim - 1, tiled=True)


def tensor_columns(value):
    if lax.axis_size("tensor") == 2:
        other = swapped(value)
        first = lax.axis_index("tensor") == 0
        return jnp.concatenate(
            [jnp.where(first, value, other), jnp.where(first, other, value)], -1
        )
    return lax.all_gather(value, "tensor", axis=value.ndim - 1, tiled=True)


def moved(value, by):
    peers = lax.axis_size("ctx")
    pairs = [(i, i + by) for i in range(peers) if 0 <= i + by < peers]
    return lax.ppermute(value, "ctx", pairs)


def carried(state, log_decay, rates, sign):
    def both(parts):
        return jnp.concatenate([parts[0], parts[1][None]], 0)

    def apply(late_log, early):
        return jnp.exp(late_log[None] * rates[:, None, :]) * early

    got = moved(both((state, log_decay)), sign)
    excl = (got[:N], got[N])
    width = 1
    peers = lax.axis_size("ctx")
    while width < peers - 1:
        incl = (state + apply(log_decay, excl[0]), log_decay + excl[1])
        got = moved(both(incl), sign * (width + 1))
        excl = (excl[0] + apply(excl[1], got[:N]), excl[1] + got[N])
        width = 2 * width + 1
    return excl[0]


def spread_matrix():
    rows = lax.broadcasted_iota(jnp.int32, (2 * N, N * LANES), 0) % N
    cols = lax.broadcasted_iota(jnp.int32, (2 * N, N * LANES), 1) // LANES
    return (rows == cols).astype(F32).astype(BF16)


def spread_into(pairs, rows):
    def turn(i, _):
        matrix = spread_matrix()
        at = pl.ds(pl.multiple_of(i * LANES, LANES), LANES)
        for source, target in pairs:
            value = source[at, :]
            high = value.astype(BF16)
            low = (value - high.astype(F32)).astype(BF16)
            target[at, :] = jnp.dot(
                jnp.concatenate([high, low], 1), matrix, preferred_element_type=F32
            )
        return 0

    lax.fori_loop(0, rows // LANES, turn, 0)


def lanes(k):
    return slice(k * LANES, (k + 1) * LANES)


def end_state_kernel(d_ref, u_ref, b_ref, r_ref, end_ref, rb, bb):
    length, seqs, width = d_ref.shape
    parts = width // LANES
    for n in range(N):
        rb[n] = jnp.broadcast_to(r_ref[n : n + 1, :], (seqs, width))

    @pl.when(pl.program_id(0) == 0)
    def _():
        spread_into([(b_ref, bb)], length * seqs)

    def body(t, carry):
        hs, total = carry
        d = d_ref[t]
        du = d * u_ref[t]
        row = pl.ds(pl.multiple_of(t * seqs, seqs), seqs)
        new = []
        for n in range(N):
            bn = bb[row, lanes(n)]
            for k in range(parts):
                a = jnp.exp(d[:, lanes(k)] * rb[n, :, lanes(k)])
                new.append(a * hs[n * parts + k] + du[:, lanes(k)] * bn)
        return tuple(new), total + d

    zero = jnp.zeros((seqs, LANES), F32)
    hs, total = lax.fori_loop(
        0, length, body, ((zero,) * (N * parts), jnp.zeros((seqs, width), F32)), unroll=4
    )
    for n in range(N):
        for k in range(parts):
            end_ref[n, :, lanes(k)] = hs[n * parts + k]
    end_ref[N] = total


def forward_kernel(d_ref, u_ref, b_ref, c_ref, r_ref, h0_ref, y_ref, st_ref, rb, bb, cb):
    length, seqs, width = d_ref.shape
    parts = width // LANES
    for n in range(N):
        rb[n] = jnp.broadcast_to(r_ref[n : n + 1, :], (seqs, width))

    @pl.when(pl.program_id(0) == 0)
    def _():
        spread_into([(b_ref, bb), (c_ref, cb)], length * seqs)

    def block(i, hs):
        for n in range(N):
            for k in range(parts):
                st_ref[i, n, :, lanes(k)] = hs[n * parts + k]

        def body(step, hs):
            t = i * BLK + step
            d = d_ref[t]
            du = d * u_ref[t]
            row = pl.ds(pl.multiple_of(t * seqs, seqs), seqs)
            ys = [jnp.zeros((seqs, LANES), F32) for _ in range(parts)]
            new = []
            for n in range(N):
                bn = bb[row, lanes(n)]
                cn = cb[row, lanes(n)]
                for k in range(parts):
                    a = jnp.exp(d[:, lanes(k)] * rb[n, :, lanes(k)])
                    h = a * hs[n * parts + k] + du[:, lanes(k)] * bn
                    ys[k] = ys[k] + h * cn
                    new.append(h)
            for k in range(parts):
                y_ref[t, :, lanes(k)] = ys[k]
            return tuple(new)

        return lax.fori_loop(0, BLK, body, hs, unroll=4)

    lax.fori_loop(
        0,
        length // BLK,
        block,
        tuple(h0_ref[n, :, lanes(k)] for n in range(N) for k in range(parts)),
    )


def start_grad_kernel(d_ref, dy_ref, c_ref, r_ref, g_ref, rb, cb):
    length, seqs, width = d_ref.shape
    parts = width // LANES
    for n in range(N):
        rb[n] = jnp.broadcast_to(r_ref[n : n + 1, :], (seqs, width))

    @pl.when(pl.program_id(0) == 0)
    def _():
        spread_into([(c_ref, cb)], length * seqs)

    def body(i, gs):
        t = length - 1 - i
        d = d_ref[t]
        dy = dy_ref[t]
        row = pl.ds(pl.multiple_of(t * seqs, seqs), seqs)
        new = []
        for n in range(N):
            cn = cb[row, lanes(n)]
            for k in range(parts):
                a = jnp.exp(d[:, lanes(k)] * rb[n, :, lanes(k)])
                new.append(a * (gs[n * parts + k] + dy[:, lanes(k)] * cn))
        return tuple(new)

    zero = jnp.zeros((seqs, LANES), F32)
    gs = lax.fori_loop(0, length, body, (zero,) * (N * parts), unroll=4)
    for n in range(N):
        for k in range(parts):
            g_ref[n, :, lanes(k)] = gs[n * parts + k]


def backward_kernel(
    d_ref,
    u_ref,
    dy_ref,
    b_ref,
    c_ref,
    r_ref,
    st_ref,
    g0_ref,
    ds_ref,
    du_ref,
    db_ref,
    dc_ref,
    rg_ref,
    rb,
    bb,
    cb,
    hb,
    ab,
    pb,
    pc,
):
    length, seqs, width = d_ref.shape
    parts = width // LANES
    for n in range(N):
        rb[n] = jnp.broadcast_to(r_ref[n : n + 1, :], (seqs, width))

    @pl.when(pl.program_id(0) == 0)
    def _():
        spread_into([(b_ref, bb), (c_ref, cb)], length * seqs)
        db_ref[...] = jnp.zeros_like(db_ref)
        dc_ref[...] = jnp.zeros_like(dc_ref)

    rg_ref[...] = jnp.zeros_like(rg_ref)
    ones = jnp.ones((LANES, LANES), BF16)
    lane = lax.broadcasted_iota(jnp.int32, (N * seqs, length), 1)

    def block(turn, gs):
        i = length // BLK - 1 - turn

        def again(step, hs):
            t = i * BLK + step
            d = d_ref[t]
            du = d * u_ref[t]
            row = pl.ds(pl.multiple_of(t * seqs, seqs), seqs)
            new = []
            for n in range(N):
                bn = bb[row, lanes(n)]
                for k in range(parts):
                    a = jnp.exp(d[:, lanes(k)] * rb[n, :, lanes(k)])
                    h = a * hs[n * parts + k] + du[:, lanes(k)] * bn
                    ab[step, n, :, lanes(k)] = a
                    hb[step + 1, n, :, lanes(k)] = h
                    new.append(h)
            return tuple(new)

        hs = tuple(st_ref[i, n, :, lanes(k)] for n in range(N) for k in range(parts))
        for n in range(N):
            for k in range(parts):
                hb[0, n, :, lanes(k)] = hs[n * parts + k]
        lax.fori_loop(0, BLK, again, hs, unroll=4)

        def back(turn, gs):
            step = BLK - 1 - turn
            t = i * BLK + step
            row = pl.ds(pl.multiple_of(t * seqs, seqs), seqs)
            d = d_ref[t]
            u = u_ref[t]
            dy = dy_ref[t]
            du = d * u
            prods = [jnp.zeros((seqs, LANES), F32) for _ in range(parts)]
            steps = [jnp.zeros((seqs, LANES), F32) for _ in range(parts)]
            new = []
            for n in range(N):
                bn = bb[row, lanes(n)]
                cn = cb[row, lanes(n)]
                b_sum = c_sum = None
                for k in range(parts):
                    g = gs[n * parts + k] + cn * dy[:, lanes(k)]
                    c_term = hb[step + 1, n, :, lanes(k)] * dy[:, lanes(k)]
                    b_term = g * du[:, lanes(k)]
                    c_sum = c_term if k == 0 else c_sum + c_term
                    b_sum = b_term if k == 0 else b_sum + b_term
                    prods[k] = prods[k] + g * bn
                    carried_g = g * ab[step, n, :, lanes(k)]
                    decay_g = carried_g * hb[step, n, :, lanes(k)]
                    steps[k] = steps[k] + decay_g * rb[n, :, lanes(k)]
                    rg_ref[n, :, lanes(k)] = rg_ref[n, :, lanes(k)] + decay_g * d[:, lanes(k)]
                    new.append(carried_g)
                pb[step, n * seqs : (n + 1) * seqs, :] = b_sum
                pc[step, n * seqs : (n + 1) * seqs, :] = c_sum
            for k in range(parts):
                ds_ref[t, :, lanes(k)] = steps[k] + prods[k] * u[:, lanes(k)]
                du_ref[t, :, lanes(k)] = prods[k] * d[:, lanes(k)]
            return tuple(new)

        gs = lax.fori_loop(0, BLK, back, gs, unroll=2)
        b_new = jnp.zeros((N * seqs, length), F32)
        c_new = jnp.zeros((N * seqs, length), F32)
        for step in range(BLK):
            here = lane == i * BLK + step
            b_new = jnp.where(
                here, jnp.dot(pb[step].astype(BF16), ones, preferred_element_type=F32), b_new
            )
            c_new = jnp.where(
                here, jnp.dot(pc[step].astype(BF16), ones, preferred_element_type=F32), c_new
            )
        db_ref[...] += b_new
        dc_ref[...] += c_new
        return gs

    lax.fori_loop(
        0,
        length // BLK,
        block,
        tuple(g0_ref[n, :, lanes(k)] for n in range(N) for k in range(parts)),
    )


def scan_call(kernel, arrays, outs, scratch, width, chans):
    def spec(shape):
        if shape[-1] == chans:
            rank = len(shape)
            return pl.BlockSpec(
                (*shape[:-1], width), lambda j, rank=rank: (0,) * (rank - 1) + (j,)
            )
        return pl.BlockSpec(shape, lambda j, rank=len(shape): (0,) * rank)

    return pl.pallas_call(
        kernel,
        grid=(chans // width,),
        in_specs=[spec(a.shape) for a in arrays],
        out_specs=[spec(s) for s in outs],
        out_shape=[jax.ShapeDtypeStruct(s, F32) for s in outs],
        scratch_shapes=[pltpu.VMEM(s, F32) for s in scratch],
        compiler_params=pltpu.CompilerParams(vmem_limit_bytes=62 << 20),
    )(*arrays)


def per_device(
    inputs,
    out_grad,
    lengths,
    routes,
    slots,
    norm_gains,
    router_matrix,
    input_projection,
    inner_projection,
    step_projection,
    step_bias,
    channel_params,
    output_projection,
    expert_up,
    expert_down,
):
    micros, group, length, width = inputs.shape
    seqs = micros * group
    tokens = length * seqs
    owners = lax.axis_size("fsdp") * lax.axis_size("ctx")
    experts = router_matrix.shape[1]
    capacity = max(2, (25 * group * length + 32 * experts - 1) // (32 * experts))
    slots_each = micros * capacity
    rows = experts * slots_each

    def by_token(value):
        return jnp.moveaxis(value, 2, 0).reshape(tokens, *value.shape[3:])

    def by_sequence(value):
        return jnp.moveaxis(value.reshape(length, micros, group, value.shape[-1]), 0, 2)

    narrow = jnp.concatenate(
        [inner_projection, step_projection, channel_params, step_bias[:, None]], 1
    )
    x_cols = inner_projection.shape[1]
    cuts = [x_cols, x_cols + R, x_cols + R + channel_params.shape[1]]
    routing = jnp.concatenate([router_matrix, norm_gains.T], 1)
    joined = narrow.shape[0] == routing.shape[0]
    if joined:
        narrow = jnp.concatenate([narrow, routing], 1)
    narrow_cols = narrow.shape[1]
    pad = -narrow_cols % LANES
    wide = jnp.concatenate(
        [
            input_projection[0],
            input_projection[1],
            output_projection,
            jnp.pad(narrow, ((0, 0), (0, pad))),
        ],
        1,
    )
    full = lax.all_gather(wide, OWNERS, axis=0, tiled=True)
    w_in, w_gate, w_out = (full[:, i * width : (i + 1) * width] for i in range(3))
    tail = full[:, 3 * width :]
    w_x = tail[:, : cuts[0]]
    w_step = tail[:, cuts[0] : cuts[1]]
    channel_f = tail[:, cuts[1] : cuts[2]].astype(F32)
    bias_f = tail[:, cuts[2]].astype(F32)
    if joined:
        full_routing = tail[:, cuts[2] + 1 : cuts[2] + 1 + routing.shape[1]]
    else:
        full_routing = lax.all_gather(routing, OWNERS, axis=0, tiled=True)
    w_router = full_routing[:, :experts]
    gains = full_routing[:, experts:].T.astype(F32)
    chans = channel_f.shape[0]
    taps = channel_f[:, :CONV_TAPS].T
    conv_bias = channel_f[:, CONV_TAPS]
    skip = channel_f[:, CONV_TAPS + 1]
    rates = -jnp.exp(channel_f[:, CONV_TAPS + 2 :]).T

    position = lax.axis_index("ctx") * length + jnp.arange(length)
    valid = (position[:, None] < lengths.reshape(1, seqs)).astype(F32).reshape(tokens, 1)
    route = by_token(routes)
    slot = by_token(slots)
    kept = slot >= 0
    kept_f = kept.astype(F32)
    micro_of = (jnp.arange(tokens) // group) % micros
    place = jnp.where(kept, route * slots_each + micro_of * capacity + slot, -1)
    pick = (jnp.arange(rows)[:, None] == place[None, :]).astype(BF16)
    grad_tok = by_token(out_grad)
    grad_act = grad_tok.astype(F32) * valid

    def to_experts(value):
        return lax.all_to_all(
            value.reshape(experts, slots_each, value.shape[-1]),
            OWNERS,
            split_axis=0,
            concat_axis=0,
            tiled=True,
        ).reshape(rows, value.shape[-1])

    grad_rows_raw = to_experts(
        jnp.dot(pick, grad_tok, preferred_element_type=F32).astype(BF16)
    )

    x = by_token(inputs).astype(F32)
    scale1 = lax.rsqrt(jnp.mean(x * x, -1, keepdims=True) + EPS)
    xhat1 = x * scale1
    normed1 = (xhat1 * gains[0]).astype(BF16)
    nt = (((1,), (1,)), ((), ()))
    tn = (((0,), (0,)), ((), ()))

    def dot(a, b, dims=(((1,), (0,)), ((), ()))):
        return lax.dot_general(a, b, dims, preferred_element_type=F32)

    inner = dot(normed1, w_in, nt).astype(BF16)
    rim = (CONV_TAPS - 1) * seqs
    before = moved(inner[tokens - rim :], 1)
    gate_z = dot(normed1, w_gate, nt)
    extended = jnp.concatenate([before, inner], 0).astype(F32)
    conv = conv_bias
    for tap in range(CONV_TAPS):
        conv = conv + taps[tap] * extended[tap * seqs : tap * seqs + tokens]
    u_float, conv_slope = silu_parts(conv)
    u = u_float.astype(BF16)
    u_wide = u.astype(F32)
    proj = tensor_total(dot(u, w_x), F32)
    rank = proj[:, :R].astype(BF16)
    b_vals = proj[:, R : R + N]
    c_vals = proj[:, R + N :]
    step_pre = dot(rank, w_step, nt) + bias_f
    delta = jax.nn.softplus(step_pre)
    cube = (length, seqs, chans)
    delta3 = delta.reshape(cube)
    u3 = u_wide.reshape(cube)
    lane_width = 2 * LANES if chans % (2 * LANES) == 0 else LANES
    wide_rates = (N, seqs, lane_width)
    spread = (tokens, N * LANES)
    call = functools.partial(scan_call, width=lane_width, chans=chans)
    [end] = call(
        end_state_kernel,
        [delta3, u3, b_vals, rates],
        [(N + 1, seqs, chans)],
        [wide_rates, spread],
    )
    state_end, log_decay = end[:N], end[N]
    entry = carried(state_end, log_decay, rates, 1)
    y_scan, starts = call(
        forward_kernel,
        [delta3, u3, b_vals, c_vals, rates, entry],
        [cube, (length // BLK, N, seqs, chans)],
        [wide_rates, spread, spread],
    )
    y_vals = y_scan.reshape(tokens, chans) + skip * u_wide
    silu_z, gate_slope = silu_parts(gate_z)
    gated = (y_vals * silu_z).astype(BF16)
    resid = x + tensor_total(dot(gated, w_out), BF16)

    scale2 = lax.rsqrt(jnp.mean(resid * resid, -1, keepdims=True) + EPS)
    xhat2 = resid * scale2
    normed2 = (xhat2 * gains[1]).astype(BF16)
    probs = jax.nn.softmax(dot(normed2, w_router), -1)
    onehot = (route[:, None] == jnp.arange(experts)).astype(F32)
    gate = jnp.sum(probs * onehot, -1, keepdims=True) * kept_f[:, None]
    high = gate.astype(BF16)
    middle = (gate - high.astype(F32)).astype(BF16)
    low = (gate - high.astype(F32) - middle.astype(F32)).astype(BF16)
    sent = jnp.concatenate(
        [normed2, high, middle, low, jnp.zeros((tokens, LANES - 3), BF16)], 1
    )
    arrived = to_experts(dot(pick, sent).astype(BF16))
    x_rows = arrived[:, :width]
    pieces = arrived[:, width : width + 3].astype(F32)
    gate_rows = pieces[:, :1] + pieces[:, 1:2] + pieces[:, 2:3]
    grad_rows = (gate_rows * grad_rows_raw.astype(F32)).astype(BF16)
    up, down = expert_up[0], expert_down[0]
    hidden = dot(x_rows, up)
    act_float, gelu_pull = jax.vjp(lambda v: jax.nn.gelu(v, approximate=True), hidden)
    act = act_float.astype(BF16)
    part_y = dot(act, down)
    d_hidden = gelu_pull(dot(grad_rows, down, nt))[0].astype(BF16)
    part_x = dot(d_hidden, up, nt)
    returned = jnp.concatenate(
        [tensor_share(part_y).astype(BF16), tensor_share(part_x).astype(BF16)], 1
    )
    grad_up = dot(x_rows, d_hidden, tn)
    grad_down = dot(act, grad_rows, tn)
    back = to_experts(returned)
    share = returned.shape[1] // 2
    own = dot(pick, back, tn).astype(BF16)
    expert_y = tensor_columns(own[:, :share]).astype(F32)
    expert_dx = tensor_columns(own[:, share:]).astype(F32)
    activations = (valid * (resid + gate * expert_y)).astype(BF16)
    gate_grad = jnp.sum(grad_act * expert_y, -1, keepdims=True)
    d_logits = (gate_grad * gate * (onehot - probs)).astype(BF16)
    grad_router = dot(normed2, d_logits, tn)
    d_normed2 = expert_dx + dot(d_logits, w_router, nt)
    gain_grad2 = jnp.sum(d_normed2 * xhat2, 0)
    scaled2 = gains[1] * d_normed2
    d_resid = grad_act + scale2 * (scaled2 - xhat2 * jnp.mean(scaled2 * xhat2, -1, keepdims=True))

    d_mixed = d_resid.astype(BF16)
    d_gated = dot(d_mixed, w_out, nt)
    d_y = d_gated * silu_z
    dy3 = d_y.reshape(cube)
    [start_grad] = call(
        start_grad_kernel,
        [delta3, dy3, c_vals, rates],
        [(N, seqs, chans)],
        [wide_rates, spread],
    )
    grad_out = dot(gated, d_mixed, tn)
    d_gate_z = (d_gated * y_vals * gate_slope).astype(BF16)
    grad_end = carried(start_grad, log_decay, rates, -1)
    step_grad, u_grad, b_grad, c_grad, rate_grad = call(
        backward_kernel,
        [delta3, u3, dy3, b_vals, c_vals, rates, starts, grad_end],
        [cube, cube, (N * seqs, length), (N * seqs, length), (N, seqs, chans)],
        [
            wide_rates,
            spread,
            spread,
            (BLK + 1, N, seqs, lane_width),
            (BLK, N, seqs, lane_width),
            (BLK, N * seqs, LANES),
            (BLK, N * seqs, LANES),
        ],
    )

    def per_token(value):
        return jnp.transpose(value.reshape(N, seqs, length), (2, 1, 0)).reshape(tokens, N)

    d_step = (step_grad.reshape(tokens, chans) * jax.nn.sigmoid(step_pre)).astype(BF16)
    rank_grad = dot(d_step, w_step)
    d_proj = tensor_total(
        jnp.concatenate([rank_grad, per_token(b_grad), per_token(c_grad)], -1), BF16
    ).astype(BF16)
    grad_dt = dot(d_step, rank, tn)
    step_bias_grad = jnp.sum(d_step.astype(F32), 0)
    skip_grad = jnp.sum(d_y * u_wide, 0)
    grad_xproj = dot(u, d_proj, tn)
    d_u = d_y * skip + u_grad.reshape(tokens, chans) + dot(d_proj, w_x, nt)
    d_conv = d_u * conv_slope
    after = moved(d_conv[:rim], -1)
    conv_bias_grad = jnp.sum(d_conv, 0)
    tap_grads = [
        jnp.sum(d_conv * extended[tap * seqs : tap * seqs + tokens], 0) for tap in range(CONV_TAPS)
    ]
    extended_grad = jnp.concatenate([d_conv, after], 0)
    d_inner = jnp.zeros((tokens, chans), F32)
    for tap in range(CONV_TAPS):
        at = (CONV_TAPS - 1 - tap) * seqs
        d_inner = d_inner + taps[tap] * extended_grad[at : at + tokens]
    d_inner = d_inner.astype(BF16)
    d_normed1 = tensor_total(dot(d_inner, w_in) + dot(d_gate_z, w_gate), BF16)
    gain_grad1 = jnp.sum(d_normed1 * xhat1, 0)
    scaled1 = gains[0] * d_normed1
    input_grad = d_resid + scale1 * (
        scaled1 - xhat1 * jnp.mean(scaled1 * xhat1, -1, keepdims=True)
    )

    narrow_grads = jnp.concatenate(
        [
            grad_xproj,
            grad_dt,
            jnp.stack(tap_grads, 1),
            conv_bias_grad[:, None],
            skip_grad[:, None],
            (jnp.sum(rate_grad, 1) * rates).T,
            step_bias_grad[:, None],
        ],
        1,
    )
    routing_grads = jnp.concatenate([grad_router, gain_grad1[:, None], gain_grad2[:, None]], 1)
    if joined:
        narrow_grads = jnp.concatenate([narrow_grads, routing_grads], 1)
    wide_grads = jnp.concatenate(
        [
            dot(d_inner, normed1, tn),
            dot(d_gate_z, normed1, tn),
            grad_out,
            jnp.pad(narrow_grads, ((0, 0), (0, pad))),
        ],
        1,
    )

    def owned(value):
        return lax.psum_scatter(
            value.astype(BF16), OWNERS, scatter_dimension=0, tiled=True
        ).astype(F32)

    mine = owned(wide_grads)
    mine_tail = mine[:, 3 * width :]
    if joined:
        mine_routing = mine_tail[:, cuts[2] + 1 : cuts[2] + 1 + routing.shape[1]]
    else:
        mine_routing = owned(routing_grads)
    return (
        by_sequence(activations),
        by_sequence(input_grad),
        mine_routing[:, experts:].T,
        mine_routing[:, :experts],
        jnp.stack([mine[:, :width], mine[:, width : 2 * width]]),
        mine_tail[:, : cuts[0]],
        mine_tail[:, cuts[0] : cuts[1]],
        mine_tail[:, cuts[2]],
        mine_tail[:, cuts[1] : cuts[2]],
        mine[:, 2 * width : 3 * width],
        grad_up[None],
        grad_down[None],
    )


def solution(mesh):
    return jax.shard_map(
        per_device,
        mesh=mesh,
        in_specs=(
            P(None, "fsdp", "ctx", None),
            P(None, "fsdp", "ctx", None),
            P(None, "fsdp"),
            P(None, "fsdp", "ctx"),
            P(None, "fsdp", "ctx"),
            P(None, ("fsdp", "ctx")),
            P(("fsdp", "ctx"), None),
            P(None, ("fsdp", "ctx", "tensor"), None),
            P(("fsdp", "ctx", "tensor"), None),
            P(("fsdp", "ctx", "tensor"), None),
            P(("fsdp", "ctx", "tensor")),
            P(("fsdp", "ctx", "tensor"), None),
            P(("fsdp", "ctx", "tensor"), None),
            P(("fsdp", "ctx"), None, "tensor"),
            P(("fsdp", "ctx"), "tensor", None),
        ),
        out_specs=(
            P(None, "fsdp", "ctx", None),
            P(None, "fsdp", "ctx", None),
            P(None, ("fsdp", "ctx")),
            P(("fsdp", "ctx"), None),
            P(None, ("fsdp", "ctx", "tensor"), None),
            P(("fsdp", "ctx", "tensor"), None),
            P(("fsdp", "ctx", "tensor"), None),
            P(("fsdp", "ctx", "tensor")),
            P(("fsdp", "ctx", "tensor"), None),
            P(("fsdp", "ctx", "tensor"), None),
            P(("fsdp", "ctx"), None, "tensor"),
            P(("fsdp", "ctx"), "tensor", None),
        ),
        check_vma=False,
    )
```

```python
import functools

import jax
import jax.numpy as jnp
from jax import lax
from jax.experimental import pallas as pl
from jax.experimental.pallas import tpu as pltpu
from jax.sharding import PartitionSpec as P

N = 16
CONV_TAPS = 4
R = 48
EPS = 1e-05
BLK = 8
LANES = 128
F32 = jnp.float32
BF16 = jnp.bfloat16
OWNERS = ("fsdp", "ctx")


def silu_parts(value):
    sig = jax.nn.sigmoid(value)
    return value * sig, sig * (1.0 + value * (1.0 - sig))


def swapped(value):
    return lax.ppermute(value, "tensor", [(0, 1), (1, 0)])


def tensor_total(value, dtype):
    sent = value.astype(dtype)
    if lax.axis_size("tensor") == 2:
        return sent.astype(F32) + swapped(sent).astype(F32)
    return jnp.sum(lax.all_gather(sent, "tensor").astype(F32), axis=0)


def tensor_share(value):
    peers, here = lax.axis_size("tensor"), lax.axis_index("tensor")
    share = value.shape[-1] // peers
    if peers == 2:
        own = jnp.where(here == 0, value[..., :share], value[..., share:])
        other = jnp.where(here == 0, value[..., share:], value[..., :share])
        return own + swapped(other.astype(BF16)).astype(F32)
    return lax.psum_scatter(value, "tensor", scatter_dimension=value.ndim - 1, tiled=True)


def tensor_columns(value):
    if lax.axis_size("tensor") == 2:
        other = swapped(value)
        first = lax.axis_index("tensor") == 0
        return jnp.concatenate(
            [jnp.where(first, value, other), jnp.where(first, other, value)], -1
        )
    return lax.all_gather(value, "tensor", axis=value.ndim - 1, tiled=True)


def halved(value, beside=()):
    beside = list(beside)
    sizes = [lax.axis_size(axis) for axis in OWNERS]
    bits = [(axis, 1 << k) for axis, size in zip(OWNERS, sizes) for k in reversed(range(size.bit_length() - 1))]
    rows = value.shape[0] >> len(bits)
    for place in reversed(range(len(bits))):
        axis, bit = bits[place]
        view = value.reshape(1 << place, 2, rows, value.shape[-1])
        high = (lax.axis_index(axis) & bit) != 0
        own = jnp.where(high, view[:, 1], view[:, 0])
        other = jnp.where(high, view[:, 0], view[:, 1]).astype(BF16)
        got = lax.ppermute(other, axis, [(i, i ^ bit) for i in range(lax.axis_size(axis))])
        value = own.astype(F32) + got.astype(F32)
        turn = len(bits) - 1 - place
        if turn < len(beside):
            value, beside[turn] = lax.optimization_barrier((value, beside[turn]))
    return value.reshape(rows, value.shape[-1]), beside


def moved(value, by):
    peers = lax.axis_size("ctx")
    pairs = [(i, i + by) for i in range(peers) if 0 <= i + by < peers]
    return lax.ppermute(value, "ctx", pairs)


def carried(state, log_decay, rates, sign):
    def sent(parts):
        high = parts[1].astype(BF16)
        low = (parts[1] - high.astype(F32)).astype(BF16)
        both = jnp.concatenate([parts[0].astype(BF16), high[None], low[None]], 0)
        got = moved(both, sign * (width + 1)).astype(F32)
        return got[:N], got[N] + got[N + 1]

    def apply(late_log, early):
        return jnp.exp(late_log[None] * rates[:, None, :]) * early

    width = 0
    excl = sent((state, log_decay))
    width = 1
    peers = lax.axis_size("ctx")
    while width < peers - 1:
        incl = (state + apply(log_decay, excl[0]), log_decay + excl[1])
        got = sent(incl)
        excl = (excl[0] + apply(excl[1], got[0]), excl[1] + got[1])
        width = 2 * width + 1
    return excl[0]


def spread_matrix():
    rows = lax.broadcasted_iota(jnp.int32, (2 * N, N * LANES), 0) % N
    cols = lax.broadcasted_iota(jnp.int32, (2 * N, N * LANES), 1) // LANES
    return (rows == cols).astype(F32).astype(BF16)


def spread_into(pairs, rows):
    def turn(i, _):
        matrix = spread_matrix()
        at = pl.ds(pl.multiple_of(i * LANES, LANES), LANES)
        for source, target in pairs:
            value = source[at, :]
            high = value.astype(BF16)
            low = (value - high.astype(F32)).astype(BF16)
            target[at, :] = jnp.dot(
                jnp.concatenate([high, low], 1), matrix, preferred_element_type=F32
            )
        return 0

    lax.fori_loop(0, rows // LANES, turn, 0)


def lanes(k):
    return slice(k * LANES, (k + 1) * LANES)


def end_state_kernel(d_ref, u_ref, b_ref, r_ref, end_ref, rb, bb):
    rows, width = d_ref.shape
    seqs = rb.shape[1]
    length = rows // seqs
    parts = width // LANES
    for n in range(N):
        rb[n] = jnp.broadcast_to(r_ref[n : n + 1, :], (seqs, width))

    @pl.when(pl.program_id(0) == 0)
    def _():
        spread_into([(b_ref, bb)], rows)

    def body(t, carry):
        hs, total = carry
        row = pl.ds(pl.multiple_of(t * seqs, seqs), seqs)
        d = d_ref[row, :]
        du = d * u_ref[row, :]
        new = []
        for n in range(N):
            bn = bb[row, lanes(n)]
            for k in range(parts):
                a = jnp.exp(d[:, lanes(k)] * rb[n, :, lanes(k)])
                new.append(a * hs[n * parts + k] + du[:, lanes(k)] * bn)
        return tuple(new), total + d

    zero = jnp.zeros((seqs, LANES), F32)
    hs, total = lax.fori_loop(
        0, length, body, ((zero,) * (N * parts), jnp.zeros((seqs, width), F32)), unroll=4
    )
    for n in range(N):
        for k in range(parts):
            end_ref[n, :, lanes(k)] = hs[n * parts + k]
    end_ref[N] = total


def forward_kernel(
    d_ref,
    u_ref,
    z_ref,
    b_ref,
    c_ref,
    r_ref,
    skip_ref,
    w_ref,
    h0_ref,
    y_ref,
    gated_ref,
    mixed_ref,
    st_ref,
    h1_ref,
    rb,
    bb,
    cb,
    total,
):
    rows, width = d_ref.shape
    seqs = rb.shape[1]
    length = rows // seqs
    parts = width // LANES
    for n in range(N):
        rb[n] = jnp.broadcast_to(r_ref[n : n + 1, :], (seqs, width))

    @pl.when(pl.program_id(0) == 0)
    def _():
        spread_into([(b_ref, bb), (c_ref, cb)], rows)
        total[...] = jnp.zeros_like(total)

    def block(i, hs):
        for n in range(N):
            for k in range(parts):
                st_ref[i, n, :, lanes(k)] = hs[n * parts + k]

        def body(step, hs):
            t = i * BLK + step
            row = pl.ds(pl.multiple_of(t * seqs, seqs), seqs)
            d = d_ref[row, :]
            u = u_ref[row, :]
            du = d * u
            ys = [u[:, lanes(k)] * skip_ref[:, lanes(k)] for k in range(parts)]
            new = []
            for n in range(N):
                bn = bb[row, lanes(n)]
                cn = cb[row, lanes(n)]
                for k in range(parts):
                    a = jnp.exp(d[:, lanes(k)] * rb[n, :, lanes(k)])
                    h = a * hs[n * parts + k] + du[:, lanes(k)] * bn
                    ys[k] = ys[k] + h * cn
                    new.append(h)
            for k in range(parts):
                y_ref[row, lanes(k)] = ys[k]
            return tuple(new)

        return lax.fori_loop(0, BLK, body, hs, unroll=4)

    hs = lax.fori_loop(
        0,
        length // BLK,
        block,
        tuple(h0_ref[n, :, lanes(k)] for n in range(N) for k in range(parts)),
    )
    for n in range(N):
        for k in range(parts):
            h1_ref[n, :, lanes(k)] = hs[n * parts + k]
    z = z_ref[...]
    gated = (y_ref[...] * (z * jax.nn.sigmoid(z))).astype(BF16)
    gated_ref[...] = gated
    total[...] += jnp.dot(gated, w_ref[...], preferred_element_type=F32)
    mixed_ref[...] = total[...].astype(BF16)


def start_grad_kernel(d_ref, dy_ref, c_ref, r_ref, g_ref, rb, cb):
    rows, width = d_ref.shape
    seqs = rb.shape[1]
    length = rows // seqs
    parts = width // LANES
    for n in range(N):
        rb[n] = jnp.broadcast_to(r_ref[n : n + 1, :], (seqs, width))

    @pl.when(pl.program_id(0) == 0)
    def _():
        spread_into([(c_ref, cb)], rows)

    def body(i, gs):
        t = length - 1 - i
        row = pl.ds(pl.multiple_of(t * seqs, seqs), seqs)
        d = d_ref[row, :]
        dy = dy_ref[row, :]
        new = []
        for n in range(N):
            cn = cb[row, lanes(n)]
            for k in range(parts):
                a = jnp.exp(d[:, lanes(k)] * rb[n, :, lanes(k)])
                new.append(a * (gs[n * parts + k] + dy[:, lanes(k)] * cn))
        return tuple(new)

    zero = jnp.zeros((seqs, LANES), F32)
    gs = lax.fori_loop(0, length, body, (zero,) * (N * parts), unroll=4)
    for n in range(N):
        for k in range(parts):
            g_ref[n, :, lanes(k)] = gs[n * parts + k]


def backward_kernel(
    d_ref,
    u_ref,
    dy_ref,
    sig_ref,
    b_ref,
    c_ref,
    r_ref,
    skip_ref,
    w_ref,
    st_ref,
    g0_ref,
    dstep_ref,
    du_ref,
    dproj_ref,
    rg_ref,
    bias_ref,
    skipg_ref,
    rb,
    bb,
    cb,
    hb,
    ab,
    pb,
    pc,
    dsb,
    total,
    columns,
):
    rows, width = d_ref.shape
    seqs = rb.shape[1]
    length = rows // seqs
    parts = width // LANES
    group = pl.program_id(0)
    for n in range(N):
        rb[n] = jnp.broadcast_to(r_ref[n : n + 1, :], (seqs, width))

    @pl.when(group == 0)
    def _():
        spread_into([(b_ref, bb), (c_ref, cb)], rows)
        total[...] = jnp.zeros_like(total)
        source = lax.broadcasted_iota(jnp.int32, columns.shape, 0) // LANES
        target = lax.broadcasted_iota(jnp.int32, columns.shape, 1)
        columns[...] = (source + R == target).astype(F32).astype(BF16)

    rg_ref[...] = jnp.zeros_like(rg_ref)
    bias_ref[...] = jnp.zeros_like(bias_ref)
    skipg_ref[...] = jnp.zeros_like(skipg_ref)

    def block(turn, gs):
        i = length // BLK - 1 - turn

        def again(step, hs):
            t = i * BLK + step
            row = pl.ds(pl.multiple_of(t * seqs, seqs), seqs)
            d = d_ref[row, :]
            du = d * u_ref[row, :]
            new = []
            for n in range(N):
                bn = bb[row, lanes(n)]
                for k in range(parts):
                    a = jnp.exp(d[:, lanes(k)] * rb[n, :, lanes(k)])
                    h = a * hs[n * parts + k] + du[:, lanes(k)] * bn
                    ab[step, n, :, lanes(k)] = a
                    hb[step + 1, n, :, lanes(k)] = h
                    new.append(h)
            return tuple(new)

        hs = tuple(st_ref[i, n, :, lanes(k)] for n in range(N) for k in range(parts))
        for n in range(N):
            for k in range(parts):
                hb[0, n, :, lanes(k)] = hs[n * parts + k]
        lax.fori_loop(0, BLK, again, hs, unroll=4)

        def back(turn, gs):
            step = BLK - 1 - turn
            t = i * BLK + step
            row = pl.ds(pl.multiple_of(t * seqs, seqs), seqs)
            here = pl.ds(pl.multiple_of(step * seqs, seqs), seqs)
            d = d_ref[row, :]
            u = u_ref[row, :]
            dy = dy_ref[row, :]
            du = d * u
            prods = [jnp.zeros((seqs, LANES), F32) for _ in range(parts)]
            steps = [jnp.zeros((seqs, LANES), F32) for _ in range(parts)]
            new = []
            for n in range(N):
                bn = bb[row, lanes(n)]
                cn = cb[row, lanes(n)]
                b_sum = c_sum = None
                for k in range(parts):
                    g = gs[n * parts + k] + cn * dy[:, lanes(k)]
                    c_term = hb[step + 1, n, :, lanes(k)] * dy[:, lanes(k)]
                    b_term = g * du[:, lanes(k)]
                    c_sum = c_term if k == 0 else c_sum + c_term
                    b_sum = b_term if k == 0 else b_sum + b_term
                    prods[k] = prods[k] + g * bn
                    carried_g = g * ab[step, n, :, lanes(k)]
                    decay_g = carried_g * hb[step, n, :, lanes(k)]
                    steps[k] = steps[k] + decay_g * rb[n, :, lanes(k)]
                    rg_ref[n, :, lanes(k)] = rg_ref[n, :, lanes(k)] + decay_g * d[:, lanes(k)]
                    new.append(carried_g)
                pb[here, lanes(n)] = b_sum
                pc[here, lanes(n)] = c_sum
            skipg_ref[...] += dy * u
            for k in range(parts):
                dsb[here, lanes(k)] = steps[k] + prods[k] * u[:, lanes(k)]
                du_ref[row, lanes(k)] = (
                    prods[k] * d[:, lanes(k)] + dy[:, lanes(k)] * skip_ref[:, lanes(k)]
                )
            return tuple(new)

        gs = lax.fori_loop(0, BLK, back, gs, unroll=2)
        at = pl.ds(pl.multiple_of(i * BLK * seqs, BLK * seqs), BLK * seqs)
        d_step = (dsb[...] * sig_ref[at, :]).astype(BF16)
        dstep_ref[at, :] = d_step
        bias_ref[...] += jnp.sum(d_step.astype(F32).reshape(BLK, seqs, width), 0)
        total[at, :] += (
            jnp.dot(d_step, w_ref[...], preferred_element_type=F32)
            + jnp.dot(pb[...].astype(BF16), columns[: N * LANES], preferred_element_type=F32)
            + jnp.dot(pc[...].astype(BF16), columns[N * LANES :], preferred_element_type=F32)
        )
        return gs

    lax.fori_loop(
        0,
        length // BLK,
        block,
        tuple(g0_ref[n, :, lanes(k)] for n in range(N) for k in range(parts)),
    )

    @pl.when(group == pl.num_programs(0) - 1)
    def _():
        dproj_ref[...] = total[...].astype(BF16)


TN = (((0,), (0,)), ((), ()))
NT = (((1,), (1,)), ((), ()))
NN = (((1,), (0,)), ((), ()))


def dot(a, b, dims=NN):
    return lax.dot_general(a, b, dims, preferred_element_type=F32)


def normalized(x):
    return x * lax.rsqrt(jnp.mean(x * x, -1, keepdims=True) + EPS)


def inner_grad_kernel(
    seqs,
    du_ref,
    dproj_ref,
    conv_ref,
    ext_ref,
    normed_ref,
    x_ref,
    u_ref,
    rank_ref,
    dstep_ref,
    dgate_ref,
    w_in_ref,
    w_gate_ref,
    w_x_ref,
    taps_ref,
    after_ref,
    late_ref,
    early_ref,
    gin_ref,
    gx_ref,
    gdt_ref,
    chan_ref,
    gain_ref,
    dconv,
):
    rows, chans = du_ref.shape
    rim = (CONV_TAPS - 1) * seqs
    turn = pl.program_id(0)
    first = pl.multiple_of((pl.num_programs(0) - 1 - turn) * rows, rows)

    @pl.when(turn == 0)
    def _():
        for ref in (gin_ref, gx_ref, gdt_ref, chan_ref, gain_ref):
            ref[...] = jnp.zeros_like(ref)
        dconv[rows:, :] = after_ref[...]

    @pl.when(turn > 0)
    def _():
        dconv[rows:, :] = dconv[:rim, :]

    def by_seq(value):
        return jnp.sum(value.reshape(rows // seqs, seqs, value.shape[-1]), 0)

    d_proj = dproj_ref[...]
    conv = conv_ref[...]
    sig = jax.nn.sigmoid(conv)
    d_conv = (du_ref[...] + dot(d_proj, w_x_ref[...], NT)) * (sig * (1.0 + conv * (1.0 - sig)))
    dconv[:rows, :] = d_conv
    d_inner = jnp.zeros_like(d_conv)
    for tap in range(CONV_TAPS):
        at = (CONV_TAPS - 1 - tap) * seqs
        d_inner = d_inner + taps_ref[tap : tap + 1, :] * dconv[at : at + rows, :]
        ext = ext_ref[pl.ds(pl.multiple_of(first + tap * seqs, seqs), rows), :]
        chan_ref[tap * seqs : (tap + 1) * seqs, :] += by_seq(d_conv * ext)
    chan_ref[CONV_TAPS * seqs :, :] += by_seq(d_conv)
    d_inner = d_inner.astype(BF16)
    part = dot(d_inner, w_in_ref[...]) + dot(dgate_ref[...], w_gate_ref[...])
    half = pl.num_programs(0) // 2

    @pl.when(turn < half)
    def _():
        late_ref[...] = part.astype(BF16)

    @pl.when(turn >= half)
    def _():
        early_ref[...] = part.astype(BF16)

    gain_ref[...] += by_seq(part * normalized(x_ref[...].astype(F32)))
    gin_ref[...] += dot(d_inner, normed_ref[...], TN)
    gx_ref[...] += dot(u_ref[...], d_proj, TN)
    gdt_ref[...] += dot(dstep_ref[...], rank_ref[...], TN)


def output_kernel(shape, peers, *refs):
    micros, group = shape
    early, late, refs = refs[:peers], refs[peers : 2 * peers], refs[2 * peers :]
    x_ref, dres_ref, act_in_ref, gain_ref, grad_ref, act_ref, grad_tok, act_tok = refs
    x = x_ref[...].astype(F32)
    scale = lax.rsqrt(jnp.mean(x * x, -1, keepdims=True) + EPS)
    xhat = x * scale
    is_early = pl.program_id(0) < pl.num_programs(0) // 2
    d_normed = jnp.zeros_like(x)
    for first, second in zip(early, late):
        d_normed = d_normed + jnp.where(is_early, first[...], second[...]).astype(F32)
    scaled = gain_ref[...] * d_normed
    mean = jnp.mean(scaled * xhat, -1, keepdims=True)
    grad = dres_ref[...].astype(F32) + scale * (scaled - xhat * mean)
    seqs = micros * group
    rows, width = x.shape
    count = rows // seqs
    act = act_in_ref[...].astype(F32)
    for k in range(width // LANES):
        grad_tok[k] = grad[:, lanes(k)]
        act_tok[k] = act[:, lanes(k)]
    for m in range(micros):
        for g in range(group):
            at = pl.ds(m * group + g, count, stride=seqs)
            for k in range(width // LANES):
                grad_ref[m, g, :, lanes(k)] = grad_tok[k, at, :]
                act_ref[m, g, :, lanes(k)] = act_tok[k, at, :].astype(BF16)


def scan_call(kernel, arrays, outs, scratch, width, chans, chunk=0, cost=None):
    def spec(shape, kind):
        def place(j, rank=len(shape)):
            at = [0] * rank
            if "t" in kind:
                at[0] = chunk
            if "c" in kind:
                at[-1] = j
            if "r" in kind:
                at[0] = j
            return tuple(at)

        return pl.BlockSpec(shape, place)

    return pl.pallas_call(
        kernel,
        grid=(chans // width,),
        in_specs=[spec(shape, kind) for _, shape, kind in arrays],
        out_specs=[spec(shape, kind) for _, shape, kind in outs],
        out_shape=[a for a, _, _ in outs],
        scratch_shapes=[
            s if not isinstance(s, tuple) else pltpu.VMEM(s, F32) for s in scratch
        ],
        compiler_params=pltpu.CompilerParams(vmem_limit_bytes=62 << 20),
        cost_estimate=cost,
    )(*[a for a, _, _ in arrays])


def per_device(
    inputs,
    out_grad,
    lengths,
    routes,
    slots,
    norm_gains,
    router_matrix,
    input_projection,
    inner_projection,
    step_projection,
    step_bias,
    channel_params,
    output_projection,
    expert_up,
    expert_down,
):
    micros, group, length, width = inputs.shape
    seqs = micros * group
    tokens = length * seqs
    owners = lax.axis_size("fsdp") * lax.axis_size("ctx")
    experts = router_matrix.shape[1]
    capacity = max(2, (25 * group * length + 32 * experts - 1) // (32 * experts))
    slots_each = micros * capacity
    rows = experts * slots_each

    def by_token(value):
        return jnp.moveaxis(value, 2, 0).reshape(tokens, *value.shape[3:])

    narrow = jnp.concatenate(
        [inner_projection, step_projection, channel_params, step_bias[:, None]], 1
    )
    x_cols = inner_projection.shape[1]
    cuts = [x_cols, x_cols + R, x_cols + R + channel_params.shape[1]]
    routing = jnp.concatenate([router_matrix, norm_gains.T], 1)
    joined = narrow.shape[0] == routing.shape[0]
    if joined:
        narrow = jnp.concatenate([narrow, routing], 1)
    narrow_cols = narrow.shape[1]
    pad = -narrow_cols % LANES
    first = jnp.concatenate([input_projection[0], jnp.pad(narrow, ((0, 0), (0, pad)))], 1)
    later = jnp.concatenate([input_projection[1], output_projection], 1)
    full = lax.all_gather(first, OWNERS, axis=0, tiled=True)
    later_full = lax.all_gather(later, OWNERS, axis=0, tiled=True)

    position = lax.axis_index("ctx") * length + jnp.arange(length)
    valid = (position[:, None] < lengths.reshape(1, seqs)).astype(F32).reshape(tokens, 1)
    route = by_token(routes)
    slot = by_token(slots)
    kept = slot >= 0
    kept_f = kept.astype(F32)
    micro_of = (jnp.arange(tokens) // group) % micros
    place = jnp.where(kept, route * slots_each + micro_of * capacity + slot, -1)
    pick = (
        jnp.arange(rows).reshape(experts, slots_each, 1) == place[None, None, :]
    ).astype(BF16)
    grad_tok = by_token(out_grad)
    grad_act = grad_tok.astype(F32) * valid

    def packed(value):
        return jnp.einsum("est,td->esd", pick, value, preferred_element_type=F32).astype(BF16)

    def unpacked(value):
        flat = value.reshape(rows, value.shape[-1])
        return lax.optimization_barrier(dot(pick.reshape(rows, tokens), flat, TN))

    def swap_owners(value):
        return lax.all_to_all(value, OWNERS, split_axis=0, concat_axis=0, tiled=True)

    grad_packed = packed(grad_tok)

    w_in = full[:, :width]
    tail = full[:, width:]
    w_gate, w_out = later_full[:, :width], later_full[:, width:]
    w_x = tail[:, : cuts[0]]
    w_step = tail[:, cuts[0] : cuts[1]]
    channel_f = tail[:, cuts[1] : cuts[2]].astype(F32)
    bias_f = tail[:, cuts[2]].astype(F32)
    if joined:
        full_routing = tail[:, cuts[2] + 1 : cuts[2] + 1 + routing.shape[1]]
    else:
        full_routing = lax.all_gather(routing, OWNERS, axis=0, tiled=True)
    w_router = full_routing[:, :experts]
    gains = full_routing[:, experts:].T.astype(F32)
    chans = channel_f.shape[0]
    taps = channel_f[:, :CONV_TAPS].T
    conv_bias = channel_f[:, CONV_TAPS]
    skip = channel_f[:, CONV_TAPS + 1]
    rates = -jnp.exp(channel_f[:, CONV_TAPS + 2 :]).T

    x_tok = lax.optimization_barrier(by_token(inputs))
    x = x_tok.astype(F32)
    normed1 = (normalized(x) * gains[0]).astype(BF16)
    inner = dot(normed1, w_in, NT).astype(BF16)
    rim = (CONV_TAPS - 1) * seqs
    before = moved(inner[tokens - rim :], 1)
    gate_z = dot(normed1, w_gate, NT)
    extended = jnp.concatenate([before, inner], 0).astype(F32)
    conv = conv_bias
    for tap in range(CONV_TAPS):
        conv = conv + taps[tap] * extended[tap * seqs : tap * seqs + tokens]
    u = jax.nn.silu(conv).astype(BF16)
    u_wide = u.astype(F32)
    proj = tensor_total(dot(u, w_x), BF16)
    rank = proj[:, :R].astype(BF16)
    b_vals = proj[:, R : R + N]
    c_vals = proj[:, R + N :]
    step_pre = dot(rank, w_step, NT) + bias_f
    delta = jax.nn.softplus(step_pre)
    lane_width = 2 * LANES if chans % (2 * LANES) == 0 else LANES
    wide_rates = (N, seqs, lane_width)
    state_block = (N, seqs, lane_width)
    call = functools.partial(scan_call, width=lane_width, chans=chans)

    def both_in(value, steps=length):
        return (value, (steps * seqs, lane_width), "tc")

    def by_chan(value):
        return (value, (*value.shape[:-1], lane_width), "c")

    def by_rows(value, steps=length):
        return (value, (steps * seqs, value.shape[1]), "t")

    def cost(steps, ops):
        elements = steps * seqs * chans * N
        return pl.CostEstimate(flops=300 * ops * elements, bytes_accessed=elements, transcendentals=0)

    def out(shape, dtype=F32):
        return jax.ShapeDtypeStruct(shape, dtype)

    [end] = call(
        end_state_kernel,
        [both_in(delta), both_in(u_wide), by_rows(b_vals), by_chan(rates)],
        [by_chan(out((N + 1, seqs, chans)))],
        [wide_rates, (tokens, N * LANES)],
        cost=cost(length, 6),
    )
    state_end, log_decay = end[:N], end[N]
    state = carried(state_end, log_decay, rates, 1)
    state, grad_packed = lax.optimization_barrier((state, grad_packed))
    grad_rows_raw = swap_owners(grad_packed)
    pieces = 4 if length % (4 * BLK) == 0 else 1
    steps = length // pieces
    y_parts, gated_parts, mixed_parts, start_parts = [], [], [], []
    for piece in range(pieces):
        if piece > 1:
            state, mixed_parts[piece - 2] = lax.optimization_barrier(
                (state, mixed_parts[piece - 2])
            )
        if piece == pieces - 1:
            state, grad_rows_raw = lax.optimization_barrier((state, grad_rows_raw))
        y_part, gated_part, mixed_part, start_part, state = call(
            forward_kernel,
            [
                both_in(delta, steps),
                both_in(u_wide, steps),
                (gate_z, (steps * seqs, lane_width), "tc"),
                by_rows(b_vals, steps),
                by_rows(c_vals, steps),
                by_chan(rates),
                by_chan(skip[None]),
                (w_out, (lane_width, width), "r"),
                by_chan(state),
            ],
            [
                by_chan(out((steps * seqs, chans))),
                by_chan(out((steps * seqs, chans), BF16)),
                (out((steps * seqs, width), BF16), (steps * seqs, width), ""),
                by_chan(out((steps // BLK, N, seqs, chans))),
                by_chan(out((N, seqs, chans))),
            ],
            [wide_rates, (steps * seqs, N * LANES), (steps * seqs, N * LANES), (steps * seqs, width)],
            chunk=piece,
            cost=cost(steps, 10),
        )
        y_parts.append(y_part)
        gated_parts.append(gated_part)
        mixed_parts.append(tensor_total(mixed_part, BF16))
        start_parts.append(start_part)
    y_vals = jnp.concatenate(y_parts, 0)
    gated = jnp.concatenate(gated_parts, 0)
    starts = jnp.concatenate(start_parts, 0)
    silu_z, gate_slope = silu_parts(gate_z)
    resid = x + jnp.concatenate(mixed_parts, 0)

    scale2 = lax.rsqrt(jnp.mean(resid * resid, -1, keepdims=True) + EPS)
    xhat2 = resid * scale2
    normed2 = (xhat2 * gains[1]).astype(BF16)
    probs = jax.nn.softmax(dot(normed2, w_router), -1)
    onehot = (route[:, None] == jnp.arange(experts)).astype(F32)
    gate = jnp.sum(probs * onehot, -1, keepdims=True) * kept_f[:, None]
    peers, here = lax.axis_size("tensor"), lax.axis_index("tensor")
    share = width // peers

    def half(value):
        cut = value[..., :share]
        for peer in range(1, peers):
            cut = jnp.where(here == peer, value[..., peer * share : (peer + 1) * share], cut)
        return cut

    x_rows = tensor_columns(swap_owners(packed(half(normed2))))
    gate_rows = swap_owners(
        jnp.sum(jnp.where(pick > 0, gate[:, 0], 0.0), -1)[:, None, :]
    )
    grad_rows = (jnp.swapaxes(gate_rows, 1, 2) * grad_rows_raw.astype(F32)).astype(BF16)
    up, down = expert_up[0], expert_down[0]

    def product(a, b, terms):
        return jnp.einsum(terms, a, b, preferred_element_type=F32)

    hidden = product(x_rows, up, "srd,df->srf")
    act_float, gelu_pull = jax.vjp(lambda v: jax.nn.gelu(v, approximate=True), hidden)
    act = act_float.astype(BF16)
    back_y = swap_owners(tensor_share(product(act, down, "srf,fd->srd")).astype(BF16))
    d_hidden = gelu_pull(product(grad_rows, down, "srd,fd->srf"))[0].astype(BF16)
    back_x = swap_owners(tensor_share(product(d_hidden, up, "srf,df->srd")).astype(BF16))
    grad_up = product(x_rows, d_hidden, "srd,srf->df")
    grad_down = product(act, grad_rows, "srf,srd->fd")
    expert_y = unpacked(back_y)
    expert_dx = unpacked(back_x)
    x_half = half(xhat2)
    gain_half = half(gains[1])
    grad_half = half(grad_act)
    router_half = half(w_router.T)
    sums = jnp.stack(
        [jnp.sum(grad_half * expert_y, -1), jnp.sum(gain_half * expert_dx * x_half, -1)]
    )
    sums = tensor_total(sums, F32)
    gate_grad = sums[0][:, None]
    d_logits = (gate_grad * gate * (onehot - probs)).astype(BF16)
    grad_router = dot(normed2, d_logits, TN)
    by_router = dot((xhat2 * gains[1]).astype(BF16), w_router)
    mean_term = (
        sums[1][:, None] + jnp.sum(d_logits.astype(F32) * by_router, -1, keepdims=True)
    ) / width
    d_normed2 = expert_dx + dot(d_logits, router_half)
    gain_grad2 = tensor_columns(jnp.sum(d_normed2 * x_half, 0, keepdims=True))[0]
    d_resid_half = grad_half + scale2 * (gain_half * d_normed2 - x_half * mean_term)
    act_half = (valid * (half(resid) + gate * expert_y)).astype(BF16)

    d_mixed = tensor_columns(d_resid_half.astype(BF16))
    d_mixed, act_half = lax.optimization_barrier((d_mixed, act_half))
    activations = tensor_columns(act_half)
    d_gated = dot(d_mixed, w_out, NT)
    d_y = d_gated * silu_z
    [start_grad] = call(
        start_grad_kernel,
        [both_in(delta), both_in(d_y), by_rows(c_vals), by_chan(rates)],
        [by_chan(out((N, seqs, chans)))],
        [wide_rates, (tokens, N * LANES)],
        cost=cost(length, 6),
    )
    d_gate_z = (d_gated * y_vals * gate_slope).astype(BF16)

    def owned(value):
        return lax.psum_scatter(
            value.astype(BF16), OWNERS, scatter_dimension=0, tiled=True
        ).astype(F32)

    mine_early = owned(
        jnp.concatenate([dot(d_gate_z, normed1, TN), dot(gated, d_mixed, TN)], 1)
    )
    grad_end = carried(start_grad, log_decay, rates, -1)
    w_step_wide = jnp.pad(w_step, ((0, 0), (0, LANES - R)))
    d_step, du_part, d_proj_part, rate_grad, bias_sums, skip_sums = call(
        backward_kernel,
        [
            both_in(delta),
            both_in(u_wide),
            both_in(d_y),
            (jax.nn.sigmoid(step_pre), (tokens, lane_width), "tc"),
            by_rows(b_vals),
            by_rows(c_vals),
            by_chan(rates),
            by_chan(skip[None]),
            (w_step_wide, (lane_width, LANES), "r"),
            by_chan(starts),
            by_chan(grad_end),
        ],
        [
            by_chan(out((tokens, chans), BF16)),
            by_chan(out((tokens, chans))),
            (out((tokens, LANES), BF16), (tokens, LANES), ""),
            by_chan(out((N, seqs, chans))),
            by_chan(out((seqs, chans))),
            by_chan(out((seqs, chans))),
        ],
        [
            wide_rates,
            (tokens, N * LANES),
            (tokens, N * LANES),
            (BLK + 1, N, seqs, lane_width),
            (BLK, N, seqs, lane_width),
            (BLK * seqs, N * LANES),
            (BLK * seqs, N * LANES),
            (BLK * seqs, lane_width),
            (tokens, LANES),
            pltpu.VMEM((2 * N * LANES, LANES), BF16),
        ],
        cost=cost(length, 24),
    )
    d_step, mine_early, activations = lax.optimization_barrier((d_step, mine_early, activations))
    d_proj = tensor_total(d_proj_part, BF16).astype(BF16)
    step_bias_grad = jnp.sum(bias_sums, 0)
    skip_grad = jnp.sum(skip_sums, 0)
    w_x_wide = jnp.pad(w_x, ((0, 0), (0, LANES - x_cols)))
    rim_u = du_part[:rim] + dot(d_proj[:rim], w_x_wide, NT)
    after = moved(rim_u * silu_parts(conv[:rim])[1], -1)
    steps = length // 4
    block = steps * seqs
    turns = length // steps

    def from_end(value):
        return value, pl.BlockSpec((block, value.shape[1]), lambda i: (turns - 1 - i, 0))

    def whole(value):
        return value, pl.BlockSpec(value.shape, lambda i: (0, 0))

    arrays = [
        from_end(du_part),
        from_end(d_proj),
        from_end(conv),
        whole(extended),
        from_end(normed1),
        from_end(x_tok),
        from_end(u),
        from_end(rank),
        from_end(d_step),
        from_end(d_gate_z),
        whole(w_in),
        whole(w_gate),
        whole(w_x_wide),
        whole(taps),
        whole(after),
    ]
    results = [
        (
            out((tokens // 2, width), BF16),
            pl.BlockSpec((block, width), lambda i: (jnp.maximum(turns // 2 - 1 - i, 0), 0)),
        ),
        (
            out((tokens // 2, width), BF16),
            pl.BlockSpec(
                (block, width), lambda i: (jnp.minimum(turns - 1 - i, turns // 2 - 1), 0)
            ),
        ),
        whole(out((chans, width))),
        whole(out((chans, LANES))),
        whole(out((chans, R))),
        whole(out(((CONV_TAPS + 1) * seqs, chans))),
        whole(out((seqs, width))),
    ]
    late_part, early_part, grad_in, grad_xproj, grad_dt, conv_sums, gain_sums = pl.pallas_call(
        functools.partial(inner_grad_kernel, seqs),
        grid=(turns,),
        in_specs=[spec for _, spec in arrays],
        out_specs=[spec for _, spec in results],
        out_shape=[value for value, _ in results],
        scratch_shapes=[pltpu.VMEM((block + rim, chans), F32)],
        compiler_params=pltpu.CompilerParams(vmem_limit_bytes=62 << 20),
    )(*[value for value, _ in arrays])
    grad_xproj = grad_xproj[:, :x_cols]
    conv_sums = jnp.sum(conv_sums.reshape(CONV_TAPS + 1, seqs, chans), 1)
    gain_grad1 = jnp.sum(gain_sums, 0)

    narrow_grads = jnp.concatenate(
        [
            grad_xproj,
            grad_dt,
            conv_sums.T,
            skip_grad[:, None],
            (jnp.sum(rate_grad, 1) * rates).T,
            step_bias_grad[:, None],
        ],
        1,
    )
    routing_grads = jnp.concatenate([grad_router, gain_grad1[:, None], gain_grad2[:, None]], 1)
    if joined:
        narrow_grads = jnp.concatenate([narrow_grads, routing_grads], 1)
    wide_grads = jnp.concatenate(
        [grad_in, jnp.pad(narrow_grads, ((0, 0), (0, pad)))], 1
    )

    halves = [late_part, early_part]
    if peers == 2:
        exchanged = [swapped(part) for part in halves]
    else:
        exchanged = [lax.all_gather(part, "tensor") for part in halves]
    mine, exchanged = halved(wide_grads, exchanged)
    normed_parts = []
    for own, others in zip(halves, exchanged):
        if peers == 2:
            normed_parts.append([own, others])
        else:
            normed_parts.append([others[k] for k in range(peers)])
    late_parts, early_parts = normed_parts

    def rows_of(value):
        return value, pl.BlockSpec((block, value.shape[1]), lambda i: (i, 0))

    def early_rows(value):
        return value, pl.BlockSpec((block, width), lambda i: (jnp.minimum(i, turns // 2 - 1), 0))

    def late_rows(value):
        return value, pl.BlockSpec((block, width), lambda i: (jnp.maximum(i - turns // 2, 0), 0))

    arrays = (
        [early_rows(part) for part in early_parts]
        + [late_rows(part) for part in late_parts]
        + [rows_of(x_tok), rows_of(d_mixed), rows_of(activations), whole(gains[:1])]
    )
    out_spec = pl.BlockSpec((micros, group, steps, width), lambda i: (0, 0, i, 0))
    input_grad, activations = pl.pallas_call(
        functools.partial(output_kernel, (micros, group), peers),
        grid=(turns,),
        in_specs=[spec for _, spec in arrays],
        out_specs=[out_spec, out_spec],
        out_shape=[out(inputs.shape), out(inputs.shape, BF16)],
        scratch_shapes=[pltpu.VMEM((width // LANES, block, LANES), F32)] * 2,
        compiler_params=pltpu.CompilerParams(vmem_limit_bytes=62 << 20),
    )(*[value for value, _ in arrays])
    mine_tail = mine[:, width:]
    if joined:
        mine_routing = mine_tail[:, cuts[2] + 1 : cuts[2] + 1 + routing.shape[1]]
    else:
        mine_routing, _ = halved(routing_grads)
    gains_out = jnp.stack(
        [tensor_total(mine_routing[None, :, experts], F32)[0], mine_routing[:, experts + 1]]
    )
    return (
        activations,
        input_grad,
        gains_out,
        mine_routing[:, :experts],
        jnp.stack([mine[:, :width], mine_early[:, :width]]),
        mine_tail[:, : cuts[0]],
        mine_tail[:, cuts[0] : cuts[1]],
        mine_tail[:, cuts[2]],
        mine_tail[:, cuts[1] : cuts[2]],
        mine_early[:, width:],
        grad_up[None],
        grad_down[None],
    )


def solution(mesh):
    return jax.shard_map(
        per_device,
        mesh=mesh,
        in_specs=(
            P(None, "fsdp", "ctx", None),
            P(None, "fsdp", "ctx", None),
            P(None, "fsdp"),
            P(None, "fsdp", "ctx"),
            P(None, "fsdp", "ctx"),
            P(None, ("fsdp", "ctx")),
            P(("fsdp", "ctx"), None),
            P(None, ("fsdp", "ctx", "tensor"), None),
            P(("fsdp", "ctx", "tensor"), None),
            P(("fsdp", "ctx", "tensor"), None),
            P(("fsdp", "ctx", "tensor")),
            P(("fsdp", "ctx", "tensor"), None),
            P(("fsdp", "ctx", "tensor"), None),
            P(("fsdp", "ctx"), None, "tensor"),
            P(("fsdp", "ctx"), "tensor", None),
        ),
        out_specs=(
            P(None, "fsdp", "ctx", None),
            P(None, "fsdp", "ctx", None),
            P(None, ("fsdp", "ctx")),
            P(("fsdp", "ctx"), None),
            P(None, ("fsdp", "ctx", "tensor"), None),
            P(("fsdp", "ctx", "tensor"), None),
            P(("fsdp", "ctx", "tensor"), None),
            P(("fsdp", "ctx", "tensor")),
            P(("fsdp", "ctx", "tensor"), None),
            P(("fsdp", "ctx", "tensor"), None),
            P(("fsdp", "ctx"), None, "tensor"),
            P(("fsdp", "ctx"), "tensor", None),
        ),
        check_vma=False,
    )
```

```python
import functools

import jax
import jax.numpy as jnp
from jax import lax
from jax.experimental import pallas as pl
from jax.experimental.pallas import tpu as pltpu
from jax.sharding import PartitionSpec as P

N = 16
CONV_TAPS = 4
R = 48
EPS = 1e-05
BLK = 8
LANES = 128
F32 = jnp.float32
BF16 = jnp.bfloat16
OWNERS = ("fsdp", "ctx")


def silu_parts(value):
    sig = jax.nn.sigmoid(value)
    return value * sig, sig * (1.0 + value * (1.0 - sig))


def swapped(value):
    return lax.ppermute(value, "tensor", [(0, 1), (1, 0)])


def tensor_total(value, dtype):
    sent = value.astype(dtype)
    if lax.axis_size("tensor") == 2:
        return sent.astype(F32) + swapped(sent).astype(F32)
    return jnp.sum(lax.all_gather(sent, "tensor").astype(F32), axis=0)


def tensor_columns(value):
    if lax.axis_size("tensor") == 2:
        other = swapped(value)
        first = lax.axis_index("tensor") == 0
        return jnp.concatenate(
            [jnp.where(first, value, other), jnp.where(first, other, value)], -1
        )
    return lax.all_gather(value, "tensor", axis=value.ndim - 1, tiled=True)


def halved(value, beside=()):
    beside = list(beside)
    sizes = [lax.axis_size(axis) for axis in OWNERS]
    bits = [(axis, 1 << k) for axis, size in zip(OWNERS, sizes) for k in reversed(range(size.bit_length() - 1))]
    rows = value.shape[0] >> len(bits)
    for place in reversed(range(len(bits))):
        axis, bit = bits[place]
        view = value.reshape(1 << place, 2, rows, value.shape[-1])
        high = (lax.axis_index(axis) & bit) != 0
        own = jnp.where(high, view[:, 1], view[:, 0])
        other = jnp.where(high, view[:, 0], view[:, 1]).astype(BF16)
        got = lax.ppermute(other, axis, [(i, i ^ bit) for i in range(lax.axis_size(axis))])
        value = own.astype(F32) + got.astype(F32)
        turn = len(bits) - 1 - place
        if 0 < turn <= len(beside):
            turn -= 1
            value, beside[turn] = lax.optimization_barrier((value, beside[turn]))
    return value.reshape(rows, value.shape[-1]), beside


def moved(value, by):
    peers = lax.axis_size("ctx")
    pairs = [(i, i + by) for i in range(peers) if 0 <= i + by < peers]
    return lax.ppermute(value, "ctx", pairs)


MESH = pl.DeviceIdType.MESH


def greet(peers):
    barrier = pltpu.get_barrier_semaphore()
    for peer in peers:
        pl.semaphore_signal(barrier, inc=1, device_id=peer, device_id_type=MESH)
    pl.semaphore_wait(barrier, len(peers))


def carry_kernel(sign, ranges, peers, end_ref, log_ref, r_ref, *refs):
    if peers:
        own_ref, out_ref, others_ref, sent, got, log_out, send_sem, recv_sem, own_sem, others_sem = refs
    else:
        out_ref, sent, got, log_out, send_sem, recv_sem = refs
    turns, groups, _, width = sent.shape
    seqs = log_ref.shape[0]
    fsdp, me, tensor = lax.axis_index("fsdp"), lax.axis_index("ctx"), lax.axis_index("tensor")

    def peer(by):
        return (fsdp, lax.rem(me + by + ranges, ranges), tensor)

    shifts = [sign * (1 << turn) for turn in range(turns)]
    partners = [(fsdp, me, lax.rem(tensor + by, peers)) for by in range(1, peers)]
    near = sorted({s % ranges for s in shifts} | {-s % ranges for s in shifts})
    greet([peer(by) for by in near] + partners)
    beside = [
        pltpu.make_async_remote_copy(
            src_ref=own_ref,
            dst_ref=others_ref.at[k],
            send_sem=own_sem.at[k],
            recv_sem=others_sem.at[k],
            device_id=partner,
            device_id_type=MESH,
        )
        for k, partner in enumerate(partners)
    ]
    for extra in beside:
        extra.start()

    def copy(turn, group):
        return pltpu.make_async_remote_copy(
            src_ref=sent.at[turn, group],
            dst_ref=got.at[turn, group],
            send_sem=send_sem.at[turn, group],
            recv_sem=recv_sem.at[turn, group],
            device_id=peer(shifts[turn]),
            device_id_type=MESH,
        )

    def decayed(log, cols, n):
        return jnp.exp(log * r_ref[n : n + 1, cols])

    def receive(turn, group):
        copy(turn, group).wait_recv()
        cols = slice(group * width, (group + 1) * width)
        reach = 1 << turn
        real = (me >= reach) if sign > 0 else (me < ranges - reach)

        def part(k):
            rows = got[turn, group, k * seqs : (k + 1) * seqs, :].astype(F32)
            return jnp.where(real, rows, 0.0)

        log = part(N) + part(N + 1)
        if turn == 0:
            for n in range(N):
                out_ref[n, :, cols] = part(n)
            log_out[:, cols] = log
        else:
            late = log_out[:, cols]
            for n in range(N):
                out_ref[n, :, cols] = out_ref[n, :, cols] + decayed(late, cols, n) * part(n)
            log_out[:, cols] = late + log

    for turn in range(turns):
        for group in range(groups):
            cols = slice(group * width, (group + 1) * width)
            own_log = log_ref[:, cols]
            if turn > 0:
                receive(turn - 1, group)
            for n in range(0, N, 2):
                pair = []
                for k in (n, n + 1):
                    value = end_ref[k, :, cols]
                    if turn > 0:
                        value = value + decayed(own_log, cols, k) * out_ref[k, :, cols]
                    pair.append(value)
                sent[turn, group, n * seqs : (n + 2) * seqs, :] = jnp.concatenate(pair, 0).astype(
                    BF16
                )
            log = own_log if turn == 0 else own_log + log_out[:, cols]
            high = log.astype(BF16).astype(F32)
            sent[turn, group, N * seqs :, :] = jnp.concatenate([high, log - high], 0).astype(BF16)
            copy(turn, group).start()
    for group in range(groups):
        receive(turns - 1, group)
    for turn in range(turns):
        for group in range(groups):
            copy(turn, group).wait_send()
    for extra in beside:
        extra.wait()


def carried(end, log_decay, rates, sign, ident, shared=None):
    _, seqs, chans = end.shape
    ranges = lax.axis_size("ctx")
    turns = (ranges - 1).bit_length()
    groups = 3 if chans % (3 * LANES) == 0 else 1
    block = (turns, groups, (N + 2) * seqs, chans // groups)
    vmem = pl.BlockSpec(memory_space=pltpu.VMEM)
    anywhere = pl.BlockSpec(memory_space=pl.ANY)
    peers = 0 if shared is None else lax.axis_size("tensor")
    state = jax.ShapeDtypeStruct((N, seqs, chans), F32)
    scratch = [
        pltpu.VMEM(block, BF16),
        pltpu.VMEM(block, BF16),
        pltpu.VMEM((seqs, chans), F32),
        pltpu.SemaphoreType.DMA((turns, groups)),
        pltpu.SemaphoreType.DMA((turns, groups)),
    ]
    if peers:
        others = jax.ShapeDtypeStruct((peers - 1, *shared.shape), shared.dtype)
        scratch += [pltpu.SemaphoreType.DMA((peers - 1,)), pltpu.SemaphoreType.DMA((peers - 1,))]
    return pl.pallas_call(
        functools.partial(carry_kernel, sign, ranges, peers),
        in_specs=[vmem] * 3 + [anywhere] * bool(peers),
        out_specs=[vmem, anywhere] if peers else vmem,
        out_shape=[state, others] if peers else state,
        scratch_shapes=scratch,
        compiler_params=pltpu.CompilerParams(
            collective_id=ident, has_side_effects=True, vmem_limit_bytes=32 << 20
        ),
        cost_estimate=pl.CostEstimate(flops=20 << 30, bytes_accessed=1 << 20, transcendentals=0),
    )(end[:N], log_decay, rates, *([shared] if peers else []))


def spread_matrix():
    rows = lax.broadcasted_iota(jnp.int32, (2 * N, N * LANES), 0) % N
    cols = lax.broadcasted_iota(jnp.int32, (2 * N, N * LANES), 1) // LANES
    return (rows == cols).astype(F32).astype(BF16)


def spread_into(pairs, rows):
    def turn(i, _):
        matrix = spread_matrix()
        at = pl.ds(pl.multiple_of(i * LANES, LANES), LANES)
        for source, target in pairs:
            value = source[at, :]
            high = value.astype(BF16)
            low = (value - high.astype(F32)).astype(BF16)
            target[at, :] = jnp.dot(
                jnp.concatenate([high, low], 1), matrix, preferred_element_type=F32
            )
        return 0

    lax.fori_loop(0, rows // LANES, turn, 0)


def lanes(k):
    return slice(k * LANES, (k + 1) * LANES)


def end_state_kernel(d_ref, u_ref, b_ref, r_ref, end_ref, rb, bb):
    rows, width = d_ref.shape
    seqs = rb.shape[1]
    length = rows // seqs
    parts = width // LANES
    for n in range(N):
        rb[n] = jnp.broadcast_to(r_ref[n : n + 1, :], (seqs, width))

    @pl.when(pl.program_id(0) == 0)
    def _():
        spread_into([(b_ref, bb)], rows)

    def body(t, carry):
        hs, total = carry
        row = pl.ds(pl.multiple_of(t * seqs, seqs), seqs)
        d = d_ref[row, :]
        du = d * u_ref[row, :]
        new = []
        for n in range(N):
            bn = bb[row, lanes(n)]
            for k in range(parts):
                a = jnp.exp(d[:, lanes(k)] * rb[n, :, lanes(k)])
                new.append(a * hs[n * parts + k] + du[:, lanes(k)] * bn)
        return tuple(new), total + d

    zero = jnp.zeros((seqs, LANES), F32)
    hs, total = lax.fori_loop(
        0, length, body, ((zero,) * (N * parts), jnp.zeros((seqs, width), F32)), unroll=4
    )
    for n in range(N):
        for k in range(parts):
            end_ref[n, :, lanes(k)] = hs[n * parts + k]
    end_ref[N] = total


def forward_kernel(
    d_ref,
    u_ref,
    z_ref,
    b_ref,
    c_ref,
    r_ref,
    skip_ref,
    w_ref,
    h0_ref,
    y_ref,
    gated_ref,
    mixed_ref,
    st_ref,
    h1_ref,
    rb,
    bb,
    cb,
    total,
):
    rows, width = d_ref.shape
    seqs = rb.shape[1]
    length = rows // seqs
    parts = width // LANES
    for n in range(N):
        rb[n] = jnp.broadcast_to(r_ref[n : n + 1, :], (seqs, width))

    @pl.when(pl.program_id(0) == 0)
    def _():
        spread_into([(b_ref, bb), (c_ref, cb)], rows)
        total[...] = jnp.zeros_like(total)

    def block(i, hs):
        for n in range(N):
            for k in range(parts):
                st_ref[i, n, :, lanes(k)] = hs[n * parts + k]

        def body(step, hs):
            t = i * BLK + step
            row = pl.ds(pl.multiple_of(t * seqs, seqs), seqs)
            d = d_ref[row, :]
            u = u_ref[row, :]
            du = d * u
            ys = [u[:, lanes(k)] * skip_ref[:, lanes(k)] for k in range(parts)]
            new = []
            for n in range(N):
                bn = bb[row, lanes(n)]
                cn = cb[row, lanes(n)]
                for k in range(parts):
                    a = jnp.exp(d[:, lanes(k)] * rb[n, :, lanes(k)])
                    h = a * hs[n * parts + k] + du[:, lanes(k)] * bn
                    ys[k] = ys[k] + h * cn
                    new.append(h)
            for k in range(parts):
                y_ref[row, lanes(k)] = ys[k]
            return tuple(new)

        return lax.fori_loop(0, BLK, body, hs, unroll=4)

    hs = lax.fori_loop(
        0,
        length // BLK,
        block,
        tuple(h0_ref[n, :, lanes(k)] for n in range(N) for k in range(parts)),
    )
    for n in range(N):
        for k in range(parts):
            h1_ref[n, :, lanes(k)] = hs[n * parts + k]
    z = z_ref[...]
    gated = (y_ref[...] * (z * jax.nn.sigmoid(z))).astype(BF16)
    gated_ref[...] = gated
    total[...] += jnp.dot(gated, w_ref[...], preferred_element_type=F32)
    mixed_ref[...] = total[...].astype(BF16)


def start_grad_kernel(d_ref, dy_ref, c_ref, r_ref, g_ref, rb, cb):
    rows, width = d_ref.shape
    seqs = rb.shape[1]
    length = rows // seqs
    parts = width // LANES
    for n in range(N):
        rb[n] = jnp.broadcast_to(r_ref[n : n + 1, :], (seqs, width))

    @pl.when(pl.program_id(0) == 0)
    def _():
        spread_into([(c_ref, cb)], rows)

    def body(i, gs):
        t = length - 1 - i
        row = pl.ds(pl.multiple_of(t * seqs, seqs), seqs)
        d = d_ref[row, :]
        dy = dy_ref[row, :]
        new = []
        for n in range(N):
            cn = cb[row, lanes(n)]
            for k in range(parts):
                a = jnp.exp(d[:, lanes(k)] * rb[n, :, lanes(k)])
                new.append(a * (gs[n * parts + k] + dy[:, lanes(k)] * cn))
        return tuple(new)

    zero = jnp.zeros((seqs, LANES), F32)
    gs = lax.fori_loop(0, length, body, (zero,) * (N * parts), unroll=4)
    for n in range(N):
        for k in range(parts):
            g_ref[n, :, lanes(k)] = gs[n * parts + k]


def backward_kernel(
    d_ref,
    u_ref,
    dy_ref,
    sig_ref,
    b_ref,
    c_ref,
    r_ref,
    skip_ref,
    w_ref,
    st_ref,
    g0_ref,
    dstep_ref,
    du_ref,
    dproj_ref,
    rg_ref,
    bias_ref,
    skipg_ref,
    rb,
    bb,
    cb,
    hb,
    ab,
    pb,
    pc,
    dsb,
    total,
    columns,
):
    rows, width = d_ref.shape
    seqs = rb.shape[1]
    length = rows // seqs
    parts = width // LANES
    group = pl.program_id(0)
    for n in range(N):
        rb[n] = jnp.broadcast_to(r_ref[n : n + 1, :], (seqs, width))

    @pl.when(group == 0)
    def _():
        spread_into([(b_ref, bb), (c_ref, cb)], rows)
        total[...] = jnp.zeros_like(total)
        source = lax.broadcasted_iota(jnp.int32, columns.shape, 0) // LANES
        target = lax.broadcasted_iota(jnp.int32, columns.shape, 1)
        columns[...] = (source + R == target).astype(F32).astype(BF16)

    rg_ref[...] = jnp.zeros_like(rg_ref)
    bias_ref[...] = jnp.zeros_like(bias_ref)
    skipg_ref[...] = jnp.zeros_like(skipg_ref)

    def block(turn, gs):
        i = length // BLK - 1 - turn

        def again(step, hs):
            t = i * BLK + step
            row = pl.ds(pl.multiple_of(t * seqs, seqs), seqs)
            d = d_ref[row, :]
            du = d * u_ref[row, :]
            new = []
            for n in range(N):
                bn = bb[row, lanes(n)]
                for k in range(parts):
                    a = jnp.exp(d[:, lanes(k)] * rb[n, :, lanes(k)])
                    h = a * hs[n * parts + k] + du[:, lanes(k)] * bn
                    ab[step, n, :, lanes(k)] = a
                    hb[step + 1, n, :, lanes(k)] = h
                    new.append(h)
            return tuple(new)

        hs = tuple(st_ref[i, n, :, lanes(k)] for n in range(N) for k in range(parts))
        for n in range(N):
            for k in range(parts):
                hb[0, n, :, lanes(k)] = hs[n * parts + k]
        lax.fori_loop(0, BLK, again, hs, unroll=4)

        def back(turn, gs):
            step = BLK - 1 - turn
            t = i * BLK + step
            row = pl.ds(pl.multiple_of(t * seqs, seqs), seqs)
            here = pl.ds(pl.multiple_of(step * seqs, seqs), seqs)
            d = d_ref[row, :]
            u = u_ref[row, :]
            dy = dy_ref[row, :]
            du = d * u
            prods = [jnp.zeros((seqs, LANES), F32) for _ in range(parts)]
            steps = [jnp.zeros((seqs, LANES), F32) for _ in range(parts)]
            new = []
            for n in range(N):
                bn = bb[row, lanes(n)]
                cn = cb[row, lanes(n)]
                b_sum = c_sum = None
                for k in range(parts):
                    g = gs[n * parts + k] + cn * dy[:, lanes(k)]
                    c_term = hb[step + 1, n, :, lanes(k)] * dy[:, lanes(k)]
                    b_term = g * du[:, lanes(k)]
                    c_sum = c_term if k == 0 else c_sum + c_term
                    b_sum = b_term if k == 0 else b_sum + b_term
                    prods[k] = prods[k] + g * bn
                    carried_g = g * ab[step, n, :, lanes(k)]
                    decay_g = carried_g * hb[step, n, :, lanes(k)]
                    steps[k] = steps[k] + decay_g * rb[n, :, lanes(k)]
                    rg_ref[n, :, lanes(k)] = rg_ref[n, :, lanes(k)] + decay_g * d[:, lanes(k)]
                    new.append(carried_g)
                pb[here, lanes(n)] = b_sum
                pc[here, lanes(n)] = c_sum
            skipg_ref[...] += dy * u
            for k in range(parts):
                dsb[here, lanes(k)] = steps[k] + prods[k] * u[:, lanes(k)]
                du_ref[row, lanes(k)] = (
                    prods[k] * d[:, lanes(k)] + dy[:, lanes(k)] * skip_ref[:, lanes(k)]
                )
            return tuple(new)

        gs = lax.fori_loop(0, BLK, back, gs, unroll=2)
        at = pl.ds(pl.multiple_of(i * BLK * seqs, BLK * seqs), BLK * seqs)
        d_step = (dsb[...] * sig_ref[at, :]).astype(BF16)
        dstep_ref[at, :] = d_step
        bias_ref[...] += jnp.sum(d_step.astype(F32).reshape(BLK, seqs, width), 0)
        total[at, :] += (
            jnp.dot(d_step, w_ref[...], preferred_element_type=F32)
            + jnp.dot(pb[...].astype(BF16), columns[: N * LANES], preferred_element_type=F32)
            + jnp.dot(pc[...].astype(BF16), columns[N * LANES :], preferred_element_type=F32)
        )
        return gs

    lax.fori_loop(
        0,
        length // BLK,
        block,
        tuple(g0_ref[n, :, lanes(k)] for n in range(N) for k in range(parts)),
    )

    @pl.when(group == pl.num_programs(0) - 1)
    def _():
        dproj_ref[...] = total[...].astype(BF16)


TN = (((0,), (0,)), ((), ()))
NT = (((1,), (1,)), ((), ()))
NN = (((1,), (0,)), ((), ()))


def dot(a, b, dims=NN):
    return lax.dot_general(a, b, dims, preferred_element_type=F32)


def normalized(x):
    return x * lax.rsqrt(jnp.mean(x * x, -1, keepdims=True) + EPS)


def inner_grad_kernel(
    seqs,
    du_ref,
    dproj_ref,
    conv_ref,
    ext_ref,
    normed_ref,
    x_ref,
    u_ref,
    rank_ref,
    dstep_ref,
    dgate_ref,
    w_in_ref,
    w_gate_ref,
    w_x_ref,
    taps_ref,
    after_ref,
    late_ref,
    early_ref,
    gin_ref,
    gx_ref,
    gdt_ref,
    chan_ref,
    gain_ref,
    dconv,
):
    rows, chans = du_ref.shape
    rim = (CONV_TAPS - 1) * seqs
    turn = pl.program_id(0)
    first = pl.multiple_of((pl.num_programs(0) - 1 - turn) * rows, rows)

    @pl.when(turn == 0)
    def _():
        for ref in (gin_ref, gx_ref, gdt_ref, chan_ref, gain_ref):
            ref[...] = jnp.zeros_like(ref)
        dconv[rows:, :] = after_ref[...]

    @pl.when(turn > 0)
    def _():
        dconv[rows:, :] = dconv[:rim, :]

    def by_seq(value):
        return jnp.sum(value.reshape(rows // seqs, seqs, value.shape[-1]), 0)

    d_proj = dproj_ref[...]
    conv = conv_ref[...]
    sig = jax.nn.sigmoid(conv)
    d_conv = (du_ref[...] + dot(d_proj, w_x_ref[...], NT)) * (sig * (1.0 + conv * (1.0 - sig)))
    dconv[:rows, :] = d_conv
    d_inner = jnp.zeros_like(d_conv)
    for tap in range(CONV_TAPS):
        at = (CONV_TAPS - 1 - tap) * seqs
        d_inner = d_inner + taps_ref[tap : tap + 1, :] * dconv[at : at + rows, :]
        ext = ext_ref[pl.ds(pl.multiple_of(first + tap * seqs, seqs), rows), :]
        chan_ref[tap * seqs : (tap + 1) * seqs, :] += by_seq(d_conv * ext)
    chan_ref[CONV_TAPS * seqs :, :] += by_seq(d_conv)
    d_inner = d_inner.astype(BF16)
    part = dot(d_inner, w_in_ref[...]) + dot(dgate_ref[...], w_gate_ref[...])
    half = pl.num_programs(0) // 2

    @pl.when(turn < half)
    def _():
        late_ref[...] = part.astype(BF16)

    @pl.when(turn >= half)
    def _():
        early_ref[...] = part.astype(BF16)

    gain_ref[...] += by_seq(part * normalized(x_ref[...].astype(F32)))
    gin_ref[...] += dot(d_inner, normed_ref[...], TN)
    gx_ref[...] += dot(u_ref[...], d_proj, TN)
    gdt_ref[...] += dot(dstep_ref[...], rank_ref[...], TN)


def output_kernel(shape, peers, *refs):
    micros, group = shape
    early, late, refs = refs[:peers], refs[peers : 2 * peers], refs[2 * peers :]
    x_ref, dres_ref, act_own_ref, act_others_ref, gain_ref, grad_ref, act_ref, grad_tok, act_tok = refs
    x = x_ref[...].astype(F32)
    scale = lax.rsqrt(jnp.mean(x * x, -1, keepdims=True) + EPS)
    xhat = x * scale
    is_early = pl.program_id(0) < pl.num_programs(0) // 2
    d_normed = jnp.zeros_like(x)
    for first, second in zip(early, late):
        d_normed = d_normed + jnp.where(is_early, first[...], second[...]).astype(F32)
    scaled = gain_ref[...] * d_normed
    mean = jnp.mean(scaled * xhat, -1, keepdims=True)
    grad = dres_ref[...].astype(F32) + scale * (scaled - xhat * mean)
    seqs = micros * group
    rows, width = x.shape
    count = rows // seqs
    tensor = lax.axis_index("tensor")
    pieces = []
    for owner in range(peers):
        piece = act_own_ref[...].astype(F32)
        for by in range(1, peers):
            here = lax.rem(tensor + peers - by, peers) == owner
            piece = jnp.where(here, act_others_ref[by - 1].astype(F32), piece)
        pieces.append(piece)
    act = jnp.concatenate(pieces, 1)
    for k in range(width // LANES):
        grad_tok[k] = grad[:, lanes(k)]
        act_tok[k] = act[:, lanes(k)]
    for m in range(micros):
        for g in range(group):
            at = pl.ds(m * group + g, count, stride=seqs)
            for k in range(width // LANES):
                grad_ref[m, g, :, lanes(k)] = grad_tok[k, at, :]
                act_ref[m, g, :, lanes(k)] = act_tok[k, at, :].astype(BF16)


def scan_call(kernel, arrays, outs, scratch, width, chans, chunk=0, cost=None):
    def spec(shape, kind):
        def place(j, rank=len(shape)):
            at = [0] * rank
            if "t" in kind:
                at[0] = chunk
            if "c" in kind:
                at[-1] = j
            if "r" in kind:
                at[0] = j
            return tuple(at)

        return pl.BlockSpec(shape, place)

    return pl.pallas_call(
        kernel,
        grid=(chans // width,),
        in_specs=[spec(shape, kind) for _, shape, kind in arrays],
        out_specs=[spec(shape, kind) for _, shape, kind in outs],
        out_shape=[a for a, _, _ in outs],
        scratch_shapes=[
            s if not isinstance(s, tuple) else pltpu.VMEM(s, F32) for s in scratch
        ],
        compiler_params=pltpu.CompilerParams(vmem_limit_bytes=62 << 20),
        cost_estimate=cost,
    )(*[a for a, _, _ in arrays])


def per_device(
    inputs,
    out_grad,
    lengths,
    routes,
    slots,
    norm_gains,
    router_matrix,
    input_projection,
    inner_projection,
    step_projection,
    step_bias,
    channel_params,
    output_projection,
    expert_up,
    expert_down,
):
    micros, group, length, width = inputs.shape
    seqs = micros * group
    tokens = length * seqs
    owners = lax.axis_size("fsdp") * lax.axis_size("ctx")
    experts = router_matrix.shape[1]
    capacity = max(2, (25 * group * length + 32 * experts - 1) // (32 * experts))
    slots_each = micros * capacity
    rows = experts * slots_each

    def by_token(value):
        return jnp.moveaxis(value, 2, 0).reshape(tokens, *value.shape[3:])

    narrow = jnp.concatenate(
        [inner_projection, step_projection, channel_params, step_bias[:, None]], 1
    )
    x_cols = inner_projection.shape[1]
    cuts = [x_cols, x_cols + R, x_cols + R + channel_params.shape[1]]
    routing = jnp.concatenate([router_matrix, norm_gains.T], 1)
    joined = narrow.shape[0] == routing.shape[0]
    if joined:
        narrow = jnp.concatenate([narrow, routing], 1)
    narrow_cols = narrow.shape[1]
    pad = -narrow_cols % LANES
    first = jnp.concatenate([input_projection[0], jnp.pad(narrow, ((0, 0), (0, pad)))], 1)
    later = jnp.concatenate([input_projection[1], output_projection], 1)
    full = lax.all_gather(first, OWNERS, axis=0, tiled=True)
    later_full = lax.all_gather(later, OWNERS, axis=0, tiled=True)

    position = lax.axis_index("ctx") * length + jnp.arange(length)
    valid = (position[:, None] < lengths.reshape(1, seqs)).astype(F32).reshape(tokens, 1)
    route = by_token(routes)
    slot = by_token(slots)
    kept = slot >= 0
    kept_f = kept.astype(F32)
    micro_of = (jnp.arange(tokens) // group) % micros
    place = jnp.where(kept, route * slots_each + micro_of * capacity + slot, -1)
    pick = (
        jnp.arange(rows).reshape(experts, slots_each, 1) == place[None, None, :]
    ).astype(BF16)
    grad_tok = by_token(out_grad)
    grad_act = grad_tok.astype(F32) * valid

    def packed(value):
        return jnp.einsum("est,td->esd", pick, value, preferred_element_type=F32).astype(BF16)

    def unpacked(value):
        flat = value.reshape(rows, value.shape[-1])
        return lax.optimization_barrier(dot(pick.reshape(rows, tokens), flat, TN))

    def swap_owners(value):
        return lax.all_to_all(value, OWNERS, split_axis=0, concat_axis=0, tiled=True)

    full, grad_packed = lax.optimization_barrier((full, packed(grad_tok)))
    grad_rows_raw = swap_owners(grad_packed)

    w_in = full[:, :width]
    tail = full[:, width:]
    w_gate, w_out = later_full[:, :width], later_full[:, width:]
    w_x = tail[:, : cuts[0]]
    w_step = tail[:, cuts[0] : cuts[1]]
    channel_f = tail[:, cuts[1] : cuts[2]].astype(F32)
    bias_f = tail[:, cuts[2]].astype(F32)
    if joined:
        full_routing = tail[:, cuts[2] + 1 : cuts[2] + 1 + routing.shape[1]]
    else:
        full_routing = lax.all_gather(routing, OWNERS, axis=0, tiled=True)
    w_router = full_routing[:, :experts]
    gains = full_routing[:, experts:].T.astype(F32)
    chans = channel_f.shape[0]
    taps = channel_f[:, :CONV_TAPS].T
    conv_bias = channel_f[:, CONV_TAPS]
    skip = channel_f[:, CONV_TAPS + 1]
    rates = -jnp.exp(channel_f[:, CONV_TAPS + 2 :]).T

    x_tok = lax.optimization_barrier(by_token(inputs))
    x = x_tok.astype(F32)
    normed1 = (normalized(x) * gains[0]).astype(BF16)
    inner = dot(normed1, w_in, NT).astype(BF16)
    rim = (CONV_TAPS - 1) * seqs
    before = moved(inner[tokens - rim :], 1)
    gate_z = dot(normed1, w_gate, NT)
    extended = jnp.concatenate([before, inner], 0).astype(F32)
    conv = conv_bias
    for tap in range(CONV_TAPS):
        conv = conv + taps[tap] * extended[tap * seqs : tap * seqs + tokens]
    u = jax.nn.silu(conv).astype(BF16)
    u_wide = u.astype(F32)
    proj = tensor_total(dot(u, w_x), BF16)
    rank = proj[:, :R].astype(BF16)
    b_vals = proj[:, R : R + N]
    c_vals = proj[:, R + N :]
    step_pre = dot(rank, w_step, NT) + bias_f
    delta = jax.nn.softplus(step_pre)
    lane_width = 2 * LANES if chans % (2 * LANES) == 0 else LANES
    wide_rates = (N, seqs, lane_width)
    state_block = (N, seqs, lane_width)
    call = functools.partial(scan_call, width=lane_width, chans=chans)

    def both_in(value, steps=length):
        return (value, (steps * seqs, lane_width), "tc")

    def by_chan(value):
        return (value, (*value.shape[:-1], lane_width), "c")

    def by_rows(value, steps=length):
        return (value, (steps * seqs, value.shape[1]), "t")

    def cost(steps, ops):
        elements = steps * seqs * chans * N
        return pl.CostEstimate(flops=300 * ops * elements, bytes_accessed=elements, transcendentals=0)

    def out(shape, dtype=F32):
        return jax.ShapeDtypeStruct(shape, dtype)

    [end] = call(
        end_state_kernel,
        [both_in(delta), both_in(u_wide), by_rows(b_vals), by_chan(rates)],
        [by_chan(out((N + 1, seqs, chans)))],
        [wide_rates, (tokens, N * LANES)],
        cost=cost(length, 6),
    )
    end, grad_rows_raw = lax.optimization_barrier((end, grad_rows_raw))
    log_decay = end[N]
    state = carried(end, log_decay, rates, 1, 0)
    pieces = 4 if length % (4 * BLK) == 0 else 1
    steps = length // pieces
    y_parts, gated_parts, mixed_parts, start_parts = [], [], [], []
    for piece in range(pieces):
        if piece > 1:
            state, mixed_parts[piece - 2] = lax.optimization_barrier(
                (state, mixed_parts[piece - 2])
            )
        y_part, gated_part, mixed_part, start_part, state = call(
            forward_kernel,
            [
                both_in(delta, steps),
                both_in(u_wide, steps),
                (gate_z, (steps * seqs, lane_width), "tc"),
                by_rows(b_vals, steps),
                by_rows(c_vals, steps),
                by_chan(rates),
                by_chan(skip[None]),
                (w_out, (lane_width, width), "r"),
                by_chan(state),
            ],
            [
                by_chan(out((steps * seqs, chans))),
                by_chan(out((steps * seqs, chans), BF16)),
                (out((steps * seqs, width), BF16), (steps * seqs, width), ""),
                by_chan(out((steps // BLK, N, seqs, chans))),
                by_chan(out((N, seqs, chans))),
            ],
            [wide_rates, (steps * seqs, N * LANES), (steps * seqs, N * LANES), (steps * seqs, width)],
            chunk=piece,
            cost=cost(steps, 10),
        )
        y_parts.append(y_part)
        gated_parts.append(gated_part)
        mixed_parts.append(tensor_total(mixed_part, BF16))
        start_parts.append(start_part)
    y_vals = jnp.concatenate(y_parts, 0)
    gated = jnp.concatenate(gated_parts, 0)
    starts = jnp.concatenate(start_parts, 0)
    silu_z, gate_slope = silu_parts(gate_z)
    resid = x + jnp.concatenate(mixed_parts, 0)

    scale2 = lax.rsqrt(jnp.mean(resid * resid, -1, keepdims=True) + EPS)
    xhat2 = resid * scale2
    normed2 = (xhat2 * gains[1]).astype(BF16)
    probs = jax.nn.softmax(dot(normed2, w_router), -1)
    onehot = (route[:, None] == jnp.arange(experts)).astype(F32)
    gate = jnp.sum(probs * onehot, -1, keepdims=True) * kept_f[:, None]
    peers, here = lax.axis_size("tensor"), lax.axis_index("tensor")
    share = width // peers

    def half(value):
        cut = value[..., :share]
        for peer in range(1, peers):
            cut = jnp.where(here == peer, value[..., peer * share : (peer + 1) * share], cut)
        return cut

    x_rows = tensor_columns(swap_owners(packed(half(normed2))))
    gate_rows = swap_owners(
        jnp.sum(jnp.where(pick > 0, gate[:, 0], 0.0), -1)[:, None, :]
    )
    grad_rows = (jnp.swapaxes(gate_rows, 1, 2) * grad_rows_raw.astype(F32)).astype(BF16)
    up, down = expert_up[0], expert_down[0]

    def product(a, b, terms):
        return jnp.einsum(terms, a, b, preferred_element_type=F32)

    def shared(value, matrix, terms, axis):
        if peers > 2:
            total = product(value, matrix, terms)
            share = lax.psum_scatter(total, "tensor", scatter_dimension=2, tiled=True)
            return share.astype(BF16), value
        low, high = jnp.split(matrix, 2, axis)
        sent = product(value, jnp.where(here == 0, high, low), terms).astype(BF16)
        value, sent = lax.optimization_barrier((value, sent))
        own = product(value, jnp.where(here == 0, low, high), terms)
        return (own + swapped(sent).astype(F32)).astype(BF16), sent

    hidden = product(x_rows, up, "srd,df->srf")
    act_float, gelu_pull = jax.vjp(lambda v: jax.nn.gelu(v, approximate=True), hidden)
    act = act_float.astype(BF16)
    share_y, sent_y = shared(act, down, "srf,fd->srd", 1)
    grad_rows, _ = lax.optimization_barrier((grad_rows, sent_y))
    d_hidden = gelu_pull(product(grad_rows, down, "srd,fd->srf"))[0].astype(BF16)
    back_y = swap_owners(share_y)
    share_x, _ = shared(d_hidden, up, "srf,df->srd", 0)
    back_x = swap_owners(share_x)
    grad_up = product(x_rows, d_hidden, "srd,srf->df")
    grad_down = product(act, grad_rows, "srf,srd->fd")
    back_x, grad_up, grad_down = lax.optimization_barrier((back_x, grad_up, grad_down))
    expert_y = unpacked(back_y)
    expert_dx = unpacked(back_x)
    x_half = half(xhat2)
    gain_half = half(gains[1])
    grad_half = half(grad_act)
    router_half = half(w_router.T)
    sums = jnp.stack(
        [jnp.sum(grad_half * expert_y, -1), jnp.sum(gain_half * expert_dx * x_half, -1)]
    )
    sums = tensor_total(sums, F32)
    gate_grad = sums[0][:, None]
    d_logits = (gate_grad * gate * (onehot - probs)).astype(BF16)
    grad_router = dot(normed2, d_logits, TN)
    by_router = dot((xhat2 * gains[1]).astype(BF16), w_router)
    mean_term = (
        sums[1][:, None] + jnp.sum(d_logits.astype(F32) * by_router, -1, keepdims=True)
    ) / width
    d_normed2 = expert_dx + dot(d_logits, router_half)
    gain_grad2 = tensor_columns(jnp.sum(d_normed2 * x_half, 0, keepdims=True))[0]
    d_resid_half = grad_half + scale2 * (gain_half * d_normed2 - x_half * mean_term)
    act_half = (valid * (half(resid) + gate * expert_y)).astype(BF16)

    d_mixed = tensor_columns(d_resid_half.astype(BF16))
    d_gated = dot(d_mixed, w_out, NT)
    d_y = d_gated * silu_z
    [start_grad] = call(
        start_grad_kernel,
        [both_in(delta), both_in(d_y), by_rows(c_vals), by_chan(rates)],
        [by_chan(out((N, seqs, chans)))],
        [wide_rates, (tokens, N * LANES)],
        cost=cost(length, 6),
    )
    d_gate_z = (d_gated * y_vals * gate_slope).astype(BF16)

    def owned(value):
        return lax.psum_scatter(
            value.astype(BF16), OWNERS, scatter_dimension=0, tiled=True
        ).astype(F32)

    mine_early = owned(
        jnp.concatenate([dot(d_gate_z, normed1, TN), dot(gated, d_mixed, TN)], 1)
    )
    grad_end, act_others = carried(start_grad, log_decay, rates, -1, 1, act_half)
    w_step_wide = jnp.pad(w_step, ((0, 0), (0, LANES - R)))
    d_step, du_part, d_proj_part, rate_grad, bias_sums, skip_sums = call(
        backward_kernel,
        [
            both_in(delta),
            both_in(u_wide),
            both_in(d_y),
            (jax.nn.sigmoid(step_pre), (tokens, lane_width), "tc"),
            by_rows(b_vals),
            by_rows(c_vals),
            by_chan(rates),
            by_chan(skip[None]),
            (w_step_wide, (lane_width, LANES), "r"),
            by_chan(starts),
            by_chan(grad_end),
        ],
        [
            by_chan(out((tokens, chans), BF16)),
            by_chan(out((tokens, chans))),
            (out((tokens, LANES), BF16), (tokens, LANES), ""),
            by_chan(out((N, seqs, chans))),
            by_chan(out((seqs, chans))),
            by_chan(out((seqs, chans))),
        ],
        [
            wide_rates,
            (tokens, N * LANES),
            (tokens, N * LANES),
            (BLK + 1, N, seqs, lane_width),
            (BLK, N, seqs, lane_width),
            (BLK * seqs, N * LANES),
            (BLK * seqs, N * LANES),
            (BLK * seqs, lane_width),
            (tokens, LANES),
            pltpu.VMEM((2 * N * LANES, LANES), BF16),
        ],
        cost=cost(length, 24),
    )
    d_step, mine_early = lax.optimization_barrier((d_step, mine_early))
    d_proj = tensor_total(d_proj_part, BF16).astype(BF16)
    step_bias_grad = jnp.sum(bias_sums, 0)
    skip_grad = jnp.sum(skip_sums, 0)
    w_x_wide = jnp.pad(w_x, ((0, 0), (0, LANES - x_cols)))
    rim_u = du_part[:rim] + dot(d_proj[:rim], w_x_wide, NT)
    after = moved(rim_u * silu_parts(conv[:rim])[1], -1)
    steps = length // 4
    block = steps * seqs
    turns = length // steps

    def from_end(value):
        return value, pl.BlockSpec((block, value.shape[1]), lambda i: (turns - 1 - i, 0))

    def whole(value):
        return value, pl.BlockSpec(value.shape, lambda i: (0, 0))

    arrays = [
        from_end(du_part),
        from_end(d_proj),
        from_end(conv),
        whole(extended),
        from_end(normed1),
        from_end(x_tok),
        from_end(u),
        from_end(rank),
        from_end(d_step),
        from_end(d_gate_z),
        whole(w_in),
        whole(w_gate),
        whole(w_x_wide),
        whole(taps),
        whole(after),
    ]
    results = [
        (
            out((tokens // 2, width), BF16),
            pl.BlockSpec((block, width), lambda i: (jnp.maximum(turns // 2 - 1 - i, 0), 0)),
        ),
        (
            out((tokens // 2, width), BF16),
            pl.BlockSpec(
                (block, width), lambda i: (jnp.minimum(turns - 1 - i, turns // 2 - 1), 0)
            ),
        ),
        whole(out((chans, width))),
        whole(out((chans, LANES))),
        whole(out((chans, R))),
        whole(out(((CONV_TAPS + 1) * seqs, chans))),
        whole(out((seqs, width))),
    ]
    late_part, early_part, grad_in, grad_xproj, grad_dt, conv_sums, gain_sums = pl.pallas_call(
        functools.partial(inner_grad_kernel, seqs),
        grid=(turns,),
        in_specs=[spec for _, spec in arrays],
        out_specs=[spec for _, spec in results],
        out_shape=[value for value, _ in results],
        scratch_shapes=[pltpu.VMEM((block + rim, chans), F32)],
        compiler_params=pltpu.CompilerParams(vmem_limit_bytes=62 << 20),
    )(*[value for value, _ in arrays])
    grad_xproj = grad_xproj[:, :x_cols]
    conv_sums = jnp.sum(conv_sums.reshape(CONV_TAPS + 1, seqs, chans), 1)
    gain_grad1 = jnp.sum(gain_sums, 0)

    narrow_grads = jnp.concatenate(
        [
            grad_xproj,
            grad_dt,
            conv_sums.T,
            skip_grad[:, None],
            (jnp.sum(rate_grad, 1) * rates).T,
            step_bias_grad[:, None],
        ],
        1,
    )
    routing_grads = jnp.concatenate([grad_router, gain_grad1[:, None], gain_grad2[:, None]], 1)
    if joined:
        narrow_grads = jnp.concatenate([narrow_grads, routing_grads], 1)
    wide_grads = jnp.concatenate(
        [grad_in, jnp.pad(narrow_grads, ((0, 0), (0, pad)))], 1
    )

    halves = [late_part, early_part]
    if peers == 2:
        exchanged = [swapped(part) for part in halves]
    else:
        exchanged = [lax.all_gather(part, "tensor") for part in halves]
    mine, exchanged = halved(wide_grads, exchanged)
    normed_parts = []
    for own, others in zip(halves, exchanged):
        if peers == 2:
            normed_parts.append([own, others])
        else:
            normed_parts.append([others[k] for k in range(peers)])
    late_parts, early_parts = normed_parts

    def rows_of(value):
        return value, pl.BlockSpec((block, value.shape[1]), lambda i: (i, 0))

    def early_rows(value):
        return value, pl.BlockSpec((block, width), lambda i: (jnp.minimum(i, turns // 2 - 1), 0))

    def late_rows(value):
        return value, pl.BlockSpec((block, width), lambda i: (jnp.maximum(i - turns // 2, 0), 0))

    arrays = (
        [early_rows(part) for part in early_parts]
        + [late_rows(part) for part in late_parts]
        + [
            rows_of(x_tok),
            rows_of(d_mixed),
            rows_of(act_half),
            (act_others, pl.BlockSpec((peers - 1, block, share), lambda i: (0, i, 0))),
            whole(gains[:1]),
        ]
    )
    out_spec = pl.BlockSpec((micros, group, steps, width), lambda i: (0, 0, i, 0))
    input_grad, activations = pl.pallas_call(
        functools.partial(output_kernel, (micros, group), peers),
        grid=(turns,),
        in_specs=[spec for _, spec in arrays],
        out_specs=[out_spec, out_spec],
        out_shape=[out(inputs.shape), out(inputs.shape, BF16)],
        scratch_shapes=[pltpu.VMEM((width // LANES, block, LANES), F32)] * 2,
        compiler_params=pltpu.CompilerParams(vmem_limit_bytes=62 << 20),
    )(*[value for value, _ in arrays])
    mine_tail = mine[:, width:]
    if joined:
        mine_routing = mine_tail[:, cuts[2] + 1 : cuts[2] + 1 + routing.shape[1]]
    else:
        mine_routing, _ = halved(routing_grads)
    gains_out = jnp.stack(
        [tensor_total(mine_routing[None, :, experts], F32)[0], mine_routing[:, experts + 1]]
    )
    return (
        activations,
        input_grad,
        gains_out,
        mine_routing[:, :experts],
        jnp.stack([mine[:, :width], mine_early[:, :width]]),
        mine_tail[:, : cuts[0]],
        mine_tail[:, cuts[0] : cuts[1]],
        mine_tail[:, cuts[2]],
        mine_tail[:, cuts[1] : cuts[2]],
        mine_early[:, width:],
        grad_up[None],
        grad_down[None],
    )


def solution(mesh):
    return jax.shard_map(
        per_device,
        mesh=mesh,
        in_specs=(
            P(None, "fsdp", "ctx", None),
            P(None, "fsdp", "ctx", None),
            P(None, "fsdp"),
            P(None, "fsdp", "ctx"),
            P(None, "fsdp", "ctx"),
            P(None, ("fsdp", "ctx")),
            P(("fsdp", "ctx"), None),
            P(None, ("fsdp", "ctx", "tensor"), None),
            P(("fsdp", "ctx", "tensor"), None),
            P(("fsdp", "ctx", "tensor"), None),
            P(("fsdp", "ctx", "tensor")),
            P(("fsdp", "ctx", "tensor"), None),
            P(("fsdp", "ctx", "tensor"), None),
            P(("fsdp", "ctx"), None, "tensor"),
            P(("fsdp", "ctx"), "tensor", None),
        ),
        out_specs=(
            P(None, "fsdp", "ctx", None),
            P(None, "fsdp", "ctx", None),
            P(None, ("fsdp", "ctx")),
            P(("fsdp", "ctx"), None),
            P(None, ("fsdp", "ctx", "tensor"), None),
            P(("fsdp", "ctx", "tensor"), None),
            P(("fsdp", "ctx", "tensor"), None),
            P(("fsdp", "ctx", "tensor")),
            P(("fsdp", "ctx", "tensor"), None),
            P(("fsdp", "ctx", "tensor"), None),
            P(("fsdp", "ctx"), None, "tensor"),
            P(("fsdp", "ctx"), "tensor", None),
        ),
        check_vma=False,
    )
```

```python
import functools

import jax
import jax.numpy as jnp
from jax import lax
from jax.experimental import pallas as pl
from jax.experimental.pallas import tpu as pltpu
from jax.sharding import PartitionSpec as P

N = 16
CONV_TAPS = 4
R = 48
EPS = 1e-05
BLK = 8
LANES = 128
F32 = jnp.float32
BF16 = jnp.bfloat16
OWNERS = ("fsdp", "ctx")


def silu_parts(value):
    sig = jax.nn.sigmoid(value)
    return value * sig, sig * (1.0 + value * (1.0 - sig))


def swapped(value):
    return lax.ppermute(value, "tensor", [(0, 1), (1, 0)])


def tensor_total(value, dtype):
    sent = value.astype(dtype)
    if lax.axis_size("tensor") == 2:
        return sent.astype(F32) + swapped(sent).astype(F32)
    return jnp.sum(lax.all_gather(sent, "tensor").astype(F32), axis=0)


def tensor_columns(value):
    if lax.axis_size("tensor") == 2:
        other = swapped(value)
        first = lax.axis_index("tensor") == 0
        return jnp.concatenate(
            [jnp.where(first, value, other), jnp.where(first, other, value)], -1
        )
    return lax.all_gather(value, "tensor", axis=value.ndim - 1, tiled=True)


def halved(value, beside=()):
    beside = list(beside)
    sizes = [lax.axis_size(axis) for axis in OWNERS]
    bits = [(axis, 1 << k) for axis, size in zip(OWNERS, sizes) for k in reversed(range(size.bit_length() - 1))]
    rows = value.shape[0] >> len(bits)
    for place in reversed(range(len(bits))):
        axis, bit = bits[place]
        view = value.reshape(1 << place, 2, rows, value.shape[-1])
        high = (lax.axis_index(axis) & bit) != 0
        own = jnp.where(high, view[:, 1], view[:, 0])
        other = jnp.where(high, view[:, 0], view[:, 1]).astype(BF16)
        got = lax.ppermute(other, axis, [(i, i ^ bit) for i in range(lax.axis_size(axis))])
        value = own.astype(F32) + got.astype(F32)
        turn = len(bits) - 1 - place
        if 0 < turn <= len(beside):
            turn -= 1
            value, beside[turn] = lax.optimization_barrier((value, beside[turn]))
    return value.reshape(rows, value.shape[-1]), beside


def moved(value, by):
    peers = lax.axis_size("ctx")
    pairs = [(i, i + by) for i in range(peers) if 0 <= i + by < peers]
    return lax.ppermute(value, "ctx", pairs)


TN = (((0,), (0,)), ((), ()))
NT = (((1,), (1,)), ((), ()))
NN = (((1,), (0,)), ((), ()))


def dot(a, b, dims=NN):
    return lax.dot_general(a, b, dims, preferred_element_type=F32)


MESH = pl.DeviceIdType.MESH


def greet(peers):
    barrier = pltpu.get_barrier_semaphore()
    for peer in peers:
        pl.semaphore_signal(barrier, inc=1, device_id=peer, device_id_type=MESH)
    pl.semaphore_wait(barrier, len(peers))


def carry_kernel(sign, ranges, peers, end_ref, log_ref, r_ref, *refs):
    if peers:
        own_ref, left_refs, right_refs = refs[0], refs[1:5:2], refs[2:5:2]
        out_ref, others_ref, products_ref = refs[5:8]
        sent, got, log_out, send_sem, recv_sem, own_sem, others_sem = refs[8:]
    else:
        out_ref, sent, got, log_out, send_sem, recv_sem = refs
    turns, groups, _, width = sent.shape
    seqs = log_ref.shape[0]
    fsdp, me, tensor = lax.axis_index("fsdp"), lax.axis_index("ctx"), lax.axis_index("tensor")

    def peer(by):
        return (fsdp, lax.rem(me + by + ranges, ranges), tensor)

    shifts = [sign * (1 << turn) for turn in range(turns)]
    partners = [(fsdp, me, lax.rem(tensor + by, peers)) for by in range(1, peers)]
    near = sorted({s % ranges for s in shifts} | {-s % ranges for s in shifts})
    greet([peer(by) for by in near] + partners)
    beside = [
        pltpu.make_async_remote_copy(
            src_ref=own_ref,
            dst_ref=others_ref.at[k],
            send_sem=own_sem.at[k],
            recv_sem=others_sem.at[k],
            device_id=partner,
            device_id_type=MESH,
        )
        for k, partner in enumerate(partners)
    ]
    for extra in beside:
        extra.start()

    def copy(turn, group):
        return pltpu.make_async_remote_copy(
            src_ref=sent.at[turn, group],
            dst_ref=got.at[turn, group],
            send_sem=send_sem.at[turn, group],
            recv_sem=recv_sem.at[turn, group],
            device_id=peer(shifts[turn]),
            device_id_type=MESH,
        )

    def decayed(log, cols, n):
        return jnp.exp(log * r_ref[n : n + 1, cols])

    def receive(turn, group):
        copy(turn, group).wait_recv()
        cols = slice(group * width, (group + 1) * width)
        reach = 1 << turn
        real = (me >= reach) if sign > 0 else (me < ranges - reach)

        def part(k):
            rows = got[turn, group, k * seqs : (k + 1) * seqs, :].astype(F32)
            return jnp.where(real, rows, 0.0)

        log = part(N) + part(N + 1)
        if turn == 0:
            for n in range(N):
                out_ref[n, :, cols] = part(n)
            log_out[:, cols] = log
        else:
            late = log_out[:, cols]
            for n in range(N):
                out_ref[n, :, cols] = out_ref[n, :, cols] + decayed(late, cols, n) * part(n)
            log_out[:, cols] = late + log

    for turn in range(turns):
        if turn == 1 and peers:
            for k, (left, right) in enumerate(zip(left_refs, right_refs)):
                count = right.shape[1]

                def product(i, _, k=k, left=left, right=right, count=count):
                    at = pl.ds(pl.multiple_of(i * LANES, LANES), LANES)
                    value = dot(left[:, at], right[...], TN)
                    products_ref[at, k * count : (k + 1) * count] = value.astype(BF16)
                    return 0

                lax.fori_loop(0, left.shape[1] // LANES, product, 0)
        for group in range(groups):
            cols = slice(group * width, (group + 1) * width)
            own_log = log_ref[:, cols]
            if turn > 0:
                receive(turn - 1, group)
            for n in range(0, N, 2):
                pair = []
                for k in (n, n + 1):
                    value = end_ref[k, :, cols]
                    if turn > 0:
                        value = value + decayed(own_log, cols, k) * out_ref[k, :, cols]
                    pair.append(value)
                sent[turn, group, n * seqs : (n + 2) * seqs, :] = jnp.concatenate(pair, 0).astype(
                    BF16
                )
            log = own_log if turn == 0 else own_log + log_out[:, cols]
            high = log.astype(BF16).astype(F32)
            sent[turn, group, N * seqs :, :] = jnp.concatenate([high, log - high], 0).astype(BF16)
            copy(turn, group).start()
    for group in range(groups):
        receive(turns - 1, group)
    for turn in range(turns):
        for group in range(groups):
            copy(turn, group).wait_send()
    for extra in beside:
        extra.wait()


def carried(end, log_decay, rates, sign, ident, shared=None, factors=()):
    _, seqs, chans = end.shape
    ranges = lax.axis_size("ctx")
    turns = (ranges - 1).bit_length()
    groups = 3 if chans % (3 * LANES) == 0 else 1
    block = (turns, groups, (N + 2) * seqs, chans // groups)
    vmem = pl.BlockSpec(memory_space=pltpu.VMEM)
    anywhere = pl.BlockSpec(memory_space=pl.ANY)
    peers = 0 if shared is None else lax.axis_size("tensor")
    state = jax.ShapeDtypeStruct((N, seqs, chans), F32)
    scratch = [
        pltpu.VMEM(block, BF16),
        pltpu.VMEM(block, BF16),
        pltpu.VMEM((seqs, chans), F32),
        pltpu.SemaphoreType.DMA((turns, groups)),
        pltpu.SemaphoreType.DMA((turns, groups)),
    ]
    if peers:
        others = jax.ShapeDtypeStruct((peers - 1, *shared.shape), shared.dtype)
        scratch += [pltpu.SemaphoreType.DMA((peers - 1,)), pltpu.SemaphoreType.DMA((peers - 1,))]
        products = jax.ShapeDtypeStruct(
            (factors[0].shape[1], factors[1].shape[1] + factors[3].shape[1]), BF16
        )
    return pl.pallas_call(
        functools.partial(carry_kernel, sign, ranges, peers),
        in_specs=[vmem] * 3 + ([anywhere] + [vmem] * len(factors) if peers else []),
        out_specs=[vmem, anywhere, vmem] if peers else vmem,
        out_shape=[state, others, products] if peers else state,
        scratch_shapes=scratch,
        compiler_params=pltpu.CompilerParams(
            collective_id=ident, has_side_effects=True, vmem_limit_bytes=48 << 20
        ),
        cost_estimate=pl.CostEstimate(flops=20 << 30, bytes_accessed=1 << 20, transcendentals=0),
    )(end[:N], log_decay, rates, *([shared, *factors] if peers else []))


def spread_matrix():
    rows = lax.broadcasted_iota(jnp.int32, (2 * N, N * LANES), 0) % N
    cols = lax.broadcasted_iota(jnp.int32, (2 * N, N * LANES), 1) // LANES
    return (rows == cols).astype(F32).astype(BF16)


def spread_into(pairs, rows):
    def turn(i, _):
        matrix = spread_matrix()
        at = pl.ds(pl.multiple_of(i * LANES, LANES), LANES)
        for source, target in pairs:
            value = source[at, :]
            high = value.astype(BF16)
            low = (value - high.astype(F32)).astype(BF16)
            target[at, :] = jnp.dot(
                jnp.concatenate([high, low], 1), matrix, preferred_element_type=F32
            )
        return 0

    lax.fori_loop(0, rows // LANES, turn, 0)


def lanes(k):
    return slice(k * LANES, (k + 1) * LANES)


def end_state_kernel(d_ref, u_ref, b_ref, r_ref, end_ref, rb, bb):
    rows, width = d_ref.shape
    seqs = rb.shape[1]
    length = rows // seqs
    parts = width // LANES
    for n in range(N):
        rb[n] = jnp.broadcast_to(r_ref[n : n + 1, :], (seqs, width))

    @pl.when(pl.program_id(0) == 0)
    def _():
        spread_into([(b_ref, bb)], rows)

    def body(t, carry):
        hs, total = carry
        row = pl.ds(pl.multiple_of(t * seqs, seqs), seqs)
        d = d_ref[row, :]
        du = d * u_ref[row, :]
        new = []
        for n in range(N):
            bn = bb[row, lanes(n)]
            for k in range(parts):
                a = jnp.exp(d[:, lanes(k)] * rb[n, :, lanes(k)])
                new.append(a * hs[n * parts + k] + du[:, lanes(k)] * bn)
        return tuple(new), total + d

    zero = jnp.zeros((seqs, LANES), F32)
    hs, total = lax.fori_loop(
        0, length, body, ((zero,) * (N * parts), jnp.zeros((seqs, width), F32)), unroll=4
    )
    for n in range(N):
        for k in range(parts):
            end_ref[n, :, lanes(k)] = hs[n * parts + k]
    end_ref[N] = total


def forward_kernel(
    peers,
    d_ref,
    u_ref,
    z_ref,
    b_ref,
    c_ref,
    r_ref,
    skip_ref,
    w_ref,
    h0_ref,
    x_ref,
    y_ref,
    gated_ref,
    st_ref,
    resid_ref,
    rb,
    bb,
    cb,
    state,
    total,
    sent,
    got,
    send_sem,
    recv_sem,
):
    rows, width = d_ref.shape
    seqs = rb.shape[1]
    length = rows // seqs
    parts = width // LANES
    piece, group = pl.program_id(0), pl.program_id(1)
    pieces, last = pl.num_programs(0), pl.num_programs(1) - 1
    fsdp, ctx, tensor = lax.axis_index("fsdp"), lax.axis_index("ctx"), lax.axis_index("tensor")
    partners = [(fsdp, ctx, lax.rem(tensor + by, peers)) for by in range(1, peers)]

    def copy(k, which):
        return pltpu.make_async_remote_copy(
            src_ref=sent.at[which],
            dst_ref=got.at[k, which],
            send_sem=send_sem.at[k, which],
            recv_sem=recv_sem.at[k, which],
            device_id=partners[k],
            device_id_type=MESH,
        )

    @pl.when((piece == 0) & (group == 0))
    def _():
        greet(partners)

    for n in range(N):
        rb[n] = jnp.broadcast_to(r_ref[n : n + 1, :], (seqs, width))

    @pl.when(group == 0)
    def _():
        spread_into([(b_ref, bb), (c_ref, cb)], rows)
        total[...] = jnp.zeros_like(total)

    @pl.when(piece == 0)
    def _():
        state[group] = h0_ref[...]

    def block(i, hs):
        for n in range(N):
            for k in range(parts):
                st_ref[i, n, :, lanes(k)] = hs[n * parts + k]

        def body(step, hs):
            t = i * BLK + step
            row = pl.ds(pl.multiple_of(t * seqs, seqs), seqs)
            d = d_ref[row, :]
            u = u_ref[row, :]
            du = d * u
            ys = [u[:, lanes(k)] * skip_ref[:, lanes(k)] for k in range(parts)]
            new = []
            for n in range(N):
                bn = bb[row, lanes(n)]
                cn = cb[row, lanes(n)]
                for k in range(parts):
                    a = jnp.exp(d[:, lanes(k)] * rb[n, :, lanes(k)])
                    h = a * hs[n * parts + k] + du[:, lanes(k)] * bn
                    ys[k] = ys[k] + h * cn
                    new.append(h)
            for k in range(parts):
                y_ref[row, lanes(k)] = ys[k]
            return tuple(new)

        return lax.fori_loop(0, BLK, body, hs, unroll=4)

    hs = lax.fori_loop(
        0,
        length // BLK,
        block,
        tuple(state[group, n, :, lanes(k)] for n in range(N) for k in range(parts)),
    )
    for n in range(N):
        for k in range(parts):
            state[group, n, :, lanes(k)] = hs[n * parts + k]
    z = z_ref[...]
    gated = (y_ref[...] * (z * jax.nn.sigmoid(z))).astype(BF16)
    gated_ref[...] = gated
    total[...] += jnp.dot(gated, w_ref[...], preferred_element_type=F32)

    def add(which):
        for k in range(peers - 1):
            copy(k, which).wait_recv()
        at = pl.ds(pl.multiple_of(which * rows, rows), rows)
        value = x_ref[at, :].astype(F32)
        own = sent[which].astype(F32)
        if peers == 2:
            value = value + (own + got[0, which].astype(F32))
        else:
            for owner in range(peers):
                term = own
                for k in range(peers - 1):
                    here = lax.rem(tensor + peers - k - 1, peers) == owner
                    term = jnp.where(here, got[k, which].astype(F32), term)
                value = value + term
        resid_ref[at, :] = value

    @pl.when(group == last)
    def _():
        sent[piece] = total[...].astype(BF16)
        for k in range(peers - 1):
            copy(k, piece).start()

        @pl.when(piece > 1)
        def _():
            add(piece - 2)

    @pl.when((group == last) & (piece == pieces - 1))
    def _():
        count = sent.shape[0]
        for which in range(max(count - 2, 0), count):
            add(which)
        for which in range(count):
            for k in range(peers - 1):
                copy(k, which).wait_send()


def start_grad_kernel(d_ref, dy_ref, c_ref, r_ref, g_ref, rb, cb):
    rows, width = d_ref.shape
    seqs = rb.shape[1]
    length = rows // seqs
    parts = width // LANES
    for n in range(N):
        rb[n] = jnp.broadcast_to(r_ref[n : n + 1, :], (seqs, width))

    @pl.when(pl.program_id(0) == 0)
    def _():
        spread_into([(c_ref, cb)], rows)

    def body(i, gs):
        t = length - 1 - i
        row = pl.ds(pl.multiple_of(t * seqs, seqs), seqs)
        d = d_ref[row, :]
        dy = dy_ref[row, :]
        new = []
        for n in range(N):
            cn = cb[row, lanes(n)]
            for k in range(parts):
                a = jnp.exp(d[:, lanes(k)] * rb[n, :, lanes(k)])
                new.append(a * (gs[n * parts + k] + dy[:, lanes(k)] * cn))
        return tuple(new)

    zero = jnp.zeros((seqs, LANES), F32)
    gs = lax.fori_loop(0, length, body, (zero,) * (N * parts), unroll=4)
    for n in range(N):
        for k in range(parts):
            g_ref[n, :, lanes(k)] = gs[n * parts + k]


def backward_kernel(
    d_ref,
    u_ref,
    dy_ref,
    sig_ref,
    b_ref,
    c_ref,
    r_ref,
    skip_ref,
    w_ref,
    st_ref,
    g0_ref,
    dstep_ref,
    du_ref,
    dproj_ref,
    rg_ref,
    bias_ref,
    skipg_ref,
    rb,
    bb,
    cb,
    hb,
    ab,
    pb,
    pc,
    dsb,
    total,
    columns,
):
    rows, width = d_ref.shape
    seqs = rb.shape[1]
    length = rows // seqs
    parts = width // LANES
    group = pl.program_id(0)
    for n in range(N):
        rb[n] = jnp.broadcast_to(r_ref[n : n + 1, :], (seqs, width))

    @pl.when(group == 0)
    def _():
        spread_into([(b_ref, bb), (c_ref, cb)], rows)
        total[...] = jnp.zeros_like(total)
        source = lax.broadcasted_iota(jnp.int32, columns.shape, 0) // LANES
        target = lax.broadcasted_iota(jnp.int32, columns.shape, 1)
        columns[...] = (source + R == target).astype(F32).astype(BF16)

    rg_ref[...] = jnp.zeros_like(rg_ref)
    bias_ref[...] = jnp.zeros_like(bias_ref)
    skipg_ref[...] = jnp.zeros_like(skipg_ref)

    def block(turn, gs):
        i = length // BLK - 1 - turn

        def again(step, hs):
            t = i * BLK + step
            row = pl.ds(pl.multiple_of(t * seqs, seqs), seqs)
            d = d_ref[row, :]
            du = d * u_ref[row, :]
            new = []
            for n in range(N):
                bn = bb[row, lanes(n)]
                for k in range(parts):
                    a = jnp.exp(d[:, lanes(k)] * rb[n, :, lanes(k)])
                    h = a * hs[n * parts + k] + du[:, lanes(k)] * bn
                    ab[step, n, :, lanes(k)] = a
                    hb[step + 1, n, :, lanes(k)] = h
                    new.append(h)
            return tuple(new)

        hs = tuple(st_ref[i, n, :, lanes(k)] for n in range(N) for k in range(parts))
        for n in range(N):
            for k in range(parts):
                hb[0, n, :, lanes(k)] = hs[n * parts + k]
        lax.fori_loop(0, BLK, again, hs, unroll=4)

        def back(turn, gs):
            step = BLK - 1 - turn
            t = i * BLK + step
            row = pl.ds(pl.multiple_of(t * seqs, seqs), seqs)
            here = pl.ds(pl.multiple_of(step * seqs, seqs), seqs)
            d = d_ref[row, :]
            u = u_ref[row, :]
            dy = dy_ref[row, :]
            du = d * u
            prods = [jnp.zeros((seqs, LANES), F32) for _ in range(parts)]
            steps = [jnp.zeros((seqs, LANES), F32) for _ in range(parts)]
            new = []
            for n in range(N):
                bn = bb[row, lanes(n)]
                cn = cb[row, lanes(n)]
                b_sum = c_sum = None
                for k in range(parts):
                    g = gs[n * parts + k] + cn * dy[:, lanes(k)]
                    c_term = hb[step + 1, n, :, lanes(k)] * dy[:, lanes(k)]
                    b_term = g * du[:, lanes(k)]
                    c_sum = c_term if k == 0 else c_sum + c_term
                    b_sum = b_term if k == 0 else b_sum + b_term
                    prods[k] = prods[k] + g * bn
                    carried_g = g * ab[step, n, :, lanes(k)]
                    decay_g = carried_g * hb[step, n, :, lanes(k)]
                    steps[k] = steps[k] + decay_g * rb[n, :, lanes(k)]
                    rg_ref[n, :, lanes(k)] = rg_ref[n, :, lanes(k)] + decay_g * d[:, lanes(k)]
                    new.append(carried_g)
                pb[here, lanes(n)] = b_sum
                pc[here, lanes(n)] = c_sum
            skipg_ref[...] += dy * u
            for k in range(parts):
                dsb[here, lanes(k)] = steps[k] + prods[k] * u[:, lanes(k)]
                du_ref[row, lanes(k)] = (
                    prods[k] * d[:, lanes(k)] + dy[:, lanes(k)] * skip_ref[:, lanes(k)]
                )
            return tuple(new)

        gs = lax.fori_loop(0, BLK, back, gs, unroll=2)
        at = pl.ds(pl.multiple_of(i * BLK * seqs, BLK * seqs), BLK * seqs)
        d_step = (dsb[...] * sig_ref[at, :]).astype(BF16)
        dstep_ref[at, :] = d_step
        bias_ref[...] += jnp.sum(d_step.astype(F32).reshape(BLK, seqs, width), 0)
        total[at, :] += (
            jnp.dot(d_step, w_ref[...], preferred_element_type=F32)
            + jnp.dot(pb[...].astype(BF16), columns[: N * LANES], preferred_element_type=F32)
            + jnp.dot(pc[...].astype(BF16), columns[N * LANES :], preferred_element_type=F32)
        )
        return gs

    lax.fori_loop(
        0,
        length // BLK,
        block,
        tuple(g0_ref[n, :, lanes(k)] for n in range(N) for k in range(parts)),
    )

    @pl.when(group == pl.num_programs(0) - 1)
    def _():
        dproj_ref[...] = total[...].astype(BF16)


def normalized(x):
    return x * lax.rsqrt(jnp.mean(x * x, -1, keepdims=True) + EPS)


def inner_grad_kernel(
    seqs,
    du_ref,
    dproj_ref,
    conv_ref,
    ext_ref,
    normed_ref,
    x_ref,
    u_ref,
    rank_ref,
    dstep_ref,
    dgate_ref,
    w_in_ref,
    w_gate_ref,
    w_x_ref,
    taps_ref,
    after_ref,
    late_ref,
    early_ref,
    gin_ref,
    gx_ref,
    gdt_ref,
    chan_ref,
    gain_ref,
    dconv,
):
    rows, chans = du_ref.shape
    rim = (CONV_TAPS - 1) * seqs
    turn = pl.program_id(0)
    first = pl.multiple_of((pl.num_programs(0) - 1 - turn) * rows, rows)

    @pl.when(turn == 0)
    def _():
        for ref in (gin_ref, gx_ref, gdt_ref, chan_ref, gain_ref):
            ref[...] = jnp.zeros_like(ref)
        dconv[rows:, :] = after_ref[...]

    @pl.when(turn > 0)
    def _():
        dconv[rows:, :] = dconv[:rim, :]

    def by_seq(value):
        return jnp.sum(value.reshape(rows // seqs, seqs, value.shape[-1]), 0)

    d_proj = dproj_ref[...]
    conv = conv_ref[...]
    sig = jax.nn.sigmoid(conv)
    d_conv = (du_ref[...] + dot(d_proj, w_x_ref[...], NT)) * (sig * (1.0 + conv * (1.0 - sig)))
    dconv[:rows, :] = d_conv
    d_inner = jnp.zeros_like(d_conv)
    for tap in range(CONV_TAPS):
        at = (CONV_TAPS - 1 - tap) * seqs
        d_inner = d_inner + taps_ref[tap : tap + 1, :] * dconv[at : at + rows, :]
        ext = ext_ref[pl.ds(pl.multiple_of(first + tap * seqs, seqs), rows), :]
        chan_ref[tap * seqs : (tap + 1) * seqs, :] += by_seq(d_conv * ext)
    chan_ref[CONV_TAPS * seqs :, :] += by_seq(d_conv)
    d_inner = d_inner.astype(BF16)
    part = dot(d_inner, w_in_ref[...]) + dot(dgate_ref[...], w_gate_ref[...])
    half = pl.num_programs(0) // 2

    @pl.when(turn < half)
    def _():
        late_ref[...] = part.astype(BF16)

    @pl.when(turn >= half)
    def _():
        early_ref[...] = part.astype(BF16)

    gain_ref[...] += by_seq(part * normalized(x_ref[...].astype(F32)))
    gin_ref[...] += dot(d_inner, normed_ref[...], TN)
    gx_ref[...] += dot(u_ref[...], d_proj, TN)
    gdt_ref[...] += dot(dstep_ref[...], rank_ref[...], TN)


def output_kernel(shape, peers, *refs):
    micros, group = shape
    early, late, refs = refs[:peers], refs[peers : 2 * peers], refs[2 * peers :]
    x_ref, dres_ref, act_own_ref, act_others_ref, gain_ref, grad_ref, act_ref, grad_tok, act_tok = refs
    x = x_ref[...].astype(F32)
    scale = lax.rsqrt(jnp.mean(x * x, -1, keepdims=True) + EPS)
    xhat = x * scale
    is_early = pl.program_id(0) < pl.num_programs(0) // 2
    d_normed = jnp.zeros_like(x)
    for first, second in zip(early, late):
        d_normed = d_normed + jnp.where(is_early, first[...], second[...]).astype(F32)
    scaled = gain_ref[...] * d_normed
    mean = jnp.mean(scaled * xhat, -1, keepdims=True)
    grad = dres_ref[...].astype(F32) + scale * (scaled - xhat * mean)
    seqs = micros * group
    rows, width = x.shape
    count = rows // seqs
    tensor = lax.axis_index("tensor")
    pieces = []
    for owner in range(peers):
        piece = act_own_ref[...].astype(F32)
        for by in range(1, peers):
            here = lax.rem(tensor + peers - by, peers) == owner
            piece = jnp.where(here, act_others_ref[by - 1].astype(F32), piece)
        pieces.append(piece)
    act = jnp.concatenate(pieces, 1)
    for k in range(width // LANES):
        grad_tok[k] = grad[:, lanes(k)]
        act_tok[k] = act[:, lanes(k)]
    for m in range(micros):
        for g in range(group):
            at = pl.ds(m * group + g, count, stride=seqs)
            for k in range(width // LANES):
                grad_ref[m, g, :, lanes(k)] = grad_tok[k, at, :]
                act_ref[m, g, :, lanes(k)] = act_tok[k, at, :].astype(BF16)


def scan_call(kernel, arrays, outs, scratch, width, chans, chunk=0, cost=None):
    def spec(shape, kind):
        def place(j, rank=len(shape)):
            at = [0] * rank
            if "t" in kind:
                at[0] = chunk
            if "c" in kind:
                at[-1] = j
            if "r" in kind:
                at[0] = j
            return tuple(at)

        return pl.BlockSpec(shape, place)

    return pl.pallas_call(
        kernel,
        grid=(chans // width,),
        in_specs=[spec(shape, kind) for _, shape, kind in arrays],
        out_specs=[spec(shape, kind) for _, shape, kind in outs],
        out_shape=[a for a, _, _ in outs],
        scratch_shapes=[
            s if not isinstance(s, tuple) else pltpu.VMEM(s, F32) for s in scratch
        ],
        compiler_params=pltpu.CompilerParams(vmem_limit_bytes=62 << 20),
        cost_estimate=cost,
    )(*[a for a, _, _ in arrays])


def per_device(
    inputs,
    out_grad,
    lengths,
    routes,
    slots,
    norm_gains,
    router_matrix,
    input_projection,
    inner_projection,
    step_projection,
    step_bias,
    channel_params,
    output_projection,
    expert_up,
    expert_down,
):
    micros, group, length, width = inputs.shape
    seqs = micros * group
    tokens = length * seqs
    owners = lax.axis_size("fsdp") * lax.axis_size("ctx")
    experts = router_matrix.shape[1]
    capacity = max(2, (25 * group * length + 32 * experts - 1) // (32 * experts))
    slots_each = micros * capacity
    rows = experts * slots_each

    def by_token(value):
        return jnp.moveaxis(value, 2, 0).reshape(tokens, *value.shape[3:])

    narrow = jnp.concatenate(
        [inner_projection, step_projection, channel_params, step_bias[:, None]], 1
    )
    x_cols = inner_projection.shape[1]
    cuts = [x_cols, x_cols + R, x_cols + R + channel_params.shape[1]]
    routing = jnp.concatenate([router_matrix, norm_gains.T], 1)
    joined = narrow.shape[0] == routing.shape[0]
    if joined:
        narrow = jnp.concatenate([narrow, routing], 1)
    narrow_cols = narrow.shape[1]
    pad = -narrow_cols % LANES
    first = jnp.concatenate([input_projection[0], jnp.pad(narrow, ((0, 0), (0, pad)))], 1)
    later = jnp.concatenate([input_projection[1], output_projection], 1)
    full = lax.all_gather(first, OWNERS, axis=0, tiled=True)
    later_full = lax.all_gather(later, OWNERS, axis=0, tiled=True)

    position = lax.axis_index("ctx") * length + jnp.arange(length)
    valid = (position[:, None] < lengths.reshape(1, seqs)).astype(F32).reshape(tokens, 1)
    route = by_token(routes)
    slot = by_token(slots)
    kept = slot >= 0
    kept_f = kept.astype(F32)
    micro_of = (jnp.arange(tokens) // group) % micros
    place = jnp.where(kept, route * slots_each + micro_of * capacity + slot, -1)
    pick = (
        jnp.arange(rows).reshape(experts, slots_each, 1) == place[None, None, :]
    ).astype(BF16)
    grad_tok = by_token(out_grad)
    grad_act = grad_tok.astype(F32) * valid

    def packed(value):
        return jnp.einsum("est,td->esd", pick, value, preferred_element_type=F32).astype(BF16)

    def unpacked(value):
        flat = value.reshape(rows, value.shape[-1])
        return lax.optimization_barrier(dot(pick.reshape(rows, tokens), flat, TN))

    def swap_owners(value):
        return lax.all_to_all(value, OWNERS, split_axis=0, concat_axis=0, tiled=True)

    full, grad_packed = lax.optimization_barrier((full, packed(grad_tok)))
    grad_rows_raw = swap_owners(grad_packed)

    w_in = full[:, :width]
    tail = full[:, width:]
    w_gate, w_out = later_full[:, :width], later_full[:, width:]
    w_x = tail[:, : cuts[0]]
    w_step = tail[:, cuts[0] : cuts[1]]
    channel_f = tail[:, cuts[1] : cuts[2]].astype(F32)
    bias_f = tail[:, cuts[2]].astype(F32)
    if joined:
        full_routing = tail[:, cuts[2] + 1 : cuts[2] + 1 + routing.shape[1]]
    else:
        full_routing = lax.all_gather(routing, OWNERS, axis=0, tiled=True)
    w_router = full_routing[:, :experts]
    gains = full_routing[:, experts:].T.astype(F32)
    chans = channel_f.shape[0]
    taps = channel_f[:, :CONV_TAPS].T
    conv_bias = channel_f[:, CONV_TAPS]
    skip = channel_f[:, CONV_TAPS + 1]
    rates = -jnp.exp(channel_f[:, CONV_TAPS + 2 :]).T

    x_tok = lax.optimization_barrier(by_token(inputs))
    x = x_tok.astype(F32)
    normed1 = (normalized(x) * gains[0]).astype(BF16)
    inner = dot(normed1, w_in, NT).astype(BF16)
    rim = (CONV_TAPS - 1) * seqs
    before = moved(inner[tokens - rim :], 1)
    gate_z = dot(normed1, w_gate, NT)
    extended = jnp.concatenate([before, inner], 0).astype(F32)
    conv = conv_bias
    for tap in range(CONV_TAPS):
        conv = conv + taps[tap] * extended[tap * seqs : tap * seqs + tokens]
    u = jax.nn.silu(conv).astype(BF16)
    u_wide = u.astype(F32)
    proj = tensor_total(dot(u, w_x), BF16)
    rank = proj[:, :R].astype(BF16)
    b_vals = proj[:, R : R + N]
    c_vals = proj[:, R + N :]
    step_pre = dot(rank, w_step, NT) + bias_f
    delta = jax.nn.softplus(step_pre)
    lane_width = 2 * LANES if chans % (2 * LANES) == 0 else LANES
    wide_rates = (N, seqs, lane_width)
    state_block = (N, seqs, lane_width)
    call = functools.partial(scan_call, width=lane_width, chans=chans)

    def both_in(value, steps=length):
        return (value, (steps * seqs, lane_width), "tc")

    def by_chan(value):
        return (value, (*value.shape[:-1], lane_width), "c")

    def by_rows(value, steps=length):
        return (value, (steps * seqs, value.shape[1]), "t")

    def cost(steps, ops):
        elements = steps * seqs * chans * N
        return pl.CostEstimate(flops=300 * ops * elements, bytes_accessed=elements, transcendentals=0)

    def out(shape, dtype=F32):
        return jax.ShapeDtypeStruct(shape, dtype)

    [end] = call(
        end_state_kernel,
        [both_in(delta), both_in(u_wide), by_rows(b_vals), by_chan(rates)],
        [by_chan(out((N + 1, seqs, chans)))],
        [wide_rates, (tokens, N * LANES)],
        cost=cost(length, 6),
    )
    end, grad_rows_raw = lax.optimization_barrier((end, grad_rows_raw))
    log_decay = end[N]
    state = carried(end, log_decay, rates, 1, 0)
    pieces = 4 if length % (4 * BLK) == 0 else 1
    steps = length // pieces
    block = steps * seqs
    groups = chans // lane_width
    peers, here = lax.axis_size("tensor"), lax.axis_index("tensor")

    def cut(value, *shape):
        return value, pl.BlockSpec(shape, lambda p, j: (p, j))

    def by_piece(value):
        return value, pl.BlockSpec((block, value.shape[1]), lambda p, j: (p, 0))

    def by_group(value):
        rank = value.ndim - 1
        return value, pl.BlockSpec(
            (*value.shape[:-1], lane_width), lambda p, j: (0,) * rank + (j,)
        )

    arrays = [
        cut(delta, block, lane_width),
        cut(u_wide, block, lane_width),
        cut(gate_z, block, lane_width),
        by_piece(b_vals),
        by_piece(c_vals),
        by_group(rates),
        by_group(skip[None]),
        (w_out, pl.BlockSpec((lane_width, width), lambda p, j: (j, 0))),
        by_group(state),
        (x_tok, pl.BlockSpec((tokens, width), lambda p, j: (0, 0))),
    ]
    results = [
        cut(out((tokens, chans)), block, lane_width),
        cut(out((tokens, chans), BF16), block, lane_width),
        (
            out((length // BLK, N, seqs, chans)),
            pl.BlockSpec((steps // BLK, N, seqs, lane_width), lambda p, j: (p, 0, 0, j)),
        ),
        (out((tokens, width)), pl.BlockSpec((tokens, width), lambda p, j: (0, 0))),
    ]
    y_vals, gated, starts, resid = pl.pallas_call(
        functools.partial(forward_kernel, peers),
        grid=(pieces, groups),
        in_specs=[spec for _, spec in arrays],
        out_specs=[spec for _, spec in results],
        out_shape=[value for value, _ in results],
        scratch_shapes=[
            pltpu.VMEM(wide_rates, F32),
            pltpu.VMEM((block, N * LANES), F32),
            pltpu.VMEM((block, N * LANES), F32),
            pltpu.VMEM((groups, *state_block), F32),
            pltpu.VMEM((block, width), F32),
            pltpu.VMEM((pieces, block, width), BF16),
            pltpu.VMEM((peers - 1, pieces, block, width), BF16),
            pltpu.SemaphoreType.DMA((peers - 1, pieces)),
            pltpu.SemaphoreType.DMA((peers - 1, pieces)),
        ],
        compiler_params=pltpu.CompilerParams(
            collective_id=2, has_side_effects=True, vmem_limit_bytes=62 << 20
        ),
        cost_estimate=cost(length, 10),
    )(*[value for value, _ in arrays])
    silu_z, gate_slope = silu_parts(gate_z)

    scale2 = lax.rsqrt(jnp.mean(resid * resid, -1, keepdims=True) + EPS)
    xhat2 = resid * scale2
    normed2 = (xhat2 * gains[1]).astype(BF16)
    probs = jax.nn.softmax(dot(normed2, w_router), -1)
    onehot = (route[:, None] == jnp.arange(experts)).astype(F32)
    gate = jnp.sum(probs * onehot, -1, keepdims=True) * kept_f[:, None]
    share = width // peers

    def half(value):
        cut = value[..., :share]
        for peer in range(1, peers):
            cut = jnp.where(here == peer, value[..., peer * share : (peer + 1) * share], cut)
        return cut

    x_rows = tensor_columns(swap_owners(packed(half(normed2))))
    gate_rows = swap_owners(
        jnp.sum(jnp.where(pick > 0, gate[:, 0], 0.0), -1)[:, None, :]
    )
    grad_rows = (jnp.swapaxes(gate_rows, 1, 2) * grad_rows_raw.astype(F32)).astype(BF16)
    up, down = expert_up[0], expert_down[0]

    def product(a, b, terms):
        return jnp.einsum(terms, a, b, preferred_element_type=F32)

    def halves(matrix, axis):
        low, high = jnp.split(matrix, 2, axis)
        return jnp.where(here == 0, low, high), jnp.where(here == 0, high, low)

    def scattered(value):
        return lax.psum_scatter(value, "tensor", scatter_dimension=2, tiled=True).astype(BF16)

    hidden = product(x_rows, up, "srd,df->srf")
    act_float, gelu_pull = jax.vjp(lambda v: jax.nn.gelu(v, approximate=True), hidden)
    act = act_float.astype(BF16)
    d_act = product(grad_rows, down, "srd,fd->srf")
    d_hidden = gelu_pull(d_act)[0].astype(BF16)
    q_rows = jnp.sum(act.astype(F32) * d_act, -1)
    if peers == 2:
        up_own, up_other = halves(up, 0)
        down_own, down_other = halves(down, 1)
        x_sent = product(d_hidden, up_other, "srf,df->srd").astype(BF16)
        x_got = swapped(x_sent)
        act_late, _ = lax.optimization_barrier((act, x_sent))
        x_own = product(d_hidden, up_own, "srf,df->srd")
        y_sent = product(act_late, down_other, "srf,fd->srd").astype(BF16)
        x_got, y_sent = lax.optimization_barrier((x_got, y_sent))
        back_x = swap_owners((x_own + x_got.astype(F32)).astype(BF16))
        y_got = swapped(y_sent)
        y_own = product(act_late, down_own, "srf,fd->srd")
        share_y = (y_own + y_got.astype(F32)).astype(BF16)
    else:
        back_x = swap_owners(scattered(product(d_hidden, up, "srf,df->srd")))
        share_y = scattered(product(act, down, "srf,fd->srd"))
    q_back = swap_owners(q_rows[:, None, :])
    grad_up = product(x_rows, d_hidden, "srd,srf->df")
    grad_down = product(act, grad_rows, "srf,srd->fd")
    back_x, grad_up, grad_down, share_y = lax.optimization_barrier(
        (back_x, grad_up, grad_down, share_y)
    )
    expert_dx = unpacked(back_x)
    q_part = jnp.sum(jnp.where(pick > 0, q_back[:, 0, :, None], 0.0), (0, 1))
    x_half = half(xhat2)
    gain_half = half(gains[1])
    grad_half = half(grad_act)
    router_half = half(w_router.T)
    sums = jnp.stack([q_part, jnp.sum(gain_half * expert_dx * x_half, -1)])
    sums = tensor_total(sums, F32)
    d_logits = (sums[0][:, None] * (onehot - probs)).astype(BF16)
    grad_router = dot(normed2, d_logits, TN)
    by_router = dot((xhat2 * gains[1]).astype(BF16), w_router)
    mean_term = (
        sums[1][:, None] + jnp.sum(d_logits.astype(F32) * by_router, -1, keepdims=True)
    ) / width
    d_normed2 = expert_dx + dot(d_logits, router_half)
    gain_grad2 = tensor_columns(jnp.sum(d_normed2 * x_half, 0, keepdims=True))[0]
    d_resid_half = grad_half + scale2 * (gain_half * d_normed2 - x_half * mean_term)

    d_mixed = tensor_columns(d_resid_half.astype(BF16))
    d_mixed, share_y = lax.optimization_barrier((d_mixed, share_y))
    expert_y = unpacked(swap_owners(share_y))
    act_half = (valid * (half(resid) + gate * expert_y)).astype(BF16)
    d_gated = dot(d_mixed, w_out, NT)
    d_y = d_gated * silu_z
    [start_grad] = call(
        start_grad_kernel,
        [both_in(delta), both_in(d_y), by_rows(c_vals), by_chan(rates)],
        [by_chan(out((N, seqs, chans)))],
        [wide_rates, (tokens, N * LANES)],
        cost=cost(length, 6),
    )
    d_gate_z = (d_gated * y_vals * gate_slope).astype(BF16)

    def owned(value):
        return lax.psum_scatter(
            value.astype(BF16), OWNERS, scatter_dimension=0, tiled=True
        ).astype(F32)

    grad_end, act_others, early = carried(
        start_grad, log_decay, rates, -1, 1, act_half, (d_gate_z, normed1, gated, d_mixed)
    )
    mine_early = owned(early)
    w_step_wide = jnp.pad(w_step, ((0, 0), (0, LANES - R)))
    d_step, du_part, d_proj_part, rate_grad, bias_sums, skip_sums = call(
        backward_kernel,
        [
            both_in(delta),
            both_in(u_wide),
            both_in(d_y),
            (jax.nn.sigmoid(step_pre), (tokens, lane_width), "tc"),
            by_rows(b_vals),
            by_rows(c_vals),
            by_chan(rates),
            by_chan(skip[None]),
            (w_step_wide, (lane_width, LANES), "r"),
            by_chan(starts),
            by_chan(grad_end),
        ],
        [
            by_chan(out((tokens, chans), BF16)),
            by_chan(out((tokens, chans))),
            (out((tokens, LANES), BF16), (tokens, LANES), ""),
            by_chan(out((N, seqs, chans))),
            by_chan(out((seqs, chans))),
            by_chan(out((seqs, chans))),
        ],
        [
            wide_rates,
            (tokens, N * LANES),
            (tokens, N * LANES),
            (BLK + 1, N, seqs, lane_width),
            (BLK, N, seqs, lane_width),
            (BLK * seqs, N * LANES),
            (BLK * seqs, N * LANES),
            (BLK * seqs, lane_width),
            (tokens, LANES),
            pltpu.VMEM((2 * N * LANES, LANES), BF16),
        ],
        cost=cost(length, 24),
    )
    d_proj = tensor_total(d_proj_part, BF16).astype(BF16)
    step_bias_grad = jnp.sum(bias_sums, 0)
    skip_grad = jnp.sum(skip_sums, 0)
    w_x_wide = jnp.pad(w_x, ((0, 0), (0, LANES - x_cols)))
    rim_u = du_part[:rim] + dot(d_proj[:rim], w_x_wide, NT)
    after = moved(rim_u * silu_parts(conv[:rim])[1], -1)
    steps = length // 4
    block = steps * seqs
    turns = length // steps

    def from_end(value):
        return value, pl.BlockSpec((block, value.shape[1]), lambda i: (turns - 1 - i, 0))

    def whole(value):
        return value, pl.BlockSpec(value.shape, lambda i: (0, 0))

    arrays = [
        from_end(du_part),
        from_end(d_proj),
        from_end(conv),
        whole(extended),
        from_end(normed1),
        from_end(x_tok),
        from_end(u),
        from_end(rank),
        from_end(d_step),
        from_end(d_gate_z),
        whole(w_in),
        whole(w_gate),
        whole(w_x_wide),
        whole(taps),
        whole(after),
    ]
    results = [
        (
            out((tokens // 2, width), BF16),
            pl.BlockSpec((block, width), lambda i: (jnp.maximum(turns // 2 - 1 - i, 0), 0)),
        ),
        (
            out((tokens // 2, width), BF16),
            pl.BlockSpec(
                (block, width), lambda i: (jnp.minimum(turns - 1 - i, turns // 2 - 1), 0)
            ),
        ),
        whole(out((chans, width))),
        whole(out((chans, LANES))),
        whole(out((chans, R))),
        whole(out(((CONV_TAPS + 1) * seqs, chans))),
        whole(out((seqs, width))),
    ]
    late_part, early_part, grad_in, grad_xproj, grad_dt, conv_sums, gain_sums = pl.pallas_call(
        functools.partial(inner_grad_kernel, seqs),
        grid=(turns,),
        in_specs=[spec for _, spec in arrays],
        out_specs=[spec for _, spec in results],
        out_shape=[value for value, _ in results],
        scratch_shapes=[pltpu.VMEM((block + rim, chans), F32)],
        compiler_params=pltpu.CompilerParams(vmem_limit_bytes=62 << 20),
    )(*[value for value, _ in arrays])
    late_part, mine_early = lax.optimization_barrier((late_part, mine_early))
    grad_xproj = grad_xproj[:, :x_cols]
    conv_sums = jnp.sum(conv_sums.reshape(CONV_TAPS + 1, seqs, chans), 1)
    gain_grad1 = jnp.sum(gain_sums, 0)

    narrow_grads = jnp.concatenate(
        [
            grad_xproj,
            grad_dt,
            conv_sums.T,
            skip_grad[:, None],
            (jnp.sum(rate_grad, 1) * rates).T,
            step_bias_grad[:, None],
        ],
        1,
    )
    routing_grads = jnp.concatenate([grad_router, gain_grad1[:, None], gain_grad2[:, None]], 1)
    if joined:
        narrow_grads = jnp.concatenate([narrow_grads, routing_grads], 1)
    wide_grads = jnp.concatenate(
        [grad_in, jnp.pad(narrow_grads, ((0, 0), (0, pad)))], 1
    )

    halves = [late_part, early_part]
    if peers == 2:
        exchanged = [swapped(part) for part in halves]
    else:
        exchanged = [lax.all_gather(part, "tensor") for part in halves]
    mine, exchanged = halved(wide_grads, exchanged)
    normed_parts = []
    for own, others in zip(halves, exchanged):
        if peers == 2:
            normed_parts.append([own, others])
        else:
            normed_parts.append([others[k] for k in range(peers)])
    late_parts, early_parts = normed_parts

    def rows_of(value):
        return value, pl.BlockSpec((block, value.shape[1]), lambda i: (i, 0))

    def early_rows(value):
        return value, pl.BlockSpec((block, width), lambda i: (jnp.minimum(i, turns // 2 - 1), 0))

    def late_rows(value):
        return value, pl.BlockSpec((block, width), lambda i: (jnp.maximum(i - turns // 2, 0), 0))

    arrays = (
        [early_rows(part) for part in early_parts]
        + [late_rows(part) for part in late_parts]
        + [
            rows_of(x_tok),
            rows_of(d_mixed),
            rows_of(act_half),
            (act_others, pl.BlockSpec((peers - 1, block, share), lambda i: (0, i, 0))),
            whole(gains[:1]),
        ]
    )
    out_spec = pl.BlockSpec((micros, group, steps, width), lambda i: (0, 0, i, 0))
    input_grad, activations = pl.pallas_call(
        functools.partial(output_kernel, (micros, group), peers),
        grid=(turns,),
        in_specs=[spec for _, spec in arrays],
        out_specs=[out_spec, out_spec],
        out_shape=[out(inputs.shape), out(inputs.shape, BF16)],
        scratch_shapes=[pltpu.VMEM((width // LANES, block, LANES), F32)] * 2,
        compiler_params=pltpu.CompilerParams(vmem_limit_bytes=62 << 20),
    )(*[value for value, _ in arrays])
    mine_tail = mine[:, width:]
    if joined:
        mine_routing = mine_tail[:, cuts[2] + 1 : cuts[2] + 1 + routing.shape[1]]
    else:
        mine_routing, _ = halved(routing_grads)
    gains_out = jnp.stack(
        [tensor_total(mine_routing[None, :, experts], F32)[0], mine_routing[:, experts + 1]]
    )
    return (
        activations,
        input_grad,
        gains_out,
        mine_routing[:, :experts],
        jnp.stack([mine[:, :width], mine_early[:, :width]]),
        mine_tail[:, : cuts[0]],
        mine_tail[:, cuts[0] : cuts[1]],
        mine_tail[:, cuts[2]],
        mine_tail[:, cuts[1] : cuts[2]],
        mine_early[:, width:],
        grad_up[None],
        grad_down[None],
    )


def solution(mesh):
    return jax.shard_map(
        per_device,
        mesh=mesh,
        in_specs=(
            P(None, "fsdp", "ctx", None),
            P(None, "fsdp", "ctx", None),
            P(None, "fsdp"),
            P(None, "fsdp", "ctx"),
            P(None, "fsdp", "ctx"),
            P(None, ("fsdp", "ctx")),
            P(("fsdp", "ctx"), None),
            P(None, ("fsdp", "ctx", "tensor"), None),
            P(("fsdp", "ctx", "tensor"), None),
            P(("fsdp", "ctx", "tensor"), None),
            P(("fsdp", "ctx", "tensor")),
            P(("fsdp", "ctx", "tensor"), None),
            P(("fsdp", "ctx", "tensor"), None),
            P(("fsdp", "ctx"), None, "tensor"),
            P(("fsdp", "ctx"), "tensor", None),
        ),
        out_specs=(
            P(None, "fsdp", "ctx", None),
            P(None, "fsdp", "ctx", None),
            P(None, ("fsdp", "ctx")),
            P(("fsdp", "ctx"), None),
            P(None, ("fsdp", "ctx", "tensor"), None),
            P(("fsdp", "ctx", "tensor"), None),
            P(("fsdp", "ctx", "tensor"), None),
            P(("fsdp", "ctx", "tensor")),
            P(("fsdp", "ctx", "tensor"), None),
            P(("fsdp", "ctx", "tensor"), None),
            P(("fsdp", "ctx"), None, "tensor"),
            P(("fsdp", "ctx"), "tensor", None),
        ),
        check_vma=False,
    )
```

```python
import functools

import jax
import jax.numpy as jnp
from jax import lax
from jax.experimental import pallas as pl
from jax.experimental.pallas import tpu as pltpu
from jax.sharding import PartitionSpec as P

N = 16
CONV_TAPS = 4
R = 48
EPS = 1e-05
VECTORS = CONV_TAPS + 2 + N + 1
BLK = 8
LANES = 128
F32 = jnp.float32
BF16 = jnp.bfloat16
OWNERS = ("fsdp", "ctx")


def silu_parts(value):
    sig = jax.nn.sigmoid(value)
    return value * sig, sig * (1.0 + value * (1.0 - sig))


def swapped(value):
    return lax.ppermute(value, "tensor", [(0, 1), (1, 0)])


def tensor_total(value, dtype):
    sent = value.astype(dtype)
    if lax.axis_size("tensor") == 2:
        return sent.astype(F32) + swapped(sent).astype(F32)
    return jnp.sum(lax.all_gather(sent, "tensor").astype(F32), axis=0)


def tensor_columns(value):
    if lax.axis_size("tensor") == 2:
        other = swapped(value)
        first = lax.axis_index("tensor") == 0
        return jnp.concatenate(
            [jnp.where(first, value, other), jnp.where(first, other, value)], -1
        )
    return lax.all_gather(value, "tensor", axis=value.ndim - 1, tiled=True)


def halved(value, beside=()):
    beside = list(beside)
    sizes = [lax.axis_size(axis) for axis in OWNERS]
    bits = [(axis, 1 << k) for axis, size in zip(OWNERS, sizes) for k in reversed(range(size.bit_length() - 1))]
    rows = value.shape[0] >> len(bits)
    for place in reversed(range(len(bits))):
        axis, bit = bits[place]
        view = value.reshape(1 << place, 2, rows, value.shape[-1])
        high = (lax.axis_index(axis) & bit) != 0
        own = jnp.where(high, view[:, 1], view[:, 0])
        other = jnp.where(high, view[:, 0], view[:, 1]).astype(BF16)
        got = lax.ppermute(other, axis, [(i, i ^ bit) for i in range(lax.axis_size(axis))])
        value = own.astype(F32) + got.astype(F32)
        turn = len(bits) - 1 - place
        if 0 < turn <= len(beside):
            turn -= 1
            value, beside[turn] = lax.optimization_barrier((value, beside[turn]))
    return value.reshape(rows, value.shape[-1]), beside


def moved(value, by):
    peers = lax.axis_size("ctx")
    pairs = [(i, i + by) for i in range(peers) if 0 <= i + by < peers]
    return lax.ppermute(value, "ctx", pairs)


TN = (((0,), (0,)), ((), ()))
NT = (((1,), (1,)), ((), ()))
NN = (((1,), (0,)), ((), ()))


def dot(a, b, dims=NN):
    return lax.dot_general(a, b, dims, preferred_element_type=F32)


MESH = pl.DeviceIdType.MESH


def greet(peers):
    barrier = pltpu.get_barrier_semaphore()
    for peer in peers:
        pl.semaphore_signal(barrier, inc=1, device_id=peer, device_id_type=MESH)
    pl.semaphore_wait(barrier, len(peers))


def carry_kernel(sign, ranges, peers, end_ref, log_ref, r_ref, *refs):
    if peers:
        own_ref, left_refs, right_refs = refs[0], refs[1:5:2], refs[2:5:2]
        out_ref, others_ref, products_ref = refs[5:8]
        sent, got, log_out, send_sem, recv_sem, own_sem, others_sem = refs[8:]
    else:
        out_ref, sent, got, log_out, send_sem, recv_sem = refs
    turns, groups, _, width = sent.shape
    seqs = log_ref.shape[0]
    fsdp, me, tensor = lax.axis_index("fsdp"), lax.axis_index("ctx"), lax.axis_index("tensor")

    def peer(by):
        return (fsdp, lax.rem(me + by + ranges, ranges), tensor)

    shifts = [sign * (1 << turn) for turn in range(turns)]
    partners = [(fsdp, me, lax.rem(tensor + by, peers)) for by in range(1, peers)]
    near = sorted({s % ranges for s in shifts} | {-s % ranges for s in shifts})
    greet([peer(by) for by in near] + partners)
    beside = [
        pltpu.make_async_remote_copy(
            src_ref=own_ref,
            dst_ref=others_ref.at[k],
            send_sem=own_sem.at[k],
            recv_sem=others_sem.at[k],
            device_id=partner,
            device_id_type=MESH,
        )
        for k, partner in enumerate(partners)
    ]
    for extra in beside:
        extra.start()

    def copy(turn, group):
        return pltpu.make_async_remote_copy(
            src_ref=sent.at[turn, group],
            dst_ref=got.at[turn, group],
            send_sem=send_sem.at[turn, group],
            recv_sem=recv_sem.at[turn, group],
            device_id=peer(shifts[turn]),
            device_id_type=MESH,
        )

    def decayed(log, cols, n):
        return jnp.exp(log * r_ref[n : n + 1, cols])

    def receive(turn, group):
        copy(turn, group).wait_recv()
        cols = slice(group * width, (group + 1) * width)
        reach = 1 << turn
        real = (me >= reach) if sign > 0 else (me < ranges - reach)

        def part(k):
            rows = got[turn, group, k * seqs : (k + 1) * seqs, :].astype(F32)
            return jnp.where(real, rows, 0.0)

        log = part(N) + part(N + 1)
        if turn == 0:
            for n in range(N):
                out_ref[n, :, cols] = part(n)
            log_out[:, cols] = log
        else:
            late = log_out[:, cols]
            for n in range(N):
                out_ref[n, :, cols] = out_ref[n, :, cols] + decayed(late, cols, n) * part(n)
            log_out[:, cols] = late + log

    for turn in range(turns):
        if turn == 1 and peers:
            for k, (left, right) in enumerate(zip(left_refs, right_refs)):
                count = right.shape[1]

                def product(i, _, k=k, left=left, right=right, count=count):
                    at = pl.ds(pl.multiple_of(i * LANES, LANES), LANES)
                    value = dot(left[:, at], right[...], TN)
                    products_ref[at, k * count : (k + 1) * count] = value.astype(BF16)
                    return 0

                lax.fori_loop(0, left.shape[1] // LANES, product, 0)
        for group in range(groups):
            cols = slice(group * width, (group + 1) * width)
            own_log = log_ref[:, cols]
            if turn > 0:
                receive(turn - 1, group)
            for n in range(0, N, 2):
                pair = []
                for k in (n, n + 1):
                    value = end_ref[k, :, cols]
                    if turn > 0:
                        value = value + decayed(own_log, cols, k) * out_ref[k, :, cols]
                    pair.append(value)
                sent[turn, group, n * seqs : (n + 2) * seqs, :] = jnp.concatenate(pair, 0).astype(
                    BF16
                )
            log = own_log if turn == 0 else own_log + log_out[:, cols]
            high = log.astype(BF16).astype(F32)
            sent[turn, group, N * seqs :, :] = jnp.concatenate([high, log - high], 0).astype(BF16)
            copy(turn, group).start()
    for group in range(groups):
        receive(turns - 1, group)
    for turn in range(turns):
        for group in range(groups):
            copy(turn, group).wait_send()
    for extra in beside:
        extra.wait()


def carried(end, log_decay, rates, sign, ident, shared=None, factors=()):
    _, seqs, chans = end.shape
    ranges = lax.axis_size("ctx")
    turns = (ranges - 1).bit_length()
    groups = 3 if chans % (3 * LANES) == 0 else 1
    block = (turns, groups, (N + 2) * seqs, chans // groups)
    vmem = pl.BlockSpec(memory_space=pltpu.VMEM)
    anywhere = pl.BlockSpec(memory_space=pl.ANY)
    peers = 0 if shared is None else lax.axis_size("tensor")
    state = jax.ShapeDtypeStruct((N, seqs, chans), F32)
    scratch = [
        pltpu.VMEM(block, BF16),
        pltpu.VMEM(block, BF16),
        pltpu.VMEM((seqs, chans), F32),
        pltpu.SemaphoreType.DMA((turns, groups)),
        pltpu.SemaphoreType.DMA((turns, groups)),
    ]
    if peers:
        others = jax.ShapeDtypeStruct((peers - 1, *shared.shape), shared.dtype)
        scratch += [pltpu.SemaphoreType.DMA((peers - 1,)), pltpu.SemaphoreType.DMA((peers - 1,))]
        products = jax.ShapeDtypeStruct(
            (factors[0].shape[1], factors[1].shape[1] + factors[3].shape[1]), BF16
        )
    return pl.pallas_call(
        functools.partial(carry_kernel, sign, ranges, peers),
        in_specs=[vmem] * 3 + ([anywhere] + [vmem] * len(factors) if peers else []),
        out_specs=[vmem, anywhere, vmem] if peers else vmem,
        out_shape=[state, others, products] if peers else state,
        scratch_shapes=scratch,
        compiler_params=pltpu.CompilerParams(
            collective_id=ident, has_side_effects=True, vmem_limit_bytes=48 << 20
        ),
        cost_estimate=pl.CostEstimate(flops=20 << 30, bytes_accessed=1 << 20, transcendentals=0),
    )(end[:N], log_decay, rates, *([shared, *factors] if peers else []))


def spread_matrix():
    rows = lax.broadcasted_iota(jnp.int32, (2 * N, N * LANES), 0) % N
    cols = lax.broadcasted_iota(jnp.int32, (2 * N, N * LANES), 1) // LANES
    return (rows == cols).astype(F32).astype(BF16)


def spread_into(pairs, rows):
    def turn(i, _):
        matrix = spread_matrix()
        at = pl.ds(pl.multiple_of(i * LANES, LANES), LANES)
        for source, target in pairs:
            value = source[at, :]
            high = value.astype(BF16)
            low = (value - high.astype(F32)).astype(BF16)
            target[at, :] = jnp.dot(
                jnp.concatenate([high, low], 1), matrix, preferred_element_type=F32
            )
        return 0

    lax.fori_loop(0, rows // LANES, turn, 0)


def lanes(k):
    return slice(k * LANES, (k + 1) * LANES)


def end_state_kernel(d_ref, u_ref, b_ref, r_ref, end_ref, rb, bb):
    rows, width = d_ref.shape
    seqs = rb.shape[1]
    length = rows // seqs
    parts = width // LANES
    for n in range(N):
        rb[n] = jnp.broadcast_to(r_ref[n : n + 1, :], (seqs, width))

    @pl.when(pl.program_id(0) == 0)
    def _():
        spread_into([(b_ref, bb)], rows)

    def body(t, carry):
        hs, total = carry
        row = pl.ds(pl.multiple_of(t * seqs, seqs), seqs)
        d = d_ref[row, :]
        du = d * u_ref[row, :]
        new = []
        for n in range(N):
            bn = bb[row, lanes(n)]
            for k in range(parts):
                a = jnp.exp(d[:, lanes(k)] * rb[n, :, lanes(k)])
                new.append(a * hs[n * parts + k] + du[:, lanes(k)] * bn)
        return tuple(new), total + d

    zero = jnp.zeros((seqs, LANES), F32)
    hs, total = lax.fori_loop(
        0, length, body, ((zero,) * (N * parts), jnp.zeros((seqs, width), F32)), unroll=4
    )
    for n in range(N):
        for k in range(parts):
            end_ref[n, :, lanes(k)] = hs[n * parts + k]
    end_ref[N] = total


def forward_kernel(
    peers,
    d_ref,
    u_ref,
    z_ref,
    b_ref,
    c_ref,
    r_ref,
    skip_ref,
    w_ref,
    h0_ref,
    x_ref,
    y_ref,
    gated_ref,
    st_ref,
    resid_ref,
    rb,
    bb,
    cb,
    state,
    total,
    sent,
    got,
    send_sem,
    recv_sem,
):
    rows, width = d_ref.shape
    seqs = rb.shape[1]
    length = rows // seqs
    parts = width // LANES
    piece, group = pl.program_id(0), pl.program_id(1)
    pieces, last = pl.num_programs(0), pl.num_programs(1) - 1
    fsdp, ctx, tensor = lax.axis_index("fsdp"), lax.axis_index("ctx"), lax.axis_index("tensor")
    partners = [(fsdp, ctx, lax.rem(tensor + by, peers)) for by in range(1, peers)]

    def copy(k, which):
        return pltpu.make_async_remote_copy(
            src_ref=sent.at[which],
            dst_ref=got.at[k, which],
            send_sem=send_sem.at[k, which],
            recv_sem=recv_sem.at[k, which],
            device_id=partners[k],
            device_id_type=MESH,
        )

    @pl.when((piece == 0) & (group == 0))
    def _():
        greet(partners)

    for n in range(N):
        rb[n] = jnp.broadcast_to(r_ref[n : n + 1, :], (seqs, width))

    @pl.when(group == 0)
    def _():
        spread_into([(b_ref, bb), (c_ref, cb)], rows)
        total[...] = jnp.zeros_like(total)

    @pl.when(piece == 0)
    def _():
        state[group] = h0_ref[...]

    def block(i, hs):
        for n in range(N):
            for k in range(parts):
                st_ref[i, n, :, lanes(k)] = hs[n * parts + k]

        def body(step, hs):
            t = i * BLK + step
            row = pl.ds(pl.multiple_of(t * seqs, seqs), seqs)
            d = d_ref[row, :]
            u = u_ref[row, :]
            du = d * u
            ys = [u[:, lanes(k)] * skip_ref[:, lanes(k)] for k in range(parts)]
            new = []
            for n in range(N):
                bn = bb[row, lanes(n)]
                cn = cb[row, lanes(n)]
                for k in range(parts):
                    a = jnp.exp(d[:, lanes(k)] * rb[n, :, lanes(k)])
                    h = a * hs[n * parts + k] + du[:, lanes(k)] * bn
                    ys[k] = ys[k] + h * cn
                    new.append(h)
            for k in range(parts):
                y_ref[row, lanes(k)] = ys[k]
            return tuple(new)

        return lax.fori_loop(0, BLK, body, hs, unroll=4)

    hs = lax.fori_loop(
        0,
        length // BLK,
        block,
        tuple(state[group, n, :, lanes(k)] for n in range(N) for k in range(parts)),
    )
    for n in range(N):
        for k in range(parts):
            state[group, n, :, lanes(k)] = hs[n * parts + k]
    z = z_ref[...]
    gated = (y_ref[...] * (z * jax.nn.sigmoid(z))).astype(BF16)
    gated_ref[...] = gated
    total[...] += jnp.dot(gated, w_ref[...], preferred_element_type=F32)

    def add(which):
        for k in range(peers - 1):
            copy(k, which).wait_recv()
        at = pl.ds(pl.multiple_of(which * rows, rows), rows)
        value = x_ref[at, :].astype(F32)
        own = sent[which].astype(F32)
        if peers == 2:
            value = value + (own + got[0, which].astype(F32))
        else:
            for owner in range(peers):
                term = own
                for k in range(peers - 1):
                    here = lax.rem(tensor + peers - k - 1, peers) == owner
                    term = jnp.where(here, got[k, which].astype(F32), term)
                value = value + term
        resid_ref[at, :] = value

    @pl.when(group == last)
    def _():
        sent[piece] = total[...].astype(BF16)
        for k in range(peers - 1):
            copy(k, piece).start()

        @pl.when(piece > 1)
        def _():
            add(piece - 2)

    @pl.when((group == last) & (piece == pieces - 1))
    def _():
        count = sent.shape[0]
        for which in range(max(count - 2, 0), count):
            add(which)
        for which in range(count):
            for k in range(peers - 1):
                copy(k, which).wait_send()


def start_grad_kernel(d_ref, dy_ref, c_ref, r_ref, g_ref, rb, cb):
    rows, width = d_ref.shape
    seqs = rb.shape[1]
    length = rows // seqs
    parts = width // LANES
    for n in range(N):
        rb[n] = jnp.broadcast_to(r_ref[n : n + 1, :], (seqs, width))

    @pl.when(pl.program_id(0) == 0)
    def _():
        spread_into([(c_ref, cb)], rows)

    def body(i, gs):
        t = length - 1 - i
        row = pl.ds(pl.multiple_of(t * seqs, seqs), seqs)
        d = d_ref[row, :]
        dy = dy_ref[row, :]
        new = []
        for n in range(N):
            cn = cb[row, lanes(n)]
            for k in range(parts):
                a = jnp.exp(d[:, lanes(k)] * rb[n, :, lanes(k)])
                new.append(a * (gs[n * parts + k] + dy[:, lanes(k)] * cn))
        return tuple(new)

    zero = jnp.zeros((seqs, LANES), F32)
    gs = lax.fori_loop(0, length, body, (zero,) * (N * parts), unroll=4)
    for n in range(N):
        for k in range(parts):
            g_ref[n, :, lanes(k)] = gs[n * parts + k]


def backward_kernel(
    d_ref,
    u_ref,
    dy_ref,
    sig_ref,
    b_ref,
    c_ref,
    r_ref,
    skip_ref,
    w_ref,
    st_ref,
    g0_ref,
    dstep_ref,
    du_ref,
    dproj_ref,
    rg_ref,
    bias_ref,
    skipg_ref,
    rb,
    bb,
    cb,
    hb,
    ab,
    pb,
    pc,
    dsb,
    total,
    columns,
):
    rows, width = d_ref.shape
    seqs = rb.shape[1]
    length = rows // seqs
    parts = width // LANES
    group = pl.program_id(0)
    for n in range(N):
        rb[n] = jnp.broadcast_to(r_ref[n : n + 1, :], (seqs, width))

    @pl.when(group == 0)
    def _():
        spread_into([(b_ref, bb), (c_ref, cb)], rows)
        total[...] = jnp.zeros_like(total)
        source = lax.broadcasted_iota(jnp.int32, columns.shape, 0) // LANES
        target = lax.broadcasted_iota(jnp.int32, columns.shape, 1)
        columns[...] = (source + R == target).astype(F32).astype(BF16)

    rg_ref[...] = jnp.zeros_like(rg_ref)
    bias_ref[...] = jnp.zeros_like(bias_ref)
    skipg_ref[...] = jnp.zeros_like(skipg_ref)

    def block(turn, gs):
        i = length // BLK - 1 - turn

        def again(step, hs):
            t = i * BLK + step
            row = pl.ds(pl.multiple_of(t * seqs, seqs), seqs)
            d = d_ref[row, :]
            du = d * u_ref[row, :]
            new = []
            for n in range(N):
                bn = bb[row, lanes(n)]
                for k in range(parts):
                    a = jnp.exp(d[:, lanes(k)] * rb[n, :, lanes(k)])
                    h = a * hs[n * parts + k] + du[:, lanes(k)] * bn
                    ab[step, n, :, lanes(k)] = a
                    hb[step + 1, n, :, lanes(k)] = h
                    new.append(h)
            return tuple(new)

        hs = tuple(st_ref[i, n, :, lanes(k)] for n in range(N) for k in range(parts))
        for n in range(N):
            for k in range(parts):
                hb[0, n, :, lanes(k)] = hs[n * parts + k]
        lax.fori_loop(0, BLK, again, hs, unroll=4)

        def back(turn, gs):
            step = BLK - 1 - turn
            t = i * BLK + step
            row = pl.ds(pl.multiple_of(t * seqs, seqs), seqs)
            here = pl.ds(pl.multiple_of(step * seqs, seqs), seqs)
            d = d_ref[row, :]
            u = u_ref[row, :]
            dy = dy_ref[row, :]
            du = d * u
            prods = [jnp.zeros((seqs, LANES), F32) for _ in range(parts)]
            steps = [jnp.zeros((seqs, LANES), F32) for _ in range(parts)]
            new = []
            for n in range(N):
                bn = bb[row, lanes(n)]
                cn = cb[row, lanes(n)]
                b_sum = c_sum = None
                for k in range(parts):
                    g = gs[n * parts + k] + cn * dy[:, lanes(k)]
                    c_term = hb[step + 1, n, :, lanes(k)] * dy[:, lanes(k)]
                    b_term = g * du[:, lanes(k)]
                    c_sum = c_term if k == 0 else c_sum + c_term
                    b_sum = b_term if k == 0 else b_sum + b_term
                    prods[k] = prods[k] + g * bn
                    carried_g = g * ab[step, n, :, lanes(k)]
                    decay_g = carried_g * hb[step, n, :, lanes(k)]
                    steps[k] = steps[k] + decay_g * rb[n, :, lanes(k)]
                    rg_ref[n, :, lanes(k)] = rg_ref[n, :, lanes(k)] + decay_g * d[:, lanes(k)]
                    new.append(carried_g)
                pb[here, lanes(n)] = b_sum
                pc[here, lanes(n)] = c_sum
            skipg_ref[...] += dy * u
            for k in range(parts):
                dsb[here, lanes(k)] = steps[k] + prods[k] * u[:, lanes(k)]
                du_ref[row, lanes(k)] = (
                    prods[k] * d[:, lanes(k)] + dy[:, lanes(k)] * skip_ref[:, lanes(k)]
                )
            return tuple(new)

        gs = lax.fori_loop(0, BLK, back, gs, unroll=2)
        at = pl.ds(pl.multiple_of(i * BLK * seqs, BLK * seqs), BLK * seqs)
        d_step = (dsb[...] * sig_ref[at, :]).astype(BF16)
        dstep_ref[at, :] = d_step
        bias_ref[...] += jnp.sum(d_step.astype(F32).reshape(BLK, seqs, width), 0)
        total[at, :] += (
            jnp.dot(d_step, w_ref[...], preferred_element_type=F32)
            + jnp.dot(pb[...].astype(BF16), columns[: N * LANES], preferred_element_type=F32)
            + jnp.dot(pc[...].astype(BF16), columns[N * LANES :], preferred_element_type=F32)
        )
        return gs

    lax.fori_loop(
        0,
        length // BLK,
        block,
        tuple(g0_ref[n, :, lanes(k)] for n in range(N) for k in range(parts)),
    )

    @pl.when(group == pl.num_programs(0) - 1)
    def _():
        dproj_ref[...] = total[...].astype(BF16)


def normalized(x):
    return x * lax.rsqrt(jnp.mean(x * x, -1, keepdims=True) + EPS)


def inner_grad_step(seqs, refs, x, sums, dconv):
    (
        du_ref,
        dproj_ref,
        conv_ref,
        ext_ref,
        normed_ref,
        u_ref,
        rank_ref,
        dstep_ref,
        dgate_ref,
        w_in_ref,
        w_gate_ref,
        w_x_ref,
        taps_ref,
        after_ref,
    ) = refs
    gin_ref, narrow_ref, chan_ref, gain_ref = sums
    rows, chans = du_ref.shape
    rim = (CONV_TAPS - 1) * seqs
    turn = pl.program_id(0)
    first = pl.multiple_of((pl.num_programs(0) - 1 - turn) * rows, rows)

    @pl.when(turn == 0)
    def _():
        for ref in sums:
            ref[...] = jnp.zeros_like(ref)
        dconv[rows:, :] = after_ref[...]

    @pl.when(turn > 0)
    def _():
        dconv[rows:, :] = dconv[:rim, :]

    def by_seq(value):
        return jnp.sum(value.reshape(rows // seqs, seqs, value.shape[-1]), 0)

    d_proj = dproj_ref[...]
    conv = conv_ref[...]
    sig = jax.nn.sigmoid(conv)
    d_conv = (du_ref[...] + dot(d_proj, w_x_ref[...], NT)) * (sig * (1.0 + conv * (1.0 - sig)))
    dconv[:rows, :] = d_conv
    d_inner = jnp.zeros_like(d_conv)
    for tap in range(CONV_TAPS):
        at = (CONV_TAPS - 1 - tap) * seqs
        d_inner = d_inner + taps_ref[tap : tap + 1, :] * dconv[at : at + rows, :]
        ext = ext_ref[pl.ds(pl.multiple_of(first + tap * seqs, seqs), rows), :]
        chan_ref[tap * seqs : (tap + 1) * seqs, :] += by_seq(d_conv * ext)
    chan_ref[CONV_TAPS * seqs :, :] += by_seq(d_conv)
    d_inner = d_inner.astype(BF16)
    part = dot(d_inner, w_in_ref[...]) + dot(dgate_ref[...], w_gate_ref[...])
    gain_ref[...] += by_seq(part * normalized(x.astype(F32)))
    gin_ref[...] += dot(d_inner, normed_ref[...], TN)
    narrow = dot(u_ref[...], d_proj, TN) + dot(dstep_ref[...], rank_ref[...], TN)
    narrow_ref[...] = narrow_ref[...] + narrow
    return part


def inner_grad_kernel(seqs, *refs):
    refs, x_ref, late_ref, early_ref, sums, dconv = (
        refs[:14],
        refs[14],
        refs[15],
        refs[16],
        refs[17:21],
        refs[21],
    )
    part = inner_grad_step(seqs, refs, x_ref[...], sums, dconv).astype(BF16)
    turn, half = pl.program_id(0), pl.num_programs(0) // 2

    @pl.when(turn < half)
    def _():
        late_ref[...] = part

    @pl.when(turn >= half)
    def _():
        early_ref[...] = part


def finish_kernel(shape, sizes, turns, *refs):
    micros, group = shape
    seqs = micros * group
    step_refs, refs = refs[:14], refs[14:]
    x_ref, dres_ref, act_own_ref, act_got_ref, g_ref, vec_ref, routing_ref, early_ref = refs[:8]
    grad_ref, act_ref, in_ref, out_ref, proj_ref, step_ref, channel_ref, route_ref, tail_ref = refs[
        8:17
    ]
    refs = refs[7:]
    sums, dconv, sent, got, gain_got, tail, grad_tok, act_tok = (
        refs[10:14],
        refs[14],
        refs[15],
        refs[16],
        refs[17],
        refs[18],
        refs[19],
        refs[20],
    )
    mine_ref = refs[21]
    refs = refs[22:]
    bits = [("ctx", 1 << k) for k in range(sizes[1].bit_length() - 1)]
    bits += [("fsdp", 1 << k) for k in range(sizes[0].bit_length() - 1)]
    stages = len(bits)
    sends, gots = refs[:stages], refs[stages : 2 * stages]
    part_sems, gain_sems, sum_sems = (
        refs[2 * stages : 2 * stages + 2],
        refs[2 * stages + 2 : 2 * stages + 4],
        refs[2 * stages + 4 : 2 * stages + 6],
    )
    where = {axis: lax.axis_index(axis) for axis in ("fsdp", "ctx", "tensor")}
    across = (where["fsdp"], where["ctx"], 1 - where["tensor"])
    high = [lax.rem(where[axis] // bit, 2) for axis, bit in bits]
    partners = []
    for (axis, bit), one in zip(bits, high):
        to = dict(where)
        to[axis] = where[axis] + bit - 2 * bit * one
        partners.append((to["fsdp"], to["ctx"], to["tensor"]))

    def remote(src, dst, sems, at, to):
        return pltpu.make_async_remote_copy(
            src_ref=src,
            dst_ref=dst,
            send_sem=sems[0].at[at],
            recv_sem=sems[1].at[at],
            device_id=to,
            device_id_type=MESH,
        )

    blocks = [pl.ds(0, 1), pl.ds(1, turns - 2), pl.ds(turns - 1, 1)]

    def part_copy(which):
        at = blocks[which]
        return remote(sent.at[at], got.at[at], part_sems, which, across)

    def sum_copy(stage, half):
        source = sends[stage].at[half, 1 - high[stage]]
        return remote(source, gots[stage].at[half], sum_sems, (stage, half), partners[stage])

    turn = pl.program_id(0)

    @pl.when(turn == 0)
    def _():
        greet([across] + partners)

    rows = step_refs[0].shape[0]
    first = pl.multiple_of((turns - 1 - turn) * rows, rows)
    part = inner_grad_step(seqs, step_refs, x_ref[pl.ds(first, rows), :], sums, dconv)
    sent[turn] = part.astype(BF16)

    @pl.when(turn == 0)
    def _():
        part_copy(0).start()

    @pl.when(turn == turns - 2)
    def _():
        part_copy(0).wait_send()
        part_copy(1).start()


    def output(which):
        at = slice((turns - 1 - which) * rows, (turns - which) * rows)
        x = x_ref[at, :].astype(F32)
        width = x.shape[1]
        scale = lax.rsqrt(jnp.mean(x * x, -1, keepdims=True) + EPS)
        xhat = x * scale
        scaled = g_ref[...] * (sent[which].astype(F32) + got[which].astype(F32))
        mean = jnp.mean(scaled * xhat, -1, keepdims=True)
        grad = dres_ref[at, :].astype(F32) + scale * (scaled - xhat * mean)
        own, other = act_own_ref[at, :].astype(F32), act_got_ref[0, at, :].astype(F32)
        left = where["tensor"] == 0
        act = jnp.concatenate([jnp.where(left, own, other), jnp.where(left, other, own)], 1)
        count = rows // seqs
        times = slice((turns - 1 - which) * count, (turns - which) * count)
        for k in range(width // LANES):
            grad_tok[k] = grad[:, lanes(k)]
            act_tok[k] = act[:, lanes(k)]
        for m in range(micros):
            for g in range(group):
                every = pl.ds(m * group + g, count, stride=seqs)
                for k in range(width // LANES):
                    grad_ref[m, g, times, lanes(k)] = grad_tok[k, every, :]
                    act_ref[m, g, times, lanes(k)] = act_tok[k, every, :].astype(BF16)

    @pl.when(turn == turns - 1)
    def _():
        gin_ref, narrow_ref, chan_ref, gain_ref = sums
        gain_copy = remote(gain_ref, gain_got, gain_sems, 0, across)
        gain_copy.start()
        owned = mine_ref.shape[0]
        half_cols = mine_ref.shape[1] // 2
        rest = gin_ref.shape[1] - half_cols

        def fill(stage, half):
            count = 1 << (stages - stage)
            for k in range(count):
                target = (half, k % 2, k // 2)
                if stage > 0:
                    before = (half, high[stage - 1], k)
                    value = sends[stage - 1][before].astype(F32)
                    value = value + gots[stage - 1][half, k].astype(F32)
                    sends[stage][target] = value.astype(BF16)
                    continue
                at = slice(k * owned, (k + 1) * owned)
                if half == 0:
                    sends[0][target] = gin_ref[at, :half_cols].astype(BF16)
                else:
                    joined = [gin_ref[at, half_cols:], narrow_ref[at, :], tail[at, :]]
                    sends[0][target] = jnp.concatenate(joined, 1).astype(BF16)
            sum_copy(stage, half).start()

        fill(0, 0)
        gain_copy.wait()
        vec = vec_ref[...]
        row = lax.broadcasted_iota(jnp.int32, vec.shape, 0)
        for k in range(CONV_TAPS + 1):
            value = jnp.sum(chan_ref[k * seqs : (k + 1) * seqs, :], 0, keepdims=True)
            vec = jnp.where(row == k, value, vec)
        gain = jnp.sum(gain_ref[...] + gain_got[...], 0, keepdims=True)
        vec = jnp.where(row == VECTORS, gain, vec)
        tail[...] = vec.T + routing_ref[...]
        fill(0, 1)
        part_copy(0).wait_recv()
        output(0)
        for stage in range(1, stages):
            for half in range(2):
                sum_copy(stage - 1, half).wait_recv()
                fill(stage, half)
            if stage == 1:
                part_copy(1).wait()
                part_copy(2).start()
            if stage < turns - 1:
                output(stage)
        for which in range(stages, turns - 1):
            output(which)
        part_copy(2).wait_recv()
        output(turns - 1)
        for half in range(2):
            sum_copy(stages - 1, half).wait_recv()
            value = sends[stages - 1][half, high[stages - 1], 0].astype(F32)
            mine_ref[:, half * half_cols : (half + 1) * half_cols] = value + gots[stages - 1][
                half, 0
            ].astype(F32)
        width, cols = in_ref.shape[2], proj_ref.shape[1]
        in_ref[0] = mine_ref[:, :width]
        in_ref[1] = early_ref[:, :width].astype(F32)
        out_ref[...] = early_ref[:, width:].astype(F32)
        proj_ref[...] = mine_ref[:, width : width + cols]
        step_ref[...] = mine_ref[:, width + cols : width + cols + R]
        at = width + LANES
        channel_ref[...] = mine_ref[:, at : at + VECTORS - 1]
        at += VECTORS + 1
        route_ref[...] = mine_ref[:, at : at + route_ref.shape[1]]
        tail_ref[...] = mine_ref[:, width + LANES :]
        for stage in range(stages):
            for half in range(2):
                sum_copy(stage, half).wait_send()
        part_copy(2).wait_send()


def output_kernel(shape, peers, *refs):
    micros, group = shape
    early, late, refs = refs[:peers], refs[peers : 2 * peers], refs[2 * peers :]
    x_ref, dres_ref, act_own_ref, act_others_ref, gain_ref, grad_ref, act_ref, grad_tok, act_tok = refs
    x = x_ref[...].astype(F32)
    scale = lax.rsqrt(jnp.mean(x * x, -1, keepdims=True) + EPS)
    xhat = x * scale
    is_early = pl.program_id(0) < pl.num_programs(0) // 2
    d_normed = jnp.zeros_like(x)
    for first, second in zip(early, late):
        d_normed = d_normed + jnp.where(is_early, first[...], second[...]).astype(F32)
    scaled = gain_ref[...] * d_normed
    mean = jnp.mean(scaled * xhat, -1, keepdims=True)
    grad = dres_ref[...].astype(F32) + scale * (scaled - xhat * mean)
    seqs = micros * group
    rows, width = x.shape
    count = rows // seqs
    tensor = lax.axis_index("tensor")
    pieces = []
    for owner in range(peers):
        piece = act_own_ref[...].astype(F32)
        for by in range(1, peers):
            here = lax.rem(tensor + peers - by, peers) == owner
            piece = jnp.where(here, act_others_ref[by - 1].astype(F32), piece)
        pieces.append(piece)
    act = jnp.concatenate(pieces, 1)
    for k in range(width // LANES):
        grad_tok[k] = grad[:, lanes(k)]
        act_tok[k] = act[:, lanes(k)]
    for m in range(micros):
        for g in range(group):
            at = pl.ds(m * group + g, count, stride=seqs)
            for k in range(width // LANES):
                grad_ref[m, g, :, lanes(k)] = grad_tok[k, at, :]
                act_ref[m, g, :, lanes(k)] = act_tok[k, at, :].astype(BF16)


def scan_call(kernel, arrays, outs, scratch, width, chans, chunk=0, cost=None):
    def spec(shape, kind):
        def place(j, rank=len(shape)):
            at = [0] * rank
            if "t" in kind:
                at[0] = chunk
            if "c" in kind:
                at[-1] = j
            if "r" in kind:
                at[0] = j
            return tuple(at)

        return pl.BlockSpec(shape, place)

    return pl.pallas_call(
        kernel,
        grid=(chans // width,),
        in_specs=[spec(shape, kind) for _, shape, kind in arrays],
        out_specs=[spec(shape, kind) for _, shape, kind in outs],
        out_shape=[a for a, _, _ in outs],
        scratch_shapes=[
            s if not isinstance(s, tuple) else pltpu.VMEM(s, F32) for s in scratch
        ],
        compiler_params=pltpu.CompilerParams(vmem_limit_bytes=62 << 20),
        cost_estimate=cost,
    )(*[a for a, _, _ in arrays])


def per_device(
    inputs,
    out_grad,
    lengths,
    routes,
    slots,
    norm_gains,
    router_matrix,
    input_projection,
    inner_projection,
    step_projection,
    step_bias,
    channel_params,
    output_projection,
    expert_up,
    expert_down,
):
    micros, group, length, width = inputs.shape
    seqs = micros * group
    tokens = length * seqs
    owners = lax.axis_size("fsdp") * lax.axis_size("ctx")
    experts = router_matrix.shape[1]
    capacity = max(2, (25 * group * length + 32 * experts - 1) // (32 * experts))
    slots_each = micros * capacity
    rows = experts * slots_each

    def by_token(value):
        return jnp.moveaxis(value, 2, 0).reshape(tokens, *value.shape[3:])

    narrow = jnp.concatenate(
        [inner_projection, step_projection, channel_params, step_bias[:, None]], 1
    )
    x_cols = inner_projection.shape[1]
    cuts = [x_cols, x_cols + R, x_cols + R + channel_params.shape[1]]
    routing = jnp.concatenate([router_matrix, norm_gains.T], 1)
    joined = narrow.shape[0] == routing.shape[0]
    if joined:
        narrow = jnp.concatenate([narrow, routing], 1)
    narrow_cols = narrow.shape[1]
    pad = -narrow_cols % LANES
    first = jnp.concatenate([input_projection[0], jnp.pad(narrow, ((0, 0), (0, pad)))], 1)
    later = jnp.concatenate([input_projection[1], output_projection], 1)
    full = lax.all_gather(first, OWNERS, axis=0, tiled=True)
    later_full = lax.all_gather(later, OWNERS, axis=0, tiled=True)

    position = lax.axis_index("ctx") * length + jnp.arange(length)
    valid = (position[:, None] < lengths.reshape(1, seqs)).astype(F32).reshape(tokens, 1)
    route = by_token(routes)
    slot = by_token(slots)
    kept = slot >= 0
    kept_f = kept.astype(F32)
    micro_of = (jnp.arange(tokens) // group) % micros
    place = jnp.where(kept, route * slots_each + micro_of * capacity + slot, -1)
    pick = (
        jnp.arange(rows).reshape(experts, slots_each, 1) == place[None, None, :]
    ).astype(BF16)
    grad_tok = by_token(out_grad)
    grad_act = grad_tok.astype(F32) * valid

    def packed(value):
        return jnp.einsum("est,td->esd", pick, value, preferred_element_type=F32).astype(BF16)

    def unpacked(value):
        flat = value.reshape(rows, value.shape[-1])
        return lax.optimization_barrier(dot(pick.reshape(rows, tokens), flat, TN))

    def swap_owners(value):
        return lax.all_to_all(value, OWNERS, split_axis=0, concat_axis=0, tiled=True)

    full, grad_packed = lax.optimization_barrier((full, packed(grad_tok)))
    grad_rows_raw = swap_owners(grad_packed)

    w_in = full[:, :width]
    tail = full[:, width:]
    w_gate, w_out = later_full[:, :width], later_full[:, width:]
    w_x = tail[:, : cuts[0]]
    w_step = tail[:, cuts[0] : cuts[1]]
    channel_f = tail[:, cuts[1] : cuts[2]].astype(F32)
    bias_f = tail[:, cuts[2]].astype(F32)
    if joined:
        full_routing = tail[:, cuts[2] + 1 : cuts[2] + 1 + routing.shape[1]]
    else:
        full_routing = lax.all_gather(routing, OWNERS, axis=0, tiled=True)
    w_router = full_routing[:, :experts]
    gains = full_routing[:, experts:].T.astype(F32)
    chans = channel_f.shape[0]
    taps = channel_f[:, :CONV_TAPS].T
    conv_bias = channel_f[:, CONV_TAPS]
    skip = channel_f[:, CONV_TAPS + 1]
    rates = -jnp.exp(channel_f[:, CONV_TAPS + 2 :]).T

    x_tok = lax.optimization_barrier(by_token(inputs))
    x = x_tok.astype(F32)
    normed1 = (normalized(x) * gains[0]).astype(BF16)
    inner = dot(normed1, w_in, NT).astype(BF16)
    rim = (CONV_TAPS - 1) * seqs
    before = moved(inner[tokens - rim :], 1)
    gate_z = dot(normed1, w_gate, NT)
    extended = jnp.concatenate([before, inner], 0).astype(F32)
    conv = conv_bias
    for tap in range(CONV_TAPS):
        conv = conv + taps[tap] * extended[tap * seqs : tap * seqs + tokens]
    u = jax.nn.silu(conv).astype(BF16)
    u_wide = u.astype(F32)
    proj = tensor_total(dot(u, w_x), BF16)
    rank = proj[:, :R].astype(BF16)
    b_vals = proj[:, R : R + N]
    c_vals = proj[:, R + N :]
    step_pre = dot(rank, w_step, NT) + bias_f
    delta = jax.nn.softplus(step_pre)
    lane_width = 2 * LANES if chans % (2 * LANES) == 0 else LANES
    wide_rates = (N, seqs, lane_width)
    state_block = (N, seqs, lane_width)
    call = functools.partial(scan_call, width=lane_width, chans=chans)

    def both_in(value, steps=length):
        return (value, (steps * seqs, lane_width), "tc")

    def by_chan(value):
        return (value, (*value.shape[:-1], lane_width), "c")

    def by_rows(value, steps=length):
        return (value, (steps * seqs, value.shape[1]), "t")

    def cost(steps, ops):
        elements = steps * seqs * chans * N
        return pl.CostEstimate(flops=300 * ops * elements, bytes_accessed=elements, transcendentals=0)

    def out(shape, dtype=F32):
        return jax.ShapeDtypeStruct(shape, dtype)

    [end] = call(
        end_state_kernel,
        [both_in(delta), both_in(u_wide), by_rows(b_vals), by_chan(rates)],
        [by_chan(out((N + 1, seqs, chans)))],
        [wide_rates, (tokens, N * LANES)],
        cost=cost(length, 6),
    )
    end, grad_rows_raw = lax.optimization_barrier((end, grad_rows_raw))
    log_decay = end[N]
    state = carried(end, log_decay, rates, 1, 0)
    pieces = 4 if length % (4 * BLK) == 0 else 1
    steps = length // pieces
    block = steps * seqs
    groups = chans // lane_width
    peers, here = lax.axis_size("tensor"), lax.axis_index("tensor")

    def cut(value, *shape):
        return value, pl.BlockSpec(shape, lambda p, j: (p, j))

    def by_piece(value):
        return value, pl.BlockSpec((block, value.shape[1]), lambda p, j: (p, 0))

    def by_group(value):
        rank = value.ndim - 1
        return value, pl.BlockSpec(
            (*value.shape[:-1], lane_width), lambda p, j: (0,) * rank + (j,)
        )

    arrays = [
        cut(delta, block, lane_width),
        cut(u_wide, block, lane_width),
        cut(gate_z, block, lane_width),
        by_piece(b_vals),
        by_piece(c_vals),
        by_group(rates),
        by_group(skip[None]),
        (w_out, pl.BlockSpec((lane_width, width), lambda p, j: (j, 0))),
        by_group(state),
        (x_tok, pl.BlockSpec((tokens, width), lambda p, j: (0, 0))),
    ]
    results = [
        cut(out((tokens, chans)), block, lane_width),
        cut(out((tokens, chans), BF16), block, lane_width),
        (
            out((length // BLK, N, seqs, chans)),
            pl.BlockSpec((steps // BLK, N, seqs, lane_width), lambda p, j: (p, 0, 0, j)),
        ),
        (out((tokens, width)), pl.BlockSpec((tokens, width), lambda p, j: (0, 0))),
    ]
    y_vals, gated, starts, resid = pl.pallas_call(
        functools.partial(forward_kernel, peers),
        grid=(pieces, groups),
        in_specs=[spec for _, spec in arrays],
        out_specs=[spec for _, spec in results],
        out_shape=[value for value, _ in results],
        scratch_shapes=[
            pltpu.VMEM(wide_rates, F32),
            pltpu.VMEM((block, N * LANES), F32),
            pltpu.VMEM((block, N * LANES), F32),
            pltpu.VMEM((groups, *state_block), F32),
            pltpu.VMEM((block, width), F32),
            pltpu.VMEM((pieces, block, width), BF16),
            pltpu.VMEM((peers - 1, pieces, block, width), BF16),
            pltpu.SemaphoreType.DMA((peers - 1, pieces)),
            pltpu.SemaphoreType.DMA((peers - 1, pieces)),
        ],
        compiler_params=pltpu.CompilerParams(
            collective_id=2, has_side_effects=True, vmem_limit_bytes=62 << 20
        ),
        cost_estimate=cost(length, 10),
    )(*[value for value, _ in arrays])
    silu_z, gate_slope = silu_parts(gate_z)

    scale2 = lax.rsqrt(jnp.mean(resid * resid, -1, keepdims=True) + EPS)
    xhat2 = resid * scale2
    normed2 = (xhat2 * gains[1]).astype(BF16)
    probs = jax.nn.softmax(dot(normed2, w_router), -1)
    onehot = (route[:, None] == jnp.arange(experts)).astype(F32)
    gate = jnp.sum(probs * onehot, -1, keepdims=True) * kept_f[:, None]
    share = width // peers

    def half(value):
        cut = value[..., :share]
        for peer in range(1, peers):
            cut = jnp.where(here == peer, value[..., peer * share : (peer + 1) * share], cut)
        return cut

    x_rows = tensor_columns(swap_owners(packed(half(normed2))))
    gate_rows = swap_owners(
        jnp.sum(jnp.where(pick > 0, gate[:, 0], 0.0), -1)[:, None, :]
    )
    grad_rows = (jnp.swapaxes(gate_rows, 1, 2) * grad_rows_raw.astype(F32)).astype(BF16)
    up, down = expert_up[0], expert_down[0]

    def product(a, b, terms):
        return jnp.einsum(terms, a, b, preferred_element_type=F32)

    def halves(matrix, axis):
        low, high = jnp.split(matrix, 2, axis)
        return jnp.where(here == 0, low, high), jnp.where(here == 0, high, low)

    def scattered(value):
        return lax.psum_scatter(value, "tensor", scatter_dimension=2, tiled=True).astype(BF16)

    hidden = product(x_rows, up, "srd,df->srf")
    act_float, gelu_pull = jax.vjp(lambda v: jax.nn.gelu(v, approximate=True), hidden)
    act = act_float.astype(BF16)
    d_act = product(grad_rows, down, "srd,fd->srf")
    d_hidden = gelu_pull(d_act)[0].astype(BF16)
    q_rows = jnp.sum(act.astype(F32) * d_act, -1)
    if peers == 2:
        up_own, up_other = halves(up, 0)
        down_own, down_other = halves(down, 1)
        x_sent = product(d_hidden, up_other, "srf,df->srd").astype(BF16)
        x_got = swapped(x_sent)
        act_late, _ = lax.optimization_barrier((act, x_sent))
        x_own = product(d_hidden, up_own, "srf,df->srd")
        y_sent = product(act_late, down_other, "srf,fd->srd").astype(BF16)
        x_got, y_sent = lax.optimization_barrier((x_got, y_sent))
        back_x = swap_owners((x_own + x_got.astype(F32)).astype(BF16))
        y_got = swapped(y_sent)
        y_own = product(act_late, down_own, "srf,fd->srd")
        share_y = (y_own + y_got.astype(F32)).astype(BF16)
    else:
        back_x = swap_owners(scattered(product(d_hidden, up, "srf,df->srd")))
        share_y = scattered(product(act, down, "srf,fd->srd"))
    q_back = swap_owners(q_rows[:, None, :])
    grad_up = product(x_rows, d_hidden, "srd,srf->df")
    grad_down = product(act, grad_rows, "srf,srd->fd")
    back_x, grad_up, grad_down, share_y = lax.optimization_barrier(
        (back_x, grad_up, grad_down, share_y)
    )
    expert_dx = unpacked(back_x)
    q_part = jnp.sum(jnp.where(pick > 0, q_back[:, 0, :, None], 0.0), (0, 1))
    x_half = half(xhat2)
    gain_half = half(gains[1])
    grad_half = half(grad_act)
    router_half = half(w_router.T)
    sums = jnp.stack([q_part, jnp.sum(gain_half * expert_dx * x_half, -1)])
    sums = tensor_total(sums, F32)
    d_logits = (sums[0][:, None] * (onehot - probs)).astype(BF16)
    grad_router = dot(normed2, d_logits, TN)
    by_router = dot((xhat2 * gains[1]).astype(BF16), w_router)
    mean_term = (
        sums[1][:, None] + jnp.sum(d_logits.astype(F32) * by_router, -1, keepdims=True)
    ) / width
    d_normed2 = expert_dx + dot(d_logits, router_half)
    gain_grad2 = tensor_columns(jnp.sum(d_normed2 * x_half, 0, keepdims=True))[0]
    d_resid_half = grad_half + scale2 * (gain_half * d_normed2 - x_half * mean_term)

    d_mixed = tensor_columns(d_resid_half.astype(BF16))
    d_mixed, share_y = lax.optimization_barrier((d_mixed, share_y))
    expert_y = unpacked(swap_owners(share_y))
    act_half = (valid * (half(resid) + gate * expert_y)).astype(BF16)
    d_gated = dot(d_mixed, w_out, NT)
    d_y = d_gated * silu_z
    [start_grad] = call(
        start_grad_kernel,
        [both_in(delta), both_in(d_y), by_rows(c_vals), by_chan(rates)],
        [by_chan(out((N, seqs, chans)))],
        [wide_rates, (tokens, N * LANES)],
        cost=cost(length, 6),
    )
    d_gate_z = (d_gated * y_vals * gate_slope).astype(BF16)

    def owned(value):
        return lax.psum_scatter(value.astype(BF16), OWNERS, scatter_dimension=0, tiled=True)

    grad_end, act_others, early = carried(
        start_grad, log_decay, rates, -1, 1, act_half, (d_gate_z, normed1, gated, d_mixed)
    )
    mine_early = owned(early)
    w_step_wide = jnp.pad(w_step, ((0, 0), (0, LANES - R)))
    d_step, du_part, d_proj_part, rate_grad, bias_sums, skip_sums = call(
        backward_kernel,
        [
            both_in(delta),
            both_in(u_wide),
            both_in(d_y),
            (jax.nn.sigmoid(step_pre), (tokens, lane_width), "tc"),
            by_rows(b_vals),
            by_rows(c_vals),
            by_chan(rates),
            by_chan(skip[None]),
            (w_step_wide, (lane_width, LANES), "r"),
            by_chan(starts),
            by_chan(grad_end),
        ],
        [
            by_chan(out((tokens, chans), BF16)),
            by_chan(out((tokens, chans))),
            (out((tokens, LANES), BF16), (tokens, LANES), ""),
            by_chan(out((N, seqs, chans))),
            by_chan(out((seqs, chans))),
            by_chan(out((seqs, chans))),
        ],
        [
            wide_rates,
            (tokens, N * LANES),
            (tokens, N * LANES),
            (BLK + 1, N, seqs, lane_width),
            (BLK, N, seqs, lane_width),
            (BLK * seqs, N * LANES),
            (BLK * seqs, N * LANES),
            (BLK * seqs, lane_width),
            (tokens, LANES),
            pltpu.VMEM((2 * N * LANES, LANES), BF16),
        ],
        cost=cost(length, 24),
    )
    d_proj = tensor_total(d_proj_part, BF16).astype(BF16)
    step_bias_grad = jnp.sum(bias_sums, 0)
    skip_grad = jnp.sum(skip_sums, 0)
    w_x_wide = jnp.pad(w_x, ((0, 0), (0, LANES - x_cols)))
    rim_u = du_part[:rim] + dot(d_proj[:rim], w_x_wide, NT)
    after = moved(rim_u * silu_parts(conv[:rim])[1], -1)
    steps = length // 4
    block = steps * seqs
    turns = length // steps

    def from_end(value):
        return value, pl.BlockSpec((block, value.shape[1]), lambda i: (turns - 1 - i, 0))

    def whole(value):
        return value, pl.BlockSpec(value.shape, lambda i: (0, 0))

    arrays = [
        from_end(du_part),
        from_end(d_proj),
        from_end(conv),
        whole(extended),
        from_end(normed1),
        from_end(u),
        from_end(jnp.pad(rank, ((0, 0), (x_cols, LANES - x_cols - R)))),
        from_end(d_step),
        from_end(d_gate_z),
        whole(w_in),
        whole(w_gate),
        whole(w_x_wide),
        whole(taps),
        whole(after),
    ]
    rows_each = narrow.shape[0]
    decay_grad = jnp.sum(rate_grad, 1) * rates
    fused = joined and peers == 2 and rows_each % 16 == 0 and owners >= 4 and VECTORS + 2 + experts <= LANES
    if fused:
        vectors = jnp.concatenate([skip_grad[None], decay_grad, step_bias_grad[None]], 0)
        vectors = jnp.pad(vectors, ((CONV_TAPS + 1, LANES - VECTORS), (0, 0)))
        routing_wide = jnp.pad(
            jnp.concatenate([grad_router, gain_grad2[:, None]], 1),
            ((0, 0), (VECTORS + 1, LANES - VECTORS - 2 - experts)),
        )

        def entire(value):
            return value, pl.BlockSpec(value.shape, lambda i: (0,) * value.ndim)

        arrays += [
            whole(x_tok),
            whole(d_mixed),
            whole(act_half),
            entire(act_others),
            whole(gains[:1]),
            whole(vectors),
            whole(routing_wide),
            whole(mine_early),
        ]
        cols = width + 2 * LANES
        results = [
            entire(out(inputs.shape)),
            entire(out(inputs.shape, BF16)),
            entire(out((2, rows_each, width))),
            *[
                whole(out((rows_each, count)))
                for count in (width, x_cols, R, VECTORS - 1, experts, LANES)
            ],
        ]
        sizes = (lax.axis_size("fsdp"), lax.axis_size("ctx"))
        stages = (owners - 1).bit_length()
        counts = [owners >> (stage + 1) for stage in range(stages)]
        (
            input_grad,
            activations,
            mine_in,
            mine_out,
            mine_x,
            mine_dt,
            mine_channel,
            mine_router,
            mine_tail,
        ) = pl.pallas_call(
            functools.partial(finish_kernel, (micros, group), sizes, turns),
            grid=(turns,),
            in_specs=[spec for _, spec in arrays],
            out_specs=[spec for _, spec in results],
            out_shape=[value for value, _ in results],
            scratch_shapes=[
                pltpu.VMEM((chans, width), F32),
                pltpu.VMEM((chans, LANES), F32),
                pltpu.VMEM(((CONV_TAPS + 1) * seqs, chans), F32),
                pltpu.VMEM((seqs, width), F32),
                pltpu.VMEM((block + rim, chans), F32),
                pltpu.VMEM((turns, block, width), BF16),
                pltpu.VMEM((turns, block, width), BF16),
                pltpu.VMEM((seqs, width), F32),
                pltpu.VMEM((chans, LANES), F32),
                pltpu.VMEM((width // LANES, block, LANES), F32),
                pltpu.VMEM((width // LANES, block, LANES), F32),
                pltpu.VMEM((rows_each, cols), F32),
                *[pltpu.VMEM((2, 2, count, rows_each, cols // 2), BF16) for count in counts],
                *[pltpu.VMEM((2, count, rows_each, cols // 2), BF16) for count in counts],
                pltpu.SemaphoreType.DMA((3,)),
                pltpu.SemaphoreType.DMA((3,)),
                pltpu.SemaphoreType.DMA((1,)),
                pltpu.SemaphoreType.DMA((1,)),
                pltpu.SemaphoreType.DMA((stages, 2)),
                pltpu.SemaphoreType.DMA((stages, 2)),
            ],
            compiler_params=pltpu.CompilerParams(
                collective_id=3, has_side_effects=True, vmem_limit_bytes=63 << 20
            ),
        )(*[value for value, _ in arrays])
        mine_bias = mine_tail[:, VECTORS - 1]
        gains_out = jnp.stack([mine_tail[:, VECTORS], mine_tail[:, VECTORS + 1 + experts]])
        return (
            activations,
            input_grad,
            gains_out,
            mine_router,
            mine_in,
            mine_x,
            mine_dt,
            mine_bias,
            mine_channel,
            mine_out,
            grad_up[None],
            grad_down[None],
        )
    arrays.append(from_end(x_tok))
    results = [
        (
            out((tokens // 2, width), BF16),
            pl.BlockSpec((block, width), lambda i: (jnp.maximum(turns // 2 - 1 - i, 0), 0)),
        ),
        (
            out((tokens // 2, width), BF16),
            pl.BlockSpec(
                (block, width), lambda i: (jnp.minimum(turns - 1 - i, turns // 2 - 1), 0)
            ),
        ),
        whole(out((chans, width))),
        whole(out((chans, LANES))),
        whole(out(((CONV_TAPS + 1) * seqs, chans))),
        whole(out((seqs, width))),
    ]
    late_part, early_part, grad_in, narrow_sums, conv_sums, gain_sums = pl.pallas_call(
        functools.partial(inner_grad_kernel, seqs),
        grid=(turns,),
        in_specs=[spec for _, spec in arrays],
        out_specs=[spec for _, spec in results],
        out_shape=[value for value, _ in results],
        scratch_shapes=[pltpu.VMEM((block + rim, chans), F32)],
        compiler_params=pltpu.CompilerParams(vmem_limit_bytes=62 << 20),
    )(*[value for value, _ in arrays])
    late_part, mine_early = lax.optimization_barrier((late_part, mine_early))
    grad_xproj, grad_dt = narrow_sums[:, :x_cols], narrow_sums[:, x_cols : x_cols + R]
    conv_sums = jnp.sum(conv_sums.reshape(CONV_TAPS + 1, seqs, chans), 1)
    gain_grad1 = jnp.sum(gain_sums, 0)

    narrow_grads = jnp.concatenate(
        [
            grad_xproj,
            grad_dt,
            conv_sums.T,
            skip_grad[:, None],
            decay_grad.T,
            step_bias_grad[:, None],
        ],
        1,
    )
    routing_grads = jnp.concatenate([grad_router, gain_grad1[:, None], gain_grad2[:, None]], 1)
    if joined:
        narrow_grads = jnp.concatenate([narrow_grads, routing_grads], 1)
    wide_grads = jnp.concatenate(
        [grad_in, jnp.pad(narrow_grads, ((0, 0), (0, pad)))], 1
    )

    halves = [late_part, early_part]
    if peers == 2:
        exchanged = [swapped(part) for part in halves]
    else:
        exchanged = [lax.all_gather(part, "tensor") for part in halves]
    mine, exchanged = halved(wide_grads, exchanged)
    normed_parts = []
    for own, others in zip(halves, exchanged):
        if peers == 2:
            normed_parts.append([own, others])
        else:
            normed_parts.append([others[k] for k in range(peers)])
    late_parts, early_parts = normed_parts

    def rows_of(value):
        return value, pl.BlockSpec((block, value.shape[1]), lambda i: (i, 0))

    def early_rows(value):
        return value, pl.BlockSpec((block, width), lambda i: (jnp.minimum(i, turns // 2 - 1), 0))

    def late_rows(value):
        return value, pl.BlockSpec((block, width), lambda i: (jnp.maximum(i - turns // 2, 0), 0))

    arrays = (
        [early_rows(part) for part in early_parts]
        + [late_rows(part) for part in late_parts]
        + [
            rows_of(x_tok),
            rows_of(d_mixed),
            rows_of(act_half),
            (act_others, pl.BlockSpec((peers - 1, block, share), lambda i: (0, i, 0))),
            whole(gains[:1]),
        ]
    )
    out_spec = pl.BlockSpec((micros, group, steps, width), lambda i: (0, 0, i, 0))
    input_grad, activations = pl.pallas_call(
        functools.partial(output_kernel, (micros, group), peers),
        grid=(turns,),
        in_specs=[spec for _, spec in arrays],
        out_specs=[out_spec, out_spec],
        out_shape=[out(inputs.shape), out(inputs.shape, BF16)],
        scratch_shapes=[pltpu.VMEM((width // LANES, block, LANES), F32)] * 2,
        compiler_params=pltpu.CompilerParams(vmem_limit_bytes=62 << 20),
    )(*[value for value, _ in arrays])
    mine_tail = mine[:, width:]
    if joined:
        mine_routing = mine_tail[:, cuts[2] + 1 : cuts[2] + 1 + routing.shape[1]]
    else:
        mine_routing, _ = halved(routing_grads)
    gains_out = jnp.stack(
        [tensor_total(mine_routing[None, :, experts], F32)[0], mine_routing[:, experts + 1]]
    )
    return (
        activations,
        input_grad,
        gains_out,
        mine_routing[:, :experts],
        jnp.stack([mine[:, :width], mine_early[:, :width].astype(F32)]),
        mine_tail[:, : cuts[0]],
        mine_tail[:, cuts[0] : cuts[1]],
        mine_tail[:, cuts[2]],
        mine_tail[:, cuts[1] : cuts[2]],
        mine_early[:, width:].astype(F32),
        grad_up[None],
        grad_down[None],
    )


def solution(mesh):
    return jax.shard_map(
        per_device,
        mesh=mesh,
        in_specs=(
            P(None, "fsdp", "ctx", None),
            P(None, "fsdp", "ctx", None),
            P(None, "fsdp"),
            P(None, "fsdp", "ctx"),
            P(None, "fsdp", "ctx"),
            P(None, ("fsdp", "ctx")),
            P(("fsdp", "ctx"), None),
            P(None, ("fsdp", "ctx", "tensor"), None),
            P(("fsdp", "ctx", "tensor"), None),
            P(("fsdp", "ctx", "tensor"), None),
            P(("fsdp", "ctx", "tensor")),
            P(("fsdp", "ctx", "tensor"), None),
            P(("fsdp", "ctx", "tensor"), None),
            P(("fsdp", "ctx"), None, "tensor"),
            P(("fsdp", "ctx"), "tensor", None),
        ),
        out_specs=(
            P(None, "fsdp", "ctx", None),
            P(None, "fsdp", "ctx", None),
            P(None, ("fsdp", "ctx")),
            P(("fsdp", "ctx"), None),
            P(None, ("fsdp", "ctx", "tensor"), None),
            P(("fsdp", "ctx", "tensor"), None),
            P(("fsdp", "ctx", "tensor"), None),
            P(("fsdp", "ctx", "tensor")),
            P(("fsdp", "ctx", "tensor"), None),
            P(("fsdp", "ctx", "tensor"), None),
            P(("fsdp", "ctx"), None, "tensor"),
            P(("fsdp", "ctx"), "tensor", None),
        ),
        check_vma=False,
    )
```

```python
import functools

import jax
import jax.numpy as jnp
from jax import lax
from jax.experimental import pallas as pl
from jax.experimental.pallas import tpu as pltpu
from jax.sharding import PartitionSpec as P

N = 16
CONV_TAPS = 4
R = 48
EPS = 1e-05
VECTORS = CONV_TAPS + 2 + N + 1
BLK = 8
LANES = 128
F32 = jnp.float32
BF16 = jnp.bfloat16
OWNERS = ("fsdp", "ctx")


def silu_parts(value):
    sig = jax.nn.sigmoid(value)
    return value * sig, sig * (1.0 + value * (1.0 - sig))


def swapped(value):
    return lax.ppermute(value, "tensor", [(0, 1), (1, 0)])


def tensor_total(value, dtype):
    sent = value.astype(dtype)
    if lax.axis_size("tensor") == 2:
        return sent.astype(F32) + swapped(sent).astype(F32)
    return jnp.sum(lax.all_gather(sent, "tensor").astype(F32), axis=0)


def tensor_columns(value):
    if lax.axis_size("tensor") == 2:
        other = swapped(value)
        first = lax.axis_index("tensor") == 0
        return jnp.concatenate(
            [jnp.where(first, value, other), jnp.where(first, other, value)], -1
        )
    return lax.all_gather(value, "tensor", axis=value.ndim - 1, tiled=True)


def halved(value, beside=()):
    beside = list(beside)
    sizes = [lax.axis_size(axis) for axis in OWNERS]
    bits = [(axis, 1 << k) for axis, size in zip(OWNERS, sizes) for k in reversed(range(size.bit_length() - 1))]
    rows = value.shape[0] >> len(bits)
    for place in reversed(range(len(bits))):
        axis, bit = bits[place]
        view = value.reshape(1 << place, 2, rows, value.shape[-1])
        high = (lax.axis_index(axis) & bit) != 0
        own = jnp.where(high, view[:, 1], view[:, 0])
        other = jnp.where(high, view[:, 0], view[:, 1]).astype(BF16)
        got = lax.ppermute(other, axis, [(i, i ^ bit) for i in range(lax.axis_size(axis))])
        value = own.astype(F32) + got.astype(F32)
        turn = len(bits) - 1 - place
        if 0 < turn <= len(beside):
            turn -= 1
            value, beside[turn] = lax.optimization_barrier((value, beside[turn]))
    return value.reshape(rows, value.shape[-1]), beside


def moved(value, by):
    peers = lax.axis_size("ctx")
    pairs = [(i, i + by) for i in range(peers) if 0 <= i + by < peers]
    return lax.ppermute(value, "ctx", pairs)


TN = (((0,), (0,)), ((), ()))
NT = (((1,), (1,)), ((), ()))
NN = (((1,), (0,)), ((), ()))


def dot(a, b, dims=NN):
    return lax.dot_general(a, b, dims, preferred_element_type=F32)


MESH = pl.DeviceIdType.MESH


def greet(peers):
    barrier = pltpu.get_barrier_semaphore()
    for peer in peers:
        pl.semaphore_signal(barrier, inc=1, device_id=peer, device_id_type=MESH)
    pl.semaphore_wait(barrier, len(peers))


def carry_kernel(sign, ranges, peers, end_ref, log_ref, r_ref, *refs):
    if peers:
        own_ref, left_refs, right_refs = refs[0], refs[1:5:2], refs[2:5:2]
        out_ref, others_ref, products_ref = refs[5:8]
        sent, got, log_out, send_sem, recv_sem, own_sem, others_sem = refs[8:]
    else:
        out_ref, sent, got, log_out, send_sem, recv_sem = refs
    turns, groups, _, width = sent.shape
    seqs = log_ref.shape[0]
    fsdp, me, tensor = lax.axis_index("fsdp"), lax.axis_index("ctx"), lax.axis_index("tensor")

    def peer(by):
        return (fsdp, lax.rem(me + by + ranges, ranges), tensor)

    shifts = [sign * (1 << turn) for turn in range(turns)]
    partners = [(fsdp, me, lax.rem(tensor + by, peers)) for by in range(1, peers)]
    near = sorted({s % ranges for s in shifts} | {-s % ranges for s in shifts})
    greet([peer(by) for by in near] + partners)
    beside = [
        pltpu.make_async_remote_copy(
            src_ref=own_ref,
            dst_ref=others_ref.at[k],
            send_sem=own_sem.at[k],
            recv_sem=others_sem.at[k],
            device_id=partner,
            device_id_type=MESH,
        )
        for k, partner in enumerate(partners)
    ]
    for extra in beside:
        extra.start()

    def copy(turn, group):
        return pltpu.make_async_remote_copy(
            src_ref=sent.at[turn, group],
            dst_ref=got.at[turn, group],
            send_sem=send_sem.at[turn, group],
            recv_sem=recv_sem.at[turn, group],
            device_id=peer(shifts[turn]),
            device_id_type=MESH,
        )

    def decayed(log, cols, n):
        return jnp.exp(log * r_ref[n : n + 1, cols])

    def receive(turn, group):
        copy(turn, group).wait_recv()
        cols = slice(group * width, (group + 1) * width)
        reach = 1 << turn
        real = (me >= reach) if sign > 0 else (me < ranges - reach)

        def part(k):
            rows = got[turn, group, k * seqs : (k + 1) * seqs, :].astype(F32)
            return jnp.where(real, rows, 0.0)

        log = part(N) + part(N + 1)
        if turn == 0:
            for n in range(N):
                out_ref[n, :, cols] = part(n)
            log_out[:, cols] = log
        else:
            late = log_out[:, cols]
            for n in range(N):
                out_ref[n, :, cols] = out_ref[n, :, cols] + decayed(late, cols, n) * part(n)
            log_out[:, cols] = late + log

    def multiply(k):
        left, right = left_refs[k], right_refs[k]
        count = right.shape[1]

        def product(i, _):
            at = pl.ds(pl.multiple_of(i * LANES, LANES), LANES)
            value = dot(left[:, at], right[...], TN)
            products_ref[at, k * count : (k + 1) * count] = value.astype(BF16)
            return 0

        lax.fori_loop(0, left.shape[1] // LANES, product, 0)

    for turn in range(turns):
        if turn == turns - 1 and peers:
            multiply(0)
        for group in range(groups):
            cols = slice(group * width, (group + 1) * width)
            own_log = log_ref[:, cols]
            if turn > 0:
                receive(turn - 1, group)
            for n in range(0, N, 2):
                pair = []
                for k in (n, n + 1):
                    value = end_ref[k, :, cols]
                    if turn > 0:
                        value = value + decayed(own_log, cols, k) * out_ref[k, :, cols]
                    pair.append(value)
                sent[turn, group, n * seqs : (n + 2) * seqs, :] = jnp.concatenate(pair, 0).astype(
                    BF16
                )
            log = own_log if turn == 0 else own_log + log_out[:, cols]
            high = log.astype(BF16).astype(F32)
            sent[turn, group, N * seqs :, :] = jnp.concatenate([high, log - high], 0).astype(BF16)
            copy(turn, group).start()
    if peers:
        multiply(1)
    for group in range(groups):
        receive(turns - 1, group)
    for turn in range(turns):
        for group in range(groups):
            copy(turn, group).wait_send()
    for extra in beside:
        extra.wait()


def carried(end, log_decay, rates, sign, ident, shared=None, factors=()):
    _, seqs, chans = end.shape
    ranges = lax.axis_size("ctx")
    turns = (ranges - 1).bit_length()
    groups = 3 if chans % (3 * LANES) == 0 else 1
    block = (turns, groups, (N + 2) * seqs, chans // groups)
    vmem = pl.BlockSpec(memory_space=pltpu.VMEM)
    anywhere = pl.BlockSpec(memory_space=pl.ANY)
    peers = 0 if shared is None else lax.axis_size("tensor")
    state = jax.ShapeDtypeStruct((N, seqs, chans), F32)
    scratch = [
        pltpu.VMEM(block, BF16),
        pltpu.VMEM(block, BF16),
        pltpu.VMEM((seqs, chans), F32),
        pltpu.SemaphoreType.DMA((turns, groups)),
        pltpu.SemaphoreType.DMA((turns, groups)),
    ]
    if peers:
        others = jax.ShapeDtypeStruct((peers - 1, *shared.shape), shared.dtype)
        scratch += [pltpu.SemaphoreType.DMA((peers - 1,)), pltpu.SemaphoreType.DMA((peers - 1,))]
        products = jax.ShapeDtypeStruct(
            (factors[0].shape[1], factors[1].shape[1] + factors[3].shape[1]), BF16
        )
    return pl.pallas_call(
        functools.partial(carry_kernel, sign, ranges, peers),
        in_specs=[vmem] * 3 + ([anywhere] + [vmem] * len(factors) if peers else []),
        out_specs=[vmem, anywhere, vmem] if peers else vmem,
        out_shape=[state, others, products] if peers else state,
        scratch_shapes=scratch,
        compiler_params=pltpu.CompilerParams(
            collective_id=ident, has_side_effects=True, vmem_limit_bytes=48 << 20
        ),
        cost_estimate=pl.CostEstimate(flops=20 << 30, bytes_accessed=1 << 20, transcendentals=0),
    )(end[:N], log_decay, rates, *([shared, *factors] if peers else []))


def spread_matrix():
    rows = lax.broadcasted_iota(jnp.int32, (2 * N, N * LANES), 0) % N
    cols = lax.broadcasted_iota(jnp.int32, (2 * N, N * LANES), 1) // LANES
    return (rows == cols).astype(F32).astype(BF16)


def spread_into(pairs, rows):
    def turn(i, _):
        matrix = spread_matrix()
        at = pl.ds(pl.multiple_of(i * LANES, LANES), LANES)
        for source, target in pairs:
            value = source[at, :]
            high = value.astype(BF16)
            low = (value - high.astype(F32)).astype(BF16)
            target[at, :] = jnp.dot(
                jnp.concatenate([high, low], 1), matrix, preferred_element_type=F32
            )
        return 0

    lax.fori_loop(0, rows // LANES, turn, 0)


def lanes(k):
    return slice(k * LANES, (k + 1) * LANES)


def end_state_kernel(d_ref, u_ref, b_ref, r_ref, end_ref, rb, bb):
    rows, width = d_ref.shape
    seqs = rb.shape[1]
    length = rows // seqs
    parts = width // LANES
    for n in range(N):
        rb[n] = jnp.broadcast_to(r_ref[n : n + 1, :], (seqs, width))

    @pl.when(pl.program_id(0) == 0)
    def _():
        spread_into([(b_ref, bb)], rows)

    def body(t, carry):
        hs, total = carry
        row = pl.ds(pl.multiple_of(t * seqs, seqs), seqs)
        d = d_ref[row, :]
        du = d * u_ref[row, :]
        new = []
        for n in range(N):
            bn = bb[row, lanes(n)]
            for k in range(parts):
                a = jnp.exp(d[:, lanes(k)] * rb[n, :, lanes(k)])
                new.append(a * hs[n * parts + k] + du[:, lanes(k)] * bn)
        return tuple(new), total + d

    zero = jnp.zeros((seqs, LANES), F32)
    hs, total = lax.fori_loop(
        0, length, body, ((zero,) * (N * parts), jnp.zeros((seqs, width), F32)), unroll=4
    )
    for n in range(N):
        for k in range(parts):
            end_ref[n, :, lanes(k)] = hs[n * parts + k]
    end_ref[N] = total


def forward_kernel(
    peers,
    d_ref,
    u_ref,
    z_ref,
    b_ref,
    c_ref,
    r_ref,
    skip_ref,
    w_ref,
    h0_ref,
    x_ref,
    y_ref,
    gated_ref,
    st_ref,
    resid_ref,
    rb,
    bb,
    cb,
    state,
    total,
    sent,
    got,
    send_sem,
    recv_sem,
):
    rows, width = d_ref.shape
    seqs = rb.shape[1]
    length = rows // seqs
    parts = width // LANES
    piece, group = pl.program_id(0), pl.program_id(1)
    pieces, last = pl.num_programs(0), pl.num_programs(1) - 1
    fsdp, ctx, tensor = lax.axis_index("fsdp"), lax.axis_index("ctx"), lax.axis_index("tensor")
    partners = [(fsdp, ctx, lax.rem(tensor + by, peers)) for by in range(1, peers)]

    def copy(k, which):
        return pltpu.make_async_remote_copy(
            src_ref=sent.at[which],
            dst_ref=got.at[k, which],
            send_sem=send_sem.at[k, which],
            recv_sem=recv_sem.at[k, which],
            device_id=partners[k],
            device_id_type=MESH,
        )

    @pl.when((piece == 0) & (group == 0))
    def _():
        greet(partners)

    for n in range(N):
        rb[n] = jnp.broadcast_to(r_ref[n : n + 1, :], (seqs, width))

    @pl.when(group == 0)
    def _():
        spread_into([(b_ref, bb), (c_ref, cb)], rows)
        total[...] = jnp.zeros_like(total)

    @pl.when(piece == 0)
    def _():
        state[group] = h0_ref[...]

    def block(i, hs):
        for n in range(N):
            for k in range(parts):
                st_ref[i, n, :, lanes(k)] = hs[n * parts + k]

        def body(step, hs):
            t = i * BLK + step
            row = pl.ds(pl.multiple_of(t * seqs, seqs), seqs)
            d = d_ref[row, :]
            u = u_ref[row, :]
            du = d * u
            ys = [u[:, lanes(k)] * skip_ref[:, lanes(k)] for k in range(parts)]
            new = []
            for n in range(N):
                bn = bb[row, lanes(n)]
                cn = cb[row, lanes(n)]
                for k in range(parts):
                    a = jnp.exp(d[:, lanes(k)] * rb[n, :, lanes(k)])
                    h = a * hs[n * parts + k] + du[:, lanes(k)] * bn
                    ys[k] = ys[k] + h * cn
                    new.append(h)
            for k in range(parts):
                y_ref[row, lanes(k)] = ys[k]
            return tuple(new)

        return lax.fori_loop(0, BLK, body, hs, unroll=4)

    hs = lax.fori_loop(
        0,
        length // BLK,
        block,
        tuple(state[group, n, :, lanes(k)] for n in range(N) for k in range(parts)),
    )
    for n in range(N):
        for k in range(parts):
            state[group, n, :, lanes(k)] = hs[n * parts + k]
    z = z_ref[...]
    gated = (y_ref[...] * (z * jax.nn.sigmoid(z))).astype(BF16)
    gated_ref[...] = gated
    total[...] += jnp.dot(gated, w_ref[...], preferred_element_type=F32)

    def add(which):
        for k in range(peers - 1):
            copy(k, which).wait_recv()
        at = pl.ds(pl.multiple_of(which * rows, rows), rows)
        value = x_ref[at, :].astype(F32)
        own = sent[which].astype(F32)
        if peers == 2:
            value = value + (own + got[0, which].astype(F32))
        else:
            for owner in range(peers):
                term = own
                for k in range(peers - 1):
                    here = lax.rem(tensor + peers - k - 1, peers) == owner
                    term = jnp.where(here, got[k, which].astype(F32), term)
                value = value + term
        resid_ref[at, :] = value

    @pl.when(group == last)
    def _():
        sent[piece] = total[...].astype(BF16)
        for k in range(peers - 1):
            copy(k, piece).start()

        @pl.when(piece > 1)
        def _():
            add(piece - 2)

    @pl.when((group == last) & (piece == pieces - 1))
    def _():
        count = sent.shape[0]
        for which in range(max(count - 2, 0), count):
            add(which)
        for which in range(count):
            for k in range(peers - 1):
                copy(k, which).wait_send()


def start_grad_kernel(d_ref, dy_ref, c_ref, r_ref, g_ref, rb, cb):
    rows, width = d_ref.shape
    seqs = rb.shape[1]
    length = rows // seqs
    parts = width // LANES
    for n in range(N):
        rb[n] = jnp.broadcast_to(r_ref[n : n + 1, :], (seqs, width))

    @pl.when(pl.program_id(0) == 0)
    def _():
        spread_into([(c_ref, cb)], rows)

    def body(i, gs):
        t = length - 1 - i
        row = pl.ds(pl.multiple_of(t * seqs, seqs), seqs)
        d = d_ref[row, :]
        dy = dy_ref[row, :]
        new = []
        for n in range(N):
            cn = cb[row, lanes(n)]
            for k in range(parts):
                a = jnp.exp(d[:, lanes(k)] * rb[n, :, lanes(k)])
                new.append(a * (gs[n * parts + k] + dy[:, lanes(k)] * cn))
        return tuple(new)

    zero = jnp.zeros((seqs, LANES), F32)
    gs = lax.fori_loop(0, length, body, (zero,) * (N * parts), unroll=4)
    for n in range(N):
        for k in range(parts):
            g_ref[n, :, lanes(k)] = gs[n * parts + k]


def backward_kernel(
    d_ref,
    u_ref,
    dy_ref,
    sig_ref,
    b_ref,
    c_ref,
    r_ref,
    skip_ref,
    w_ref,
    st_ref,
    g0_ref,
    dstep_ref,
    du_ref,
    dproj_ref,
    rg_ref,
    bias_ref,
    skipg_ref,
    rb,
    bb,
    cb,
    hb,
    ab,
    pb,
    pc,
    dsb,
    total,
    columns,
):
    rows, width = d_ref.shape
    seqs = rb.shape[1]
    length = rows // seqs
    parts = width // LANES
    group = pl.program_id(0)
    for n in range(N):
        rb[n] = jnp.broadcast_to(r_ref[n : n + 1, :], (seqs, width))

    @pl.when(group == 0)
    def _():
        spread_into([(b_ref, bb), (c_ref, cb)], rows)
        total[...] = jnp.zeros_like(total)
        source = lax.broadcasted_iota(jnp.int32, columns.shape, 0) // LANES
        target = lax.broadcasted_iota(jnp.int32, columns.shape, 1)
        columns[...] = (source + R == target).astype(F32).astype(BF16)

    rg_ref[...] = jnp.zeros_like(rg_ref)
    bias_ref[...] = jnp.zeros_like(bias_ref)
    skipg_ref[...] = jnp.zeros_like(skipg_ref)

    def block(turn, gs):
        i = length // BLK - 1 - turn

        def again(step, hs):
            t = i * BLK + step
            row = pl.ds(pl.multiple_of(t * seqs, seqs), seqs)
            d = d_ref[row, :]
            du = d * u_ref[row, :]
            new = []
            for n in range(N):
                bn = bb[row, lanes(n)]
                for k in range(parts):
                    a = jnp.exp(d[:, lanes(k)] * rb[n, :, lanes(k)])
                    h = a * hs[n * parts + k] + du[:, lanes(k)] * bn
                    ab[step, n, :, lanes(k)] = a
                    hb[step + 1, n, :, lanes(k)] = h
                    new.append(h)
            return tuple(new)

        hs = tuple(st_ref[i, n, :, lanes(k)] for n in range(N) for k in range(parts))
        for n in range(N):
            for k in range(parts):
                hb[0, n, :, lanes(k)] = hs[n * parts + k]
        lax.fori_loop(0, BLK, again, hs, unroll=4)

        def back(turn, gs):
            step = BLK - 1 - turn
            t = i * BLK + step
            row = pl.ds(pl.multiple_of(t * seqs, seqs), seqs)
            here = pl.ds(pl.multiple_of(step * seqs, seqs), seqs)
            d = d_ref[row, :]
            u = u_ref[row, :]
            dy = dy_ref[row, :]
            du = d * u
            prods = [jnp.zeros((seqs, LANES), F32) for _ in range(parts)]
            steps = [jnp.zeros((seqs, LANES), F32) for _ in range(parts)]
            new = []
            for n in range(N):
                bn = bb[row, lanes(n)]
                cn = cb[row, lanes(n)]
                b_sum = c_sum = None
                for k in range(parts):
                    g = gs[n * parts + k] + cn * dy[:, lanes(k)]
                    c_term = hb[step + 1, n, :, lanes(k)] * dy[:, lanes(k)]
                    b_term = g * du[:, lanes(k)]
                    c_sum = c_term if k == 0 else c_sum + c_term
                    b_sum = b_term if k == 0 else b_sum + b_term
                    prods[k] = prods[k] + g * bn
                    carried_g = g * ab[step, n, :, lanes(k)]
                    decay_g = carried_g * hb[step, n, :, lanes(k)]
                    steps[k] = steps[k] + decay_g * rb[n, :, lanes(k)]
                    rg_ref[n, :, lanes(k)] = rg_ref[n, :, lanes(k)] + decay_g * d[:, lanes(k)]
                    new.append(carried_g)
                pb[here, lanes(n)] = b_sum
                pc[here, lanes(n)] = c_sum
            skipg_ref[...] += dy * u
            for k in range(parts):
                dsb[here, lanes(k)] = steps[k] + prods[k] * u[:, lanes(k)]
                du_ref[row, lanes(k)] = (
                    prods[k] * d[:, lanes(k)] + dy[:, lanes(k)] * skip_ref[:, lanes(k)]
                )
            return tuple(new)

        gs = lax.fori_loop(0, BLK, back, gs, unroll=4)
        at = pl.ds(pl.multiple_of(i * BLK * seqs, BLK * seqs), BLK * seqs)
        d_step = (dsb[...] * sig_ref[at, :]).astype(BF16)
        dstep_ref[at, :] = d_step
        bias_ref[...] += jnp.sum(d_step.astype(F32).reshape(BLK, seqs, width), 0)
        total[at, :] += (
            jnp.dot(d_step, w_ref[...], preferred_element_type=F32)
            + jnp.dot(pb[...].astype(BF16), columns[: N * LANES], preferred_element_type=F32)
            + jnp.dot(pc[...].astype(BF16), columns[N * LANES :], preferred_element_type=F32)
        )
        return gs

    lax.fori_loop(
        0,
        length // BLK,
        block,
        tuple(g0_ref[n, :, lanes(k)] for n in range(N) for k in range(parts)),
    )

    @pl.when(group == pl.num_programs(0) - 1)
    def _():
        dproj_ref[...] = total[...].astype(BF16)


def normalized(x):
    return x * lax.rsqrt(jnp.mean(x * x, -1, keepdims=True) + EPS)


def inner_grad_step(seqs, refs, x, sums, dconv):
    (
        du_ref,
        dproj_ref,
        conv_ref,
        ext_ref,
        normed_ref,
        u_ref,
        rank_ref,
        dstep_ref,
        dgate_ref,
        w_in_ref,
        w_gate_ref,
        w_x_ref,
        taps_ref,
        after_ref,
    ) = refs
    gin_ref, narrow_ref, chan_ref, gain_ref = sums
    rows, chans = du_ref.shape
    rim = (CONV_TAPS - 1) * seqs
    turn = pl.program_id(0)
    first = pl.multiple_of((pl.num_programs(0) - 1 - turn) * rows, rows)

    @pl.when(turn == 0)
    def _():
        for ref in sums:
            ref[...] = jnp.zeros_like(ref)
        dconv[rows:, :] = after_ref[...]

    @pl.when(turn > 0)
    def _():
        dconv[rows:, :] = dconv[:rim, :]

    def by_seq(value):
        return jnp.sum(value.reshape(rows // seqs, seqs, value.shape[-1]), 0)

    d_proj = dproj_ref[...]
    conv = conv_ref[...]
    sig = jax.nn.sigmoid(conv)
    d_conv = (du_ref[...] + dot(d_proj, w_x_ref[...], NT)) * (sig * (1.0 + conv * (1.0 - sig)))
    dconv[:rows, :] = d_conv
    d_inner = jnp.zeros_like(d_conv)
    for tap in range(CONV_TAPS):
        at = (CONV_TAPS - 1 - tap) * seqs
        d_inner = d_inner + taps_ref[tap : tap + 1, :] * dconv[at : at + rows, :]
        ext = ext_ref[pl.ds(pl.multiple_of(first + tap * seqs, seqs), rows), :]
        chan_ref[tap * seqs : (tap + 1) * seqs, :] += by_seq(d_conv * ext)
    chan_ref[CONV_TAPS * seqs :, :] += by_seq(d_conv)
    d_inner = d_inner.astype(BF16)
    part = dot(d_inner, w_in_ref[...]) + dot(dgate_ref[...], w_gate_ref[...])
    gain_ref[...] += by_seq(part * normalized(x.astype(F32)))
    gin_ref[...] += dot(d_inner, normed_ref[...], TN)
    narrow = dot(u_ref[...], d_proj, TN) + dot(dstep_ref[...], rank_ref[...], TN)
    narrow_ref[...] = narrow_ref[...] + narrow
    return part


def inner_grad_kernel(seqs, *refs):
    refs, x_ref, late_ref, early_ref, sums, dconv = (
        refs[:14],
        refs[14],
        refs[15],
        refs[16],
        refs[17:21],
        refs[21],
    )
    part = inner_grad_step(seqs, refs, x_ref[...], sums, dconv).astype(BF16)
    turn, half = pl.program_id(0), pl.num_programs(0) // 2

    @pl.when(turn < half)
    def _():
        late_ref[...] = part

    @pl.when(turn >= half)
    def _():
        early_ref[...] = part


def finish_kernel(shape, sizes, turns, *refs):
    micros, group = shape
    seqs = micros * group
    step_refs, refs = refs[:14], refs[14:]
    x_ref, dres_ref, act_own_ref, act_got_ref, g_ref, vec_ref, routing_ref, early_ref = refs[:8]
    grad_ref, act_ref, in_ref, out_ref, proj_ref, step_ref, channel_ref, route_ref, tail_ref = refs[
        8:17
    ]
    refs = refs[7:]
    sums, dconv, sent, got, gain_got, tail, grad_tok, act_tok = (
        refs[10:14],
        refs[14],
        refs[15],
        refs[16],
        refs[17],
        refs[18],
        refs[19],
        refs[20],
    )
    mine_ref = refs[21]
    refs = refs[22:]
    bits = [("ctx", 1 << k) for k in range(sizes[1].bit_length() - 1)]
    bits += [("fsdp", 1 << k) for k in range(sizes[0].bit_length() - 1)]
    stages = len(bits)
    sends, gots = refs[:stages], refs[stages : 2 * stages]
    part_sems, gain_sems, sum_sems = (
        refs[2 * stages : 2 * stages + 2],
        refs[2 * stages + 2 : 2 * stages + 4],
        refs[2 * stages + 4 : 2 * stages + 6],
    )
    where = {axis: lax.axis_index(axis) for axis in ("fsdp", "ctx", "tensor")}
    across = (where["fsdp"], where["ctx"], 1 - where["tensor"])
    high = [lax.rem(where[axis] // bit, 2) for axis, bit in bits]
    partners = []
    for (axis, bit), one in zip(bits, high):
        to = dict(where)
        to[axis] = where[axis] + bit - 2 * bit * one
        partners.append((to["fsdp"], to["ctx"], to["tensor"]))

    def remote(src, dst, sems, at, to):
        return pltpu.make_async_remote_copy(
            src_ref=src,
            dst_ref=dst,
            send_sem=sems[0].at[at],
            recv_sem=sems[1].at[at],
            device_id=to,
            device_id_type=MESH,
        )

    blocks = [pl.ds(0, 1), pl.ds(1, turns - 2), pl.ds(turns - 1, 1)]

    def part_copy(which):
        at = blocks[which]
        return remote(sent.at[at], got.at[at], part_sems, which, across)

    def sum_copy(stage, half):
        source = sends[stage].at[half, 1 - high[stage]]
        return remote(source, gots[stage].at[half], sum_sems, (stage, half), partners[stage])

    turn = pl.program_id(0)

    @pl.when(turn == 0)
    def _():
        greet([across] + partners)

    rows = step_refs[0].shape[0]
    first = pl.multiple_of((turns - 1 - turn) * rows, rows)
    part = inner_grad_step(seqs, step_refs, x_ref[pl.ds(first, rows), :], sums, dconv)
    sent[turn] = part.astype(BF16)

    @pl.when(turn == 0)
    def _():
        part_copy(0).start()

    @pl.when(turn == turns - 2)
    def _():
        part_copy(0).wait_send()
        part_copy(1).start()


    def output(which):
        at = slice((turns - 1 - which) * rows, (turns - which) * rows)
        x = x_ref[at, :].astype(F32)
        width = x.shape[1]
        scale = lax.rsqrt(jnp.mean(x * x, -1, keepdims=True) + EPS)
        xhat = x * scale
        scaled = g_ref[...] * (sent[which].astype(F32) + got[which].astype(F32))
        mean = jnp.mean(scaled * xhat, -1, keepdims=True)
        grad = dres_ref[at, :].astype(F32) + scale * (scaled - xhat * mean)
        own, other = act_own_ref[at, :].astype(F32), act_got_ref[0, at, :].astype(F32)
        left = where["tensor"] == 0
        act = jnp.concatenate([jnp.where(left, own, other), jnp.where(left, other, own)], 1)
        count = rows // seqs
        times = slice((turns - 1 - which) * count, (turns - which) * count)
        for k in range(width // LANES):
            grad_tok[k] = grad[:, lanes(k)]
            act_tok[k] = act[:, lanes(k)]
        for m in range(micros):
            for g in range(group):
                every = pl.ds(m * group + g, count, stride=seqs)
                for k in range(width // LANES):
                    grad_ref[m, g, times, lanes(k)] = grad_tok[k, every, :]
                    act_ref[m, g, times, lanes(k)] = act_tok[k, every, :].astype(BF16)

    @pl.when(turn == turns - 1)
    def _():
        gin_ref, narrow_ref, chan_ref, gain_ref = sums
        gain_copy = remote(gain_ref, gain_got, gain_sems, 0, across)
        gain_copy.start()
        owned = mine_ref.shape[0]
        half_cols = mine_ref.shape[1] // 2
        rest = gin_ref.shape[1] - half_cols

        def fill(stage, half):
            count = 1 << (stages - stage)
            for k in range(count):
                target = (half, k % 2, k // 2)
                if stage > 0:
                    before = (half, high[stage - 1], k)
                    value = sends[stage - 1][before].astype(F32)
                    value = value + gots[stage - 1][half, k].astype(F32)
                    sends[stage][target] = value.astype(BF16)
                    continue
                at = slice(k * owned, (k + 1) * owned)
                if half == 0:
                    sends[0][target] = gin_ref[at, :half_cols].astype(BF16)
                else:
                    joined = [gin_ref[at, half_cols:], narrow_ref[at, :], tail[at, :]]
                    sends[0][target] = jnp.concatenate(joined, 1).astype(BF16)
            sum_copy(stage, half).start()

        fill(0, 0)
        gain_copy.wait()
        vec = vec_ref[...]
        row = lax.broadcasted_iota(jnp.int32, vec.shape, 0)
        for k in range(CONV_TAPS + 1):
            value = jnp.sum(chan_ref[k * seqs : (k + 1) * seqs, :], 0, keepdims=True)
            vec = jnp.where(row == k, value, vec)
        gain = jnp.sum(gain_ref[...] + gain_got[...], 0, keepdims=True)
        vec = jnp.where(row == VECTORS, gain, vec)
        tail[...] = vec.T + routing_ref[...]
        fill(0, 1)
        part_copy(0).wait_recv()
        output(0)
        for stage in range(1, stages):
            for half in range(2):
                sum_copy(stage - 1, half).wait_recv()
                fill(stage, half)
            if stage == 1:
                part_copy(1).wait()
                part_copy(2).start()
            if stage < turns - 1:
                output(stage)
        for which in range(stages, turns - 1):
            output(which)
        part_copy(2).wait_recv()
        output(turns - 1)
        for half in range(2):
            sum_copy(stages - 1, half).wait_recv()
            value = sends[stages - 1][half, high[stages - 1], 0].astype(F32)
            mine_ref[:, half * half_cols : (half + 1) * half_cols] = value + gots[stages - 1][
                half, 0
            ].astype(F32)
        width, cols = in_ref.shape[2], proj_ref.shape[1]
        in_ref[0] = mine_ref[:, :width]
        in_ref[1] = early_ref[:, :width].astype(F32)
        out_ref[...] = early_ref[:, width:].astype(F32)
        proj_ref[...] = mine_ref[:, width : width + cols]
        step_ref[...] = mine_ref[:, width + cols : width + cols + R]
        at = width + LANES
        channel_ref[...] = mine_ref[:, at : at + VECTORS - 1]
        at += VECTORS + 1
        route_ref[...] = mine_ref[:, at : at + route_ref.shape[1]]
        tail_ref[...] = mine_ref[:, width + LANES :]
        for stage in range(stages):
            for half in range(2):
                sum_copy(stage, half).wait_send()
        part_copy(2).wait_send()


def output_kernel(shape, peers, *refs):
    micros, group = shape
    early, late, refs = refs[:peers], refs[peers : 2 * peers], refs[2 * peers :]
    x_ref, dres_ref, act_own_ref, act_others_ref, gain_ref, grad_ref, act_ref, grad_tok, act_tok = refs
    x = x_ref[...].astype(F32)
    scale = lax.rsqrt(jnp.mean(x * x, -1, keepdims=True) + EPS)
    xhat = x * scale
    is_early = pl.program_id(0) < pl.num_programs(0) // 2
    d_normed = jnp.zeros_like(x)
    for first, second in zip(early, late):
        d_normed = d_normed + jnp.where(is_early, first[...], second[...]).astype(F32)
    scaled = gain_ref[...] * d_normed
    mean = jnp.mean(scaled * xhat, -1, keepdims=True)
    grad = dres_ref[...].astype(F32) + scale * (scaled - xhat * mean)
    seqs = micros * group
    rows, width = x.shape
    count = rows // seqs
    tensor = lax.axis_index("tensor")
    pieces = []
    for owner in range(peers):
        piece = act_own_ref[...].astype(F32)
        for by in range(1, peers):
            here = lax.rem(tensor + peers - by, peers) == owner
            piece = jnp.where(here, act_others_ref[by - 1].astype(F32), piece)
        pieces.append(piece)
    act = jnp.concatenate(pieces, 1)
    for k in range(width // LANES):
        grad_tok[k] = grad[:, lanes(k)]
        act_tok[k] = act[:, lanes(k)]
    for m in range(micros):
        for g in range(group):
            at = pl.ds(m * group + g, count, stride=seqs)
            for k in range(width // LANES):
                grad_ref[m, g, :, lanes(k)] = grad_tok[k, at, :]
                act_ref[m, g, :, lanes(k)] = act_tok[k, at, :].astype(BF16)


def scan_call(kernel, arrays, outs, scratch, width, chans, chunk=0, cost=None):
    def spec(shape, kind):
        def place(j, rank=len(shape)):
            at = [0] * rank
            if "t" in kind:
                at[0] = chunk
            if "c" in kind:
                at[-1] = j
            if "r" in kind:
                at[0] = j
            return tuple(at)

        return pl.BlockSpec(shape, place)

    return pl.pallas_call(
        kernel,
        grid=(chans // width,),
        in_specs=[spec(shape, kind) for _, shape, kind in arrays],
        out_specs=[spec(shape, kind) for _, shape, kind in outs],
        out_shape=[a for a, _, _ in outs],
        scratch_shapes=[
            s if not isinstance(s, tuple) else pltpu.VMEM(s, F32) for s in scratch
        ],
        compiler_params=pltpu.CompilerParams(vmem_limit_bytes=62 << 20),
        cost_estimate=cost,
    )(*[a for a, _, _ in arrays])


def per_device(
    inputs,
    out_grad,
    lengths,
    routes,
    slots,
    norm_gains,
    router_matrix,
    input_projection,
    inner_projection,
    step_projection,
    step_bias,
    channel_params,
    output_projection,
    expert_up,
    expert_down,
):
    micros, group, length, width = inputs.shape
    seqs = micros * group
    tokens = length * seqs
    owners = lax.axis_size("fsdp") * lax.axis_size("ctx")
    experts = router_matrix.shape[1]
    capacity = max(2, (25 * group * length + 32 * experts - 1) // (32 * experts))
    slots_each = micros * capacity
    rows = experts * slots_each

    def by_token(value):
        return jnp.moveaxis(value, 2, 0).reshape(tokens, *value.shape[3:])

    narrow = jnp.concatenate(
        [inner_projection, step_projection, channel_params, step_bias[:, None]], 1
    )
    x_cols = inner_projection.shape[1]
    cuts = [x_cols, x_cols + R, x_cols + R + channel_params.shape[1]]
    routing = jnp.concatenate([router_matrix, norm_gains.T], 1)
    joined = narrow.shape[0] == routing.shape[0]
    if joined:
        narrow = jnp.concatenate([narrow, routing], 1)
    narrow_cols = narrow.shape[1]
    pad = -narrow_cols % LANES
    first = jnp.concatenate([input_projection[0], jnp.pad(narrow, ((0, 0), (0, pad)))], 1)
    later = jnp.concatenate([input_projection[1], output_projection], 1)
    full = lax.all_gather(first, OWNERS, axis=0, tiled=True)
    later_full = lax.all_gather(later, OWNERS, axis=0, tiled=True)

    position = lax.axis_index("ctx") * length + jnp.arange(length)
    valid = (position[:, None] < lengths.reshape(1, seqs)).astype(F32).reshape(tokens, 1)
    route = by_token(routes)
    slot = by_token(slots)
    kept = slot >= 0
    kept_f = kept.astype(F32)
    micro_of = (jnp.arange(tokens) // group) % micros
    place = jnp.where(kept, route * slots_each + micro_of * capacity + slot, -1)
    pick = (
        jnp.arange(rows).reshape(experts, slots_each, 1) == place[None, None, :]
    ).astype(BF16)
    grad_tok = by_token(out_grad)
    grad_act = grad_tok.astype(F32) * valid

    def packed(value):
        return jnp.einsum("est,td->esd", pick, value, preferred_element_type=F32).astype(BF16)

    def unpacked(value):
        flat = value.reshape(rows, value.shape[-1])
        return lax.optimization_barrier(dot(pick.reshape(rows, tokens), flat, TN))

    def swap_owners(value):
        return lax.all_to_all(value, OWNERS, split_axis=0, concat_axis=0, tiled=True)

    full, grad_packed = lax.optimization_barrier((full, packed(grad_tok)))
    grad_rows_raw = swap_owners(grad_packed)

    w_in = full[:, :width]
    tail = full[:, width:]
    w_gate, w_out = later_full[:, :width], later_full[:, width:]
    w_x = tail[:, : cuts[0]]
    w_step = tail[:, cuts[0] : cuts[1]]
    channel_f = tail[:, cuts[1] : cuts[2]].astype(F32)
    bias_f = tail[:, cuts[2]].astype(F32)
    if joined:
        full_routing = tail[:, cuts[2] + 1 : cuts[2] + 1 + routing.shape[1]]
    else:
        full_routing = lax.all_gather(routing, OWNERS, axis=0, tiled=True)
    w_router = full_routing[:, :experts]
    gains = full_routing[:, experts:].T.astype(F32)
    chans = channel_f.shape[0]
    taps = channel_f[:, :CONV_TAPS].T
    conv_bias = channel_f[:, CONV_TAPS]
    skip = channel_f[:, CONV_TAPS + 1]
    rates = -jnp.exp(channel_f[:, CONV_TAPS + 2 :]).T

    x_tok = lax.optimization_barrier(by_token(inputs))
    x = x_tok.astype(F32)
    normed1 = (normalized(x) * gains[0]).astype(BF16)
    inner = dot(normed1, w_in, NT).astype(BF16)
    rim = (CONV_TAPS - 1) * seqs
    before = moved(inner[tokens - rim :], 1)
    gate_z = dot(normed1, w_gate, NT)
    extended = jnp.concatenate([before, inner], 0).astype(F32)
    conv = conv_bias
    for tap in range(CONV_TAPS):
        conv = conv + taps[tap] * extended[tap * seqs : tap * seqs + tokens]
    u = jax.nn.silu(conv).astype(BF16)
    u_wide = u.astype(F32)
    proj = tensor_total(dot(u, w_x), BF16)
    rank = proj[:, :R].astype(BF16)
    b_vals = proj[:, R : R + N]
    c_vals = proj[:, R + N :]
    step_pre = dot(rank, w_step, NT) + bias_f
    delta = jax.nn.softplus(step_pre)
    lane_width = 2 * LANES if chans % (2 * LANES) == 0 else LANES
    wide_rates = (N, seqs, lane_width)
    state_block = (N, seqs, lane_width)
    call = functools.partial(scan_call, width=lane_width, chans=chans)

    def both_in(value, steps=length):
        return (value, (steps * seqs, lane_width), "tc")

    def by_chan(value):
        return (value, (*value.shape[:-1], lane_width), "c")

    def by_rows(value, steps=length):
        return (value, (steps * seqs, value.shape[1]), "t")

    def cost(steps, ops):
        elements = steps * seqs * chans * N
        return pl.CostEstimate(flops=300 * ops * elements, bytes_accessed=elements, transcendentals=0)

    def out(shape, dtype=F32):
        return jax.ShapeDtypeStruct(shape, dtype)

    [end] = call(
        end_state_kernel,
        [both_in(delta), both_in(u_wide), by_rows(b_vals), by_chan(rates)],
        [by_chan(out((N + 1, seqs, chans)))],
        [wide_rates, (tokens, N * LANES)],
        cost=cost(length, 6),
    )
    end, grad_rows_raw = lax.optimization_barrier((end, grad_rows_raw))
    log_decay = end[N]
    state = carried(end, log_decay, rates, 1, 0)
    pieces = 4 if length % (4 * BLK) == 0 else 1
    steps = length // pieces
    block = steps * seqs
    groups = chans // lane_width
    peers, here = lax.axis_size("tensor"), lax.axis_index("tensor")

    def cut(value, *shape):
        return value, pl.BlockSpec(shape, lambda p, j: (p, j))

    def by_piece(value):
        return value, pl.BlockSpec((block, value.shape[1]), lambda p, j: (p, 0))

    def by_group(value):
        rank = value.ndim - 1
        return value, pl.BlockSpec(
            (*value.shape[:-1], lane_width), lambda p, j: (0,) * rank + (j,)
        )

    arrays = [
        cut(delta, block, lane_width),
        cut(u_wide, block, lane_width),
        cut(gate_z, block, lane_width),
        by_piece(b_vals),
        by_piece(c_vals),
        by_group(rates),
        by_group(skip[None]),
        (later_full, pl.BlockSpec((lane_width, width), lambda p, j: (j, 1))),
        by_group(state),
        (x_tok, pl.BlockSpec((tokens, width), lambda p, j: (0, 0))),
    ]
    results = [
        cut(out((tokens, chans)), block, lane_width),
        cut(out((tokens, chans), BF16), block, lane_width),
        (
            out((length // BLK, N, seqs, chans)),
            pl.BlockSpec((steps // BLK, N, seqs, lane_width), lambda p, j: (p, 0, 0, j)),
        ),
        (out((tokens, width)), pl.BlockSpec((tokens, width), lambda p, j: (0, 0))),
    ]
    y_vals, gated, starts, resid = pl.pallas_call(
        functools.partial(forward_kernel, peers),
        grid=(pieces, groups),
        in_specs=[spec for _, spec in arrays],
        out_specs=[spec for _, spec in results],
        out_shape=[value for value, _ in results],
        scratch_shapes=[
            pltpu.VMEM(wide_rates, F32),
            pltpu.VMEM((block, N * LANES), F32),
            pltpu.VMEM((block, N * LANES), F32),
            pltpu.VMEM((groups, *state_block), F32),
            pltpu.VMEM((block, width), F32),
            pltpu.VMEM((pieces, block, width), BF16),
            pltpu.VMEM((peers - 1, pieces, block, width), BF16),
            pltpu.SemaphoreType.DMA((peers - 1, pieces)),
            pltpu.SemaphoreType.DMA((peers - 1, pieces)),
        ],
        compiler_params=pltpu.CompilerParams(
            collective_id=2, has_side_effects=True, vmem_limit_bytes=62 << 20
        ),
        cost_estimate=cost(length, 10),
    )(*[value for value, _ in arrays])
    silu_z, gate_slope = silu_parts(gate_z)

    scale2 = lax.rsqrt(jnp.mean(resid * resid, -1, keepdims=True) + EPS)
    xhat2 = resid * scale2
    normed2 = (xhat2 * gains[1]).astype(BF16)
    probs = jax.nn.softmax(dot(normed2, w_router), -1)
    onehot = (route[:, None] == jnp.arange(experts)).astype(F32)
    gate = jnp.sum(probs * onehot, -1, keepdims=True) * kept_f[:, None]
    share = width // peers

    def half(value):
        cut = value[..., :share]
        for peer in range(1, peers):
            cut = jnp.where(here == peer, value[..., peer * share : (peer + 1) * share], cut)
        return cut

    x_rows = tensor_columns(swap_owners(packed(half(normed2))))
    gate_rows = swap_owners(
        jnp.sum(jnp.where(pick > 0, gate[:, 0], 0.0), -1)[:, None, :]
    )
    grad_rows = (jnp.swapaxes(gate_rows, 1, 2) * grad_rows_raw.astype(F32)).astype(BF16)
    up, down = expert_up[0], expert_down[0]

    def product(a, b, terms):
        return jnp.einsum(terms, a, b, preferred_element_type=F32)

    def halves(matrix, axis):
        low, high = jnp.split(matrix, 2, axis)
        return jnp.where(here == 0, low, high), jnp.where(here == 0, high, low)

    def scattered(value):
        return lax.psum_scatter(value, "tensor", scatter_dimension=2, tiled=True).astype(BF16)

    hidden = product(x_rows, up, "srd,df->srf")
    act_float, gelu_pull = jax.vjp(lambda v: jax.nn.gelu(v, approximate=True), hidden)
    act = act_float.astype(BF16)
    d_act = product(grad_rows, down, "srd,fd->srf")
    d_hidden = gelu_pull(d_act)[0].astype(BF16)
    q_rows = jnp.sum(act.astype(F32) * d_act, -1)
    if peers == 2:
        up_own, up_other = halves(up, 0)
        down_own, down_other = halves(down, 1)
        x_sent = product(d_hidden, up_other, "srf,df->srd").astype(BF16)
        x_got = swapped(x_sent)
        act_late, _ = lax.optimization_barrier((act, x_sent))
        x_own = product(d_hidden, up_own, "srf,df->srd")
        y_sent = product(act_late, down_other, "srf,fd->srd").astype(BF16)
        x_got, y_sent = lax.optimization_barrier((x_got, y_sent))
        back_x = swap_owners((x_own + x_got.astype(F32)).astype(BF16))
        y_got = swapped(y_sent)
        y_own = product(act_late, down_own, "srf,fd->srd")
        share_y = (y_own + y_got.astype(F32)).astype(BF16)
    else:
        back_x = swap_owners(scattered(product(d_hidden, up, "srf,df->srd")))
        share_y = scattered(product(act, down, "srf,fd->srd"))
    q_back = swap_owners(q_rows[:, None, :])
    grad_up = product(x_rows, d_hidden, "srd,srf->df")
    grad_down = product(act, grad_rows, "srf,srd->fd")
    back_x, grad_up, grad_down, share_y = lax.optimization_barrier(
        (back_x, grad_up, grad_down, share_y)
    )
    expert_dx = unpacked(back_x)
    q_part = jnp.sum(jnp.where(pick > 0, q_back[:, 0, :, None], 0.0), (0, 1))
    x_half = half(xhat2)
    gain_half = half(gains[1])
    grad_half = half(grad_act)
    router_half = half(w_router.T)
    sums = jnp.stack([q_part, jnp.sum(gain_half * expert_dx * x_half, -1)])
    sums = tensor_total(sums, F32)
    d_logits = (sums[0][:, None] * (onehot - probs)).astype(BF16)
    grad_router = dot(normed2, d_logits, TN)
    by_router = dot((xhat2 * gains[1]).astype(BF16), w_router)
    mean_term = (
        sums[1][:, None] + jnp.sum(d_logits.astype(F32) * by_router, -1, keepdims=True)
    ) / width
    d_normed2 = expert_dx + dot(d_logits, router_half)
    gain_grad2 = tensor_columns(jnp.sum(d_normed2 * x_half, 0, keepdims=True))[0]
    d_resid_half = grad_half + scale2 * (gain_half * d_normed2 - x_half * mean_term)

    d_mixed = tensor_columns(d_resid_half.astype(BF16))
    d_mixed, share_y = lax.optimization_barrier((d_mixed, share_y))
    expert_y = unpacked(swap_owners(share_y))
    act_half = (valid * (half(resid) + gate * expert_y)).astype(BF16)
    d_gated = dot(d_mixed, w_out, NT)
    d_y = d_gated * silu_z
    [start_grad] = call(
        start_grad_kernel,
        [both_in(delta), both_in(d_y), by_rows(c_vals), by_chan(rates)],
        [by_chan(out((N, seqs, chans)))],
        [wide_rates, (tokens, N * LANES)],
        cost=cost(length, 6),
    )
    d_gate_z = (d_gated * y_vals * gate_slope).astype(BF16)

    def owned(value):
        return lax.psum_scatter(value.astype(BF16), OWNERS, scatter_dimension=0, tiled=True)

    grad_end, act_others, early = carried(
        start_grad, log_decay, rates, -1, 1, act_half, (d_gate_z, normed1, gated, d_mixed)
    )
    mine_early = owned(early)
    w_step_wide = jnp.pad(w_step, ((0, 0), (0, LANES - R)))
    d_step, du_part, d_proj_part, rate_grad, bias_sums, skip_sums = call(
        backward_kernel,
        [
            both_in(delta),
            both_in(u_wide),
            both_in(d_y),
            (jax.nn.sigmoid(step_pre), (tokens, lane_width), "tc"),
            by_rows(b_vals),
            by_rows(c_vals),
            by_chan(rates),
            by_chan(skip[None]),
            (w_step_wide, (lane_width, LANES), "r"),
            by_chan(starts),
            by_chan(grad_end),
        ],
        [
            by_chan(out((tokens, chans), BF16)),
            by_chan(out((tokens, chans))),
            (out((tokens, LANES), BF16), (tokens, LANES), ""),
            by_chan(out((N, seqs, chans))),
            by_chan(out((seqs, chans))),
            by_chan(out((seqs, chans))),
        ],
        [
            wide_rates,
            (tokens, N * LANES),
            (tokens, N * LANES),
            (BLK + 1, N, seqs, lane_width),
            (BLK, N, seqs, lane_width),
            (BLK * seqs, N * LANES),
            (BLK * seqs, N * LANES),
            (BLK * seqs, lane_width),
            (tokens, LANES),
            pltpu.VMEM((2 * N * LANES, LANES), BF16),
        ],
        cost=cost(length, 24),
    )
    d_proj = tensor_total(d_proj_part, BF16).astype(BF16)
    step_bias_grad = jnp.sum(bias_sums, 0)
    skip_grad = jnp.sum(skip_sums, 0)
    w_x_wide = jnp.pad(w_x, ((0, 0), (0, LANES - x_cols)))
    rim_u = du_part[:rim] + dot(d_proj[:rim], w_x_wide, NT)
    after = moved(rim_u * silu_parts(conv[:rim])[1], -1)
    steps = length // 4
    block = steps * seqs
    turns = length // steps

    def from_end(value):
        return value, pl.BlockSpec((block, value.shape[1]), lambda i: (turns - 1 - i, 0))

    def whole(value):
        return value, pl.BlockSpec(value.shape, lambda i: (0, 0))

    arrays = [
        from_end(du_part),
        from_end(d_proj),
        from_end(conv),
        whole(extended),
        from_end(normed1),
        from_end(u),
        from_end(jnp.pad(rank, ((0, 0), (x_cols, LANES - x_cols - R)))),
        from_end(d_step),
        from_end(d_gate_z),
        (full, pl.BlockSpec((chans, width), lambda i: (0, 0))),
        (later_full, pl.BlockSpec((chans, width), lambda i: (0, 0))),
        whole(w_x_wide),
        whole(taps),
        whole(after),
    ]
    rows_each = narrow.shape[0]
    decay_grad = jnp.sum(rate_grad, 1) * rates
    fused = joined and peers == 2 and rows_each % 16 == 0 and owners >= 4 and VECTORS + 2 + experts <= LANES
    if fused:
        vectors = jnp.concatenate([skip_grad[None], decay_grad, step_bias_grad[None]], 0)
        vectors = jnp.pad(vectors, ((CONV_TAPS + 1, LANES - VECTORS), (0, 0)))
        routing_wide = jnp.pad(
            jnp.concatenate([grad_router, gain_grad2[:, None]], 1),
            ((0, 0), (VECTORS + 1, LANES - VECTORS - 2 - experts)),
        )

        def entire(value):
            return value, pl.BlockSpec(value.shape, lambda i: (0,) * value.ndim)

        arrays += [
            whole(x_tok),
            whole(d_mixed),
            whole(act_half),
            entire(act_others),
            whole(gains[:1]),
            whole(vectors),
            whole(routing_wide),
            whole(mine_early),
        ]
        cols = width + 2 * LANES
        results = [
            entire(out(inputs.shape)),
            entire(out(inputs.shape, BF16)),
            entire(out((2, rows_each, width))),
            *[
                whole(out((rows_each, count)))
                for count in (width, x_cols, R, VECTORS - 1, experts, LANES)
            ],
        ]
        sizes = (lax.axis_size("fsdp"), lax.axis_size("ctx"))
        stages = (owners - 1).bit_length()
        counts = [owners >> (stage + 1) for stage in range(stages)]
        (
            input_grad,
            activations,
            mine_in,
            mine_out,
            mine_x,
            mine_dt,
            mine_channel,
            mine_router,
            mine_tail,
        ) = pl.pallas_call(
            functools.partial(finish_kernel, (micros, group), sizes, turns),
            grid=(turns,),
            in_specs=[spec for _, spec in arrays],
            out_specs=[spec for _, spec in results],
            out_shape=[value for value, _ in results],
            scratch_shapes=[
                pltpu.VMEM((chans, width), F32),
                pltpu.VMEM((chans, LANES), F32),
                pltpu.VMEM(((CONV_TAPS + 1) * seqs, chans), F32),
                pltpu.VMEM((seqs, width), F32),
                pltpu.VMEM((block + rim, chans), F32),
                pltpu.VMEM((turns, block, width), BF16),
                pltpu.VMEM((turns, block, width), BF16),
                pltpu.VMEM((seqs, width), F32),
                pltpu.VMEM((chans, LANES), F32),
                pltpu.VMEM((width // LANES, block, LANES), F32),
                pltpu.VMEM((width // LANES, block, LANES), F32),
                pltpu.VMEM((rows_each, cols), F32),
                *[pltpu.VMEM((2, 2, count, rows_each, cols // 2), BF16) for count in counts],
                *[pltpu.VMEM((2, count, rows_each, cols // 2), BF16) for count in counts],
                pltpu.SemaphoreType.DMA((3,)),
                pltpu.SemaphoreType.DMA((3,)),
                pltpu.SemaphoreType.DMA((1,)),
                pltpu.SemaphoreType.DMA((1,)),
                pltpu.SemaphoreType.DMA((stages, 2)),
                pltpu.SemaphoreType.DMA((stages, 2)),
            ],
            compiler_params=pltpu.CompilerParams(
                collective_id=3, has_side_effects=True, vmem_limit_bytes=63 << 20
            ),
        )(*[value for value, _ in arrays])
        mine_bias = mine_tail[:, VECTORS - 1]
        gains_out = jnp.stack([mine_tail[:, VECTORS], mine_tail[:, VECTORS + 1 + experts]])
        return (
            activations,
            input_grad,
            gains_out,
            mine_router,
            mine_in,
            mine_x,
            mine_dt,
            mine_bias,
            mine_channel,
            mine_out,
            grad_up[None],
            grad_down[None],
        )
    arrays.append(from_end(x_tok))
    results = [
        (
            out((tokens // 2, width), BF16),
            pl.BlockSpec((block, width), lambda i: (jnp.maximum(turns // 2 - 1 - i, 0), 0)),
        ),
        (
            out((tokens // 2, width), BF16),
            pl.BlockSpec(
                (block, width), lambda i: (jnp.minimum(turns - 1 - i, turns // 2 - 1), 0)
            ),
        ),
        whole(out((chans, width))),
        whole(out((chans, LANES))),
        whole(out(((CONV_TAPS + 1) * seqs, chans))),
        whole(out((seqs, width))),
    ]
    late_part, early_part, grad_in, narrow_sums, conv_sums, gain_sums = pl.pallas_call(
        functools.partial(inner_grad_kernel, seqs),
        grid=(turns,),
        in_specs=[spec for _, spec in arrays],
        out_specs=[spec for _, spec in results],
        out_shape=[value for value, _ in results],
        scratch_shapes=[pltpu.VMEM((block + rim, chans), F32)],
        compiler_params=pltpu.CompilerParams(vmem_limit_bytes=62 << 20),
    )(*[value for value, _ in arrays])
    late_part, mine_early = lax.optimization_barrier((late_part, mine_early))
    grad_xproj, grad_dt = narrow_sums[:, :x_cols], narrow_sums[:, x_cols : x_cols + R]
    conv_sums = jnp.sum(conv_sums.reshape(CONV_TAPS + 1, seqs, chans), 1)
    gain_grad1 = jnp.sum(gain_sums, 0)

    narrow_grads = jnp.concatenate(
        [
            grad_xproj,
            grad_dt,
            conv_sums.T,
            skip_grad[:, None],
            decay_grad.T,
            step_bias_grad[:, None],
        ],
        1,
    )
    routing_grads = jnp.concatenate([grad_router, gain_grad1[:, None], gain_grad2[:, None]], 1)
    if joined:
        narrow_grads = jnp.concatenate([narrow_grads, routing_grads], 1)
    wide_grads = jnp.concatenate(
        [grad_in, jnp.pad(narrow_grads, ((0, 0), (0, pad)))], 1
    )

    halves = [late_part, early_part]
    if peers == 2:
        exchanged = [swapped(part) for part in halves]
    else:
        exchanged = [lax.all_gather(part, "tensor") for part in halves]
    mine, exchanged = halved(wide_grads, exchanged)
    normed_parts = []
    for own, others in zip(halves, exchanged):
        if peers == 2:
            normed_parts.append([own, others])
        else:
            normed_parts.append([others[k] for k in range(peers)])
    late_parts, early_parts = normed_parts

    def rows_of(value):
        return value, pl.BlockSpec((block, value.shape[1]), lambda i: (i, 0))

    def early_rows(value):
        return value, pl.BlockSpec((block, width), lambda i: (jnp.minimum(i, turns // 2 - 1), 0))

    def late_rows(value):
        return value, pl.BlockSpec((block, width), lambda i: (jnp.maximum(i - turns // 2, 0), 0))

    arrays = (
        [early_rows(part) for part in early_parts]
        + [late_rows(part) for part in late_parts]
        + [
            rows_of(x_tok),
            rows_of(d_mixed),
            rows_of(act_half),
            (act_others, pl.BlockSpec((peers - 1, block, share), lambda i: (0, i, 0))),
            whole(gains[:1]),
        ]
    )
    out_spec = pl.BlockSpec((micros, group, steps, width), lambda i: (0, 0, i, 0))
    input_grad, activations = pl.pallas_call(
        functools.partial(output_kernel, (micros, group), peers),
        grid=(turns,),
        in_specs=[spec for _, spec in arrays],
        out_specs=[out_spec, out_spec],
        out_shape=[out(inputs.shape), out(inputs.shape, BF16)],
        scratch_shapes=[pltpu.VMEM((width // LANES, block, LANES), F32)] * 2,
        compiler_params=pltpu.CompilerParams(vmem_limit_bytes=62 << 20),
    )(*[value for value, _ in arrays])
    mine_tail = mine[:, width:]
    if joined:
        mine_routing = mine_tail[:, cuts[2] + 1 : cuts[2] + 1 + routing.shape[1]]
    else:
        mine_routing, _ = halved(routing_grads)
    gains_out = jnp.stack(
        [tensor_total(mine_routing[None, :, experts], F32)[0], mine_routing[:, experts + 1]]
    )
    return (
        activations,
        input_grad,
        gains_out,
        mine_routing[:, :experts],
        jnp.stack([mine[:, :width], mine_early[:, :width].astype(F32)]),
        mine_tail[:, : cuts[0]],
        mine_tail[:, cuts[0] : cuts[1]],
        mine_tail[:, cuts[2]],
        mine_tail[:, cuts[1] : cuts[2]],
        mine_early[:, width:].astype(F32),
        grad_up[None],
        grad_down[None],
    )


def solution(mesh):
    return jax.shard_map(
        per_device,
        mesh=mesh,
        in_specs=(
            P(None, "fsdp", "ctx", None),
            P(None, "fsdp", "ctx", None),
            P(None, "fsdp"),
            P(None, "fsdp", "ctx"),
            P(None, "fsdp", "ctx"),
            P(None, ("fsdp", "ctx")),
            P(("fsdp", "ctx"), None),
            P(None, ("fsdp", "ctx", "tensor"), None),
            P(("fsdp", "ctx", "tensor"), None),
            P(("fsdp", "ctx", "tensor"), None),
            P(("fsdp", "ctx", "tensor")),
            P(("fsdp", "ctx", "tensor"), None),
            P(("fsdp", "ctx", "tensor"), None),
            P(("fsdp", "ctx"), None, "tensor"),
            P(("fsdp", "ctx"), "tensor", None),
        ),
        out_specs=(
            P(None, "fsdp", "ctx", None),
            P(None, "fsdp", "ctx", None),
            P(None, ("fsdp", "ctx")),
            P(("fsdp", "ctx"), None),
            P(None, ("fsdp", "ctx", "tensor"), None),
            P(("fsdp", "ctx", "tensor"), None),
            P(("fsdp", "ctx", "tensor"), None),
            P(("fsdp", "ctx", "tensor")),
            P(("fsdp", "ctx", "tensor"), None),
            P(("fsdp", "ctx", "tensor"), None),
            P(("fsdp", "ctx"), None, "tensor"),
            P(("fsdp", "ctx"), "tensor", None),
        ),
        check_vma=False,
    )
```

```python
import functools

import jax
import jax.numpy as jnp
from jax import lax
from jax.experimental import pallas as pl
from jax.experimental.pallas import tpu as pltpu
from jax.sharding import PartitionSpec as P

N = 16
CONV_TAPS = 4
R = 48
EPS = 1e-05
VECTORS = CONV_TAPS + 2 + N + 1
BLK = 8
LANES = 128
F32 = jnp.float32
BF16 = jnp.bfloat16
OWNERS = ("fsdp", "ctx")


def silu_parts(value):
    sig = jax.nn.sigmoid(value)
    return value * sig, sig * (1.0 + value * (1.0 - sig))


def swapped(value):
    return lax.ppermute(value, "tensor", [(0, 1), (1, 0)])


def tensor_total(value, dtype):
    sent = value.astype(dtype)
    if lax.axis_size("tensor") == 2:
        return sent.astype(F32) + swapped(sent).astype(F32)
    return jnp.sum(lax.all_gather(sent, "tensor").astype(F32), axis=0)


def tensor_columns(value):
    if lax.axis_size("tensor") == 2:
        other = swapped(value)
        first = lax.axis_index("tensor") == 0
        return jnp.concatenate(
            [jnp.where(first, value, other), jnp.where(first, other, value)], -1
        )
    return lax.all_gather(value, "tensor", axis=value.ndim - 1, tiled=True)


def halved(value, beside=()):
    beside = list(beside)
    sizes = [lax.axis_size(axis) for axis in OWNERS]
    bits = [(axis, 1 << k) for axis, size in zip(OWNERS, sizes) for k in reversed(range(size.bit_length() - 1))]
    rows = value.shape[0] >> len(bits)
    for place in reversed(range(len(bits))):
        axis, bit = bits[place]
        view = value.reshape(1 << place, 2, rows, value.shape[-1])
        high = (lax.axis_index(axis) & bit) != 0
        own = jnp.where(high, view[:, 1], view[:, 0])
        other = jnp.where(high, view[:, 0], view[:, 1]).astype(BF16)
        got = lax.ppermute(other, axis, [(i, i ^ bit) for i in range(lax.axis_size(axis))])
        value = own.astype(F32) + got.astype(F32)
        turn = len(bits) - 1 - place
        if 0 < turn <= len(beside):
            turn -= 1
            value, beside[turn] = lax.optimization_barrier((value, beside[turn]))
    return value.reshape(rows, value.shape[-1]), beside


def moved(value, by):
    peers = lax.axis_size("ctx")
    pairs = [(i, i + by) for i in range(peers) if 0 <= i + by < peers]
    return lax.ppermute(value, "ctx", pairs)


TN = (((0,), (0,)), ((), ()))
NT = (((1,), (1,)), ((), ()))
NN = (((1,), (0,)), ((), ()))


def dot(a, b, dims=NN):
    return lax.dot_general(a, b, dims, preferred_element_type=F32)


MESH = pl.DeviceIdType.MESH


def greet(peers):
    barrier = pltpu.get_barrier_semaphore()
    for peer in peers:
        pl.semaphore_signal(barrier, inc=1, device_id=peer, device_id_type=MESH)
    pl.semaphore_wait(barrier, len(peers))


def carry_kernel(sign, ranges, peers, end_ref, log_ref, r_ref, *refs):
    if peers:
        own_ref, left_refs, right_refs = refs[0], refs[1:5:2], refs[2:5:2]
        out_ref, others_ref, products_ref = refs[5:8]
        sent, got, log_out, send_sem, recv_sem, own_sem, others_sem = refs[8:]
    else:
        out_ref, sent, got, log_out, send_sem, recv_sem = refs
    turns, groups, _, width = sent.shape
    seqs = log_ref.shape[0]
    fsdp, me, tensor = lax.axis_index("fsdp"), lax.axis_index("ctx"), lax.axis_index("tensor")

    def peer(by):
        return (fsdp, lax.rem(me + by + ranges, ranges), tensor)

    shifts = [sign * (1 << turn) for turn in range(turns)]
    partners = [(fsdp, me, lax.rem(tensor + by, peers)) for by in range(1, peers)]
    near = sorted({s % ranges for s in shifts} | {-s % ranges for s in shifts})
    greet([peer(by) for by in near] + partners)
    beside = [
        pltpu.make_async_remote_copy(
            src_ref=own_ref,
            dst_ref=others_ref.at[k],
            send_sem=own_sem.at[k],
            recv_sem=others_sem.at[k],
            device_id=partner,
            device_id_type=MESH,
        )
        for k, partner in enumerate(partners)
    ]
    for extra in beside:
        extra.start()

    def copy(turn, group):
        return pltpu.make_async_remote_copy(
            src_ref=sent.at[turn, group],
            dst_ref=got.at[turn, group],
            send_sem=send_sem.at[turn, group],
            recv_sem=recv_sem.at[turn, group],
            device_id=peer(shifts[turn]),
            device_id_type=MESH,
        )

    def decayed(log, cols, n):
        return jnp.exp(log * r_ref[n : n + 1, cols])

    def receive(turn, group):
        copy(turn, group).wait_recv()
        cols = slice(group * width, (group + 1) * width)
        reach = 1 << turn
        real = (me >= reach) if sign > 0 else (me < ranges - reach)

        def part(k):
            rows = got[turn, group, k * seqs : (k + 1) * seqs, :].astype(F32)
            return jnp.where(real, rows, 0.0)

        log = part(N) + part(N + 1)
        if turn == 0:
            for n in range(N):
                out_ref[n, :, cols] = part(n)
            log_out[:, cols] = log
        else:
            late = log_out[:, cols]
            for n in range(N):
                out_ref[n, :, cols] = out_ref[n, :, cols] + decayed(late, cols, n) * part(n)
            log_out[:, cols] = late + log

    def multiply(k):
        left, right = left_refs[k], right_refs[k]
        count = right.shape[1]

        def product(i, _):
            at = pl.ds(pl.multiple_of(i * LANES, LANES), LANES)
            value = dot(left[:, at], right[...], TN)
            products_ref[at, k * count : (k + 1) * count] = value.astype(BF16)
            return 0

        lax.fori_loop(0, left.shape[1] // LANES, product, 0)

    for turn in range(turns):
        if turn == turns - 1 and peers:
            multiply(0)
        for group in range(groups):
            cols = slice(group * width, (group + 1) * width)
            own_log = log_ref[:, cols]
            if turn > 0:
                receive(turn - 1, group)
            for n in range(0, N, 2):
                pair = []
                for k in (n, n + 1):
                    value = end_ref[k, :, cols]
                    if turn > 0:
                        value = value + decayed(own_log, cols, k) * out_ref[k, :, cols]
                    pair.append(value)
                sent[turn, group, n * seqs : (n + 2) * seqs, :] = jnp.concatenate(pair, 0).astype(
                    BF16
                )
            log = own_log if turn == 0 else own_log + log_out[:, cols]
            high = log.astype(BF16).astype(F32)
            sent[turn, group, N * seqs :, :] = jnp.concatenate([high, log - high], 0).astype(BF16)
            copy(turn, group).start()
    if peers:
        multiply(1)
    for group in range(groups):
        receive(turns - 1, group)
    for turn in range(turns):
        for group in range(groups):
            copy(turn, group).wait_send()
    for extra in beside:
        extra.wait()


def carried(end, log_decay, rates, sign, ident, shared=None, factors=()):
    _, seqs, chans = end.shape
    ranges = lax.axis_size("ctx")
    turns = (ranges - 1).bit_length()
    groups = 3 if chans % (3 * LANES) == 0 else 1
    block = (turns, groups, (N + 2) * seqs, chans // groups)
    vmem = pl.BlockSpec(memory_space=pltpu.VMEM)
    anywhere = pl.BlockSpec(memory_space=pl.ANY)
    peers = 0 if shared is None else lax.axis_size("tensor")
    state = jax.ShapeDtypeStruct((N, seqs, chans), F32)
    scratch = [
        pltpu.VMEM(block, BF16),
        pltpu.VMEM(block, BF16),
        pltpu.VMEM((seqs, chans), F32),
        pltpu.SemaphoreType.DMA((turns, groups)),
        pltpu.SemaphoreType.DMA((turns, groups)),
    ]
    if peers:
        others = jax.ShapeDtypeStruct((peers - 1, *shared.shape), shared.dtype)
        scratch += [pltpu.SemaphoreType.DMA((peers - 1,)), pltpu.SemaphoreType.DMA((peers - 1,))]
        products = jax.ShapeDtypeStruct(
            (factors[0].shape[1], factors[1].shape[1] + factors[3].shape[1]), BF16
        )
    return pl.pallas_call(
        functools.partial(carry_kernel, sign, ranges, peers),
        in_specs=[vmem] * 3 + ([anywhere] + [vmem] * len(factors) if peers else []),
        out_specs=[vmem, anywhere, vmem] if peers else vmem,
        out_shape=[state, others, products] if peers else state,
        scratch_shapes=scratch,
        compiler_params=pltpu.CompilerParams(
            collective_id=ident, has_side_effects=True, vmem_limit_bytes=48 << 20
        ),
        cost_estimate=pl.CostEstimate(flops=20 << 30, bytes_accessed=1 << 20, transcendentals=0),
    )(end[:N], log_decay, rates, *([shared, *factors] if peers else []))


def spread_matrix():
    rows = lax.broadcasted_iota(jnp.int32, (2 * N, N * LANES), 0) % N
    cols = lax.broadcasted_iota(jnp.int32, (2 * N, N * LANES), 1) // LANES
    return (rows == cols).astype(F32).astype(BF16)


def spread_into(pairs, rows):
    def turn(i, _):
        matrix = spread_matrix()
        at = pl.ds(pl.multiple_of(i * LANES, LANES), LANES)
        for source, target in pairs:
            value = source[at, :]
            high = value.astype(BF16)
            low = (value - high.astype(F32)).astype(BF16)
            target[at, :] = jnp.dot(
                jnp.concatenate([high, low], 1), matrix, preferred_element_type=F32
            )
        return 0

    lax.fori_loop(0, rows // LANES, turn, 0)


def lanes(k):
    return slice(k * LANES, (k + 1) * LANES)


def end_state_kernel(d_ref, u_ref, b_ref, r_ref, end_ref, rb, bb):
    rows, width = d_ref.shape
    seqs = rb.shape[1]
    length = rows // seqs
    parts = width // LANES
    for n in range(N):
        rb[n] = jnp.broadcast_to(r_ref[n : n + 1, :], (seqs, width))

    @pl.when(pl.program_id(0) == 0)
    def _():
        spread_into([(b_ref, bb)], rows)

    def body(t, carry):
        hs, total = carry
        row = pl.ds(pl.multiple_of(t * seqs, seqs), seqs)
        d = d_ref[row, :]
        du = d * u_ref[row, :]
        new = []
        for n in range(N):
            bn = bb[row, lanes(n)]
            for k in range(parts):
                a = jnp.exp(d[:, lanes(k)] * rb[n, :, lanes(k)])
                new.append(a * hs[n * parts + k] + du[:, lanes(k)] * bn)
        return tuple(new), total + d

    zero = jnp.zeros((seqs, LANES), F32)
    hs, total = lax.fori_loop(
        0, length, body, ((zero,) * (N * parts), jnp.zeros((seqs, width), F32)), unroll=8
    )
    for n in range(N):
        for k in range(parts):
            end_ref[n, :, lanes(k)] = hs[n * parts + k]
    end_ref[N] = total


def forward_kernel(
    peers,
    d_ref,
    u_ref,
    z_ref,
    b_ref,
    c_ref,
    r_ref,
    skip_ref,
    w_ref,
    h0_ref,
    x_ref,
    y_ref,
    gated_ref,
    st_ref,
    resid_ref,
    rb,
    bb,
    cb,
    state,
    total,
    sent,
    got,
    send_sem,
    recv_sem,
):
    rows, width = d_ref.shape
    seqs = rb.shape[1]
    length = rows // seqs
    parts = width // LANES
    piece, group = pl.program_id(0), pl.program_id(1)
    pieces, last = pl.num_programs(0), pl.num_programs(1) - 1
    fsdp, ctx, tensor = lax.axis_index("fsdp"), lax.axis_index("ctx"), lax.axis_index("tensor")
    partners = [(fsdp, ctx, lax.rem(tensor + by, peers)) for by in range(1, peers)]

    def copy(k, which):
        return pltpu.make_async_remote_copy(
            src_ref=sent.at[which],
            dst_ref=got.at[k, which],
            send_sem=send_sem.at[k, which],
            recv_sem=recv_sem.at[k, which],
            device_id=partners[k],
            device_id_type=MESH,
        )

    @pl.when((piece == 0) & (group == 0))
    def _():
        greet(partners)

    for n in range(N):
        rb[n] = jnp.broadcast_to(r_ref[n : n + 1, :], (seqs, width))

    @pl.when(group == 0)
    def _():
        spread_into([(b_ref, bb), (c_ref, cb)], rows)
        total[...] = jnp.zeros_like(total)

    @pl.when(piece == 0)
    def _():
        state[group] = h0_ref[...]

    def block(i, hs):
        for n in range(N):
            for k in range(parts):
                st_ref[i, n, :, lanes(k)] = hs[n * parts + k]

        def body(step, hs):
            t = i * BLK + step
            row = pl.ds(pl.multiple_of(t * seqs, seqs), seqs)
            d = d_ref[row, :]
            u = u_ref[row, :]
            du = d * u
            ys = [u[:, lanes(k)] * skip_ref[:, lanes(k)] for k in range(parts)]
            new = []
            for n in range(N):
                bn = bb[row, lanes(n)]
                cn = cb[row, lanes(n)]
                for k in range(parts):
                    a = jnp.exp(d[:, lanes(k)] * rb[n, :, lanes(k)])
                    h = a * hs[n * parts + k] + du[:, lanes(k)] * bn
                    ys[k] = ys[k] + h * cn
                    new.append(h)
            for k in range(parts):
                y_ref[row, lanes(k)] = ys[k]
            return tuple(new)

        return lax.fori_loop(0, BLK, body, hs, unroll=8)

    hs = lax.fori_loop(
        0,
        length // BLK,
        block,
        tuple(state[group, n, :, lanes(k)] for n in range(N) for k in range(parts)),
    )
    for n in range(N):
        for k in range(parts):
            state[group, n, :, lanes(k)] = hs[n * parts + k]
    z = z_ref[...]
    gated = (y_ref[...] * (z * jax.nn.sigmoid(z))).astype(BF16)
    gated_ref[...] = gated
    total[...] += jnp.dot(gated, w_ref[...], preferred_element_type=F32)

    def add(which):
        for k in range(peers - 1):
            copy(k, which).wait_recv()
        at = pl.ds(pl.multiple_of(which * rows, rows), rows)
        value = x_ref[at, :].astype(F32)
        own = sent[which].astype(F32)
        if peers == 2:
            value = value + (own + got[0, which].astype(F32))
        else:
            for owner in range(peers):
                term = own
                for k in range(peers - 1):
                    here = lax.rem(tensor + peers - k - 1, peers) == owner
                    term = jnp.where(here, got[k, which].astype(F32), term)
                value = value + term
        resid_ref[at, :] = value

    @pl.when(group == last)
    def _():
        sent[piece] = total[...].astype(BF16)
        for k in range(peers - 1):
            copy(k, piece).start()

        @pl.when(piece > 1)
        def _():
            add(piece - 2)

    @pl.when((group == last) & (piece == pieces - 1))
    def _():
        count = sent.shape[0]
        for which in range(max(count - 2, 0), count):
            add(which)
        for which in range(count):
            for k in range(peers - 1):
                copy(k, which).wait_send()


def start_grad_kernel(d_ref, dy_ref, c_ref, r_ref, g_ref, rb, cb):
    rows, width = d_ref.shape
    seqs = rb.shape[1]
    length = rows // seqs
    parts = width // LANES
    for n in range(N):
        rb[n] = jnp.broadcast_to(r_ref[n : n + 1, :], (seqs, width))

    @pl.when(pl.program_id(0) == 0)
    def _():
        spread_into([(c_ref, cb)], rows)

    def body(i, gs):
        t = length - 1 - i
        row = pl.ds(pl.multiple_of(t * seqs, seqs), seqs)
        d = d_ref[row, :]
        dy = dy_ref[row, :]
        new = []
        for n in range(N):
            cn = cb[row, lanes(n)]
            for k in range(parts):
                a = jnp.exp(d[:, lanes(k)] * rb[n, :, lanes(k)])
                new.append(a * (gs[n * parts + k] + dy[:, lanes(k)] * cn))
        return tuple(new)

    zero = jnp.zeros((seqs, LANES), F32)
    gs = lax.fori_loop(0, length, body, (zero,) * (N * parts), unroll=8)
    for n in range(N):
        for k in range(parts):
            g_ref[n, :, lanes(k)] = gs[n * parts + k]


def backward_kernel(
    d_ref,
    u_ref,
    dy_ref,
    sig_ref,
    b_ref,
    c_ref,
    r_ref,
    skip_ref,
    w_ref,
    st_ref,
    g0_ref,
    dstep_ref,
    du_ref,
    dproj_ref,
    rg_ref,
    bias_ref,
    skipg_ref,
    rb,
    bb,
    cb,
    hb,
    ab,
    pb,
    pc,
    dsb,
    total,
    columns,
):
    rows, width = d_ref.shape
    seqs = rb.shape[1]
    length = rows // seqs
    parts = width // LANES
    group = pl.program_id(0)
    for n in range(N):
        rb[n] = jnp.broadcast_to(r_ref[n : n + 1, :], (seqs, width))

    @pl.when(group == 0)
    def _():
        spread_into([(b_ref, bb), (c_ref, cb)], rows)
        total[...] = jnp.zeros_like(total)
        source = lax.broadcasted_iota(jnp.int32, columns.shape, 0) // LANES
        target = lax.broadcasted_iota(jnp.int32, columns.shape, 1)
        columns[...] = (source + R == target).astype(F32).astype(BF16)

    rg_ref[...] = jnp.zeros_like(rg_ref)
    bias_ref[...] = jnp.zeros_like(bias_ref)
    skipg_ref[...] = jnp.zeros_like(skipg_ref)

    def block(turn, gs):
        i = length // BLK - 1 - turn

        def again(step, hs):
            t = i * BLK + step
            row = pl.ds(pl.multiple_of(t * seqs, seqs), seqs)
            d = d_ref[row, :]
            du = d * u_ref[row, :]
            new = []
            for n in range(N):
                bn = bb[row, lanes(n)]
                for k in range(parts):
                    a = jnp.exp(d[:, lanes(k)] * rb[n, :, lanes(k)])
                    h = a * hs[n * parts + k] + du[:, lanes(k)] * bn
                    ab[step, n, :, lanes(k)] = a
                    hb[step + 1, n, :, lanes(k)] = h
                    new.append(h)
            return tuple(new)

        hs = tuple(st_ref[i, n, :, lanes(k)] for n in range(N) for k in range(parts))
        for n in range(N):
            for k in range(parts):
                hb[0, n, :, lanes(k)] = hs[n * parts + k]
        lax.fori_loop(0, BLK, again, hs, unroll=4)

        def back(turn, gs):
            step = BLK - 1 - turn
            t = i * BLK + step
            row = pl.ds(pl.multiple_of(t * seqs, seqs), seqs)
            here = pl.ds(pl.multiple_of(step * seqs, seqs), seqs)
            d = d_ref[row, :]
            u = u_ref[row, :]
            dy = dy_ref[row, :]
            du = d * u
            prods = [jnp.zeros((seqs, LANES), F32) for _ in range(parts)]
            steps = [jnp.zeros((seqs, LANES), F32) for _ in range(parts)]
            new = []
            for n in range(N):
                bn = bb[row, lanes(n)]
                cn = cb[row, lanes(n)]
                b_sum = c_sum = None
                for k in range(parts):
                    g = gs[n * parts + k] + cn * dy[:, lanes(k)]
                    c_term = hb[step + 1, n, :, lanes(k)] * dy[:, lanes(k)]
                    b_term = g * du[:, lanes(k)]
                    c_sum = c_term if k == 0 else c_sum + c_term
                    b_sum = b_term if k == 0 else b_sum + b_term
                    prods[k] = prods[k] + g * bn
                    carried_g = g * ab[step, n, :, lanes(k)]
                    decay_g = carried_g * hb[step, n, :, lanes(k)]
                    steps[k] = steps[k] + decay_g * rb[n, :, lanes(k)]
                    rg_ref[n, :, lanes(k)] = rg_ref[n, :, lanes(k)] + decay_g * d[:, lanes(k)]
                    new.append(carried_g)
                pb[here, lanes(n)] = b_sum
                pc[here, lanes(n)] = c_sum
            skipg_ref[...] += dy * u
            for k in range(parts):
                dsb[here, lanes(k)] = steps[k] + prods[k] * u[:, lanes(k)]
                du_ref[row, lanes(k)] = (
                    prods[k] * d[:, lanes(k)] + dy[:, lanes(k)] * skip_ref[:, lanes(k)]
                )
            return tuple(new)

        gs = lax.fori_loop(0, BLK, back, gs, unroll=4)
        at = pl.ds(pl.multiple_of(i * BLK * seqs, BLK * seqs), BLK * seqs)
        d_step = (dsb[...] * sig_ref[at, :]).astype(BF16)
        dstep_ref[at, :] = d_step
        bias_ref[...] += jnp.sum(d_step.astype(F32).reshape(BLK, seqs, width), 0)
        total[at, :] += (
            jnp.dot(d_step, w_ref[...], preferred_element_type=F32)
            + jnp.dot(pb[...].astype(BF16), columns[: N * LANES], preferred_element_type=F32)
            + jnp.dot(pc[...].astype(BF16), columns[N * LANES :], preferred_element_type=F32)
        )
        return gs

    lax.fori_loop(
        0,
        length // BLK,
        block,
        tuple(g0_ref[n, :, lanes(k)] for n in range(N) for k in range(parts)),
    )

    @pl.when(group == pl.num_programs(0) - 1)
    def _():
        dproj_ref[...] = total[...].astype(BF16)


def normalized(x):
    return x * lax.rsqrt(jnp.mean(x * x, -1, keepdims=True) + EPS)


def inner_grad_step(seqs, refs, x, sums, dconv):
    (
        du_ref,
        dproj_ref,
        conv_ref,
        ext_ref,
        normed_ref,
        u_ref,
        rank_ref,
        dstep_ref,
        dgate_ref,
        w_in_ref,
        w_gate_ref,
        w_x_ref,
        taps_ref,
        after_ref,
    ) = refs
    gin_ref, narrow_ref, chan_ref, gain_ref = sums
    rows, chans = du_ref.shape
    rim = (CONV_TAPS - 1) * seqs
    turn = pl.program_id(0)
    first = pl.multiple_of((pl.num_programs(0) - 1 - turn) * rows, rows)

    @pl.when(turn == 0)
    def _():
        for ref in sums:
            ref[...] = jnp.zeros_like(ref)
        dconv[rows:, :] = after_ref[...]

    @pl.when(turn > 0)
    def _():
        dconv[rows:, :] = dconv[:rim, :]

    def by_seq(value):
        return jnp.sum(value.reshape(rows // seqs, seqs, value.shape[-1]), 0)

    d_proj = dproj_ref[...]
    conv = conv_ref[...]
    sig = jax.nn.sigmoid(conv)
    d_conv = (du_ref[...] + dot(d_proj, w_x_ref[...], NT)) * (sig * (1.0 + conv * (1.0 - sig)))
    dconv[:rows, :] = d_conv
    d_inner = jnp.zeros_like(d_conv)
    for tap in range(CONV_TAPS):
        at = (CONV_TAPS - 1 - tap) * seqs
        d_inner = d_inner + taps_ref[tap : tap + 1, :] * dconv[at : at + rows, :]
        ext = ext_ref[pl.ds(pl.multiple_of(first + tap * seqs, seqs), rows), :]
        chan_ref[tap * seqs : (tap + 1) * seqs, :] += by_seq(d_conv * ext)
    chan_ref[CONV_TAPS * seqs :, :] += by_seq(d_conv)
    d_inner = d_inner.astype(BF16)
    part = dot(d_inner, w_in_ref[...]) + dot(dgate_ref[...], w_gate_ref[...])
    gain_ref[...] += by_seq(part * normalized(x.astype(F32)))
    gin_ref[...] += dot(d_inner, normed_ref[...], TN)
    narrow = dot(u_ref[...], d_proj, TN) + dot(dstep_ref[...], rank_ref[...], TN)
    narrow_ref[...] = narrow_ref[...] + narrow
    return part


def inner_grad_kernel(seqs, *refs):
    refs, x_ref, late_ref, early_ref, sums, dconv = (
        refs[:14],
        refs[14],
        refs[15],
        refs[16],
        refs[17:21],
        refs[21],
    )
    part = inner_grad_step(seqs, refs, x_ref[...], sums, dconv).astype(BF16)
    turn, half = pl.program_id(0), pl.num_programs(0) // 2

    @pl.when(turn < half)
    def _():
        late_ref[...] = part

    @pl.when(turn >= half)
    def _():
        early_ref[...] = part


def finish_kernel(shape, sizes, turns, *refs):
    micros, group = shape
    seqs = micros * group
    step_refs, refs = refs[:14], refs[14:]
    x_ref, dres_ref, act_own_ref, act_got_ref, g_ref, vec_ref, routing_ref, early_ref = refs[:8]
    grad_ref, act_ref, in_ref, out_ref, proj_ref, step_ref, channel_ref, route_ref, tail_ref = refs[
        8:17
    ]
    refs = refs[7:]
    sums, dconv, sent, got, gain_got, tail, grad_tok, act_tok = (
        refs[10:14],
        refs[14],
        refs[15],
        refs[16],
        refs[17],
        refs[18],
        refs[19],
        refs[20],
    )
    mine_ref = refs[21]
    refs = refs[22:]
    bits = [("ctx", 1 << k) for k in range(sizes[1].bit_length() - 1)]
    bits += [("fsdp", 1 << k) for k in range(sizes[0].bit_length() - 1)]
    stages = len(bits)
    sends, gots = refs[:stages], refs[stages : 2 * stages]
    part_sems, gain_sems, sum_sems = (
        refs[2 * stages : 2 * stages + 2],
        refs[2 * stages + 2 : 2 * stages + 4],
        refs[2 * stages + 4 : 2 * stages + 6],
    )
    where = {axis: lax.axis_index(axis) for axis in ("fsdp", "ctx", "tensor")}
    across = (where["fsdp"], where["ctx"], 1 - where["tensor"])
    high = [lax.rem(where[axis] // bit, 2) for axis, bit in bits]
    partners = []
    for (axis, bit), one in zip(bits, high):
        to = dict(where)
        to[axis] = where[axis] + bit - 2 * bit * one
        partners.append((to["fsdp"], to["ctx"], to["tensor"]))

    def remote(src, dst, sems, at, to):
        return pltpu.make_async_remote_copy(
            src_ref=src,
            dst_ref=dst,
            send_sem=sems[0].at[at],
            recv_sem=sems[1].at[at],
            device_id=to,
            device_id_type=MESH,
        )

    blocks = [pl.ds(0, 1), pl.ds(1, turns - 2), pl.ds(turns - 1, 1)]

    def part_copy(which):
        at = blocks[which]
        return remote(sent.at[at], got.at[at], part_sems, which, across)

    def sum_copy(stage, half):
        source = sends[stage].at[half, 1 - high[stage]]
        return remote(source, gots[stage].at[half], sum_sems, (stage, half), partners[stage])

    turn = pl.program_id(0)

    @pl.when(turn == 0)
    def _():
        greet([across] + partners)

    rows = step_refs[0].shape[0]
    first = pl.multiple_of((turns - 1 - turn) * rows, rows)
    part = inner_grad_step(seqs, step_refs, x_ref[pl.ds(first, rows), :], sums, dconv)
    sent[turn] = part.astype(BF16)

    @pl.when(turn == 0)
    def _():
        part_copy(0).start()

    @pl.when(turn == turns - 2)
    def _():
        part_copy(0).wait_send()
        part_copy(1).start()


    def output(which):
        at = slice((turns - 1 - which) * rows, (turns - which) * rows)
        x = x_ref[at, :].astype(F32)
        width = x.shape[1]
        scale = lax.rsqrt(jnp.mean(x * x, -1, keepdims=True) + EPS)
        xhat = x * scale
        scaled = g_ref[...] * (sent[which].astype(F32) + got[which].astype(F32))
        mean = jnp.mean(scaled * xhat, -1, keepdims=True)
        grad = dres_ref[at, :].astype(F32) + scale * (scaled - xhat * mean)
        own, other = act_own_ref[at, :].astype(F32), act_got_ref[0, at, :].astype(F32)
        left = where["tensor"] == 0
        act = jnp.concatenate([jnp.where(left, own, other), jnp.where(left, other, own)], 1)
        count = rows // seqs
        times = slice((turns - 1 - which) * count, (turns - which) * count)
        for k in range(width // LANES):
            grad_tok[k] = grad[:, lanes(k)]
            act_tok[k] = act[:, lanes(k)]
        for m in range(micros):
            for g in range(group):
                every = pl.ds(m * group + g, count, stride=seqs)
                for k in range(width // LANES):
                    grad_ref[m, g, times, lanes(k)] = grad_tok[k, every, :]
                    act_ref[m, g, times, lanes(k)] = act_tok[k, every, :].astype(BF16)

    @pl.when(turn == turns - 1)
    def _():
        gin_ref, narrow_ref, chan_ref, gain_ref = sums
        gain_copy = remote(gain_ref, gain_got, gain_sems, 0, across)
        gain_copy.start()
        owned = mine_ref.shape[0]
        half_cols = mine_ref.shape[1] // 2
        rest = gin_ref.shape[1] - half_cols

        def fill(stage, half):
            count = 1 << (stages - stage)
            for k in range(count):
                target = (half, k % 2, k // 2)
                if stage > 0:
                    before = (half, high[stage - 1], k)
                    value = sends[stage - 1][before].astype(F32)
                    value = value + gots[stage - 1][half, k].astype(F32)
                    sends[stage][target] = value.astype(BF16)
                    continue
                at = slice(k * owned, (k + 1) * owned)
                if half == 0:
                    sends[0][target] = gin_ref[at, :half_cols].astype(BF16)
                else:
                    joined = [gin_ref[at, half_cols:], narrow_ref[at, :], tail[at, :]]
                    sends[0][target] = jnp.concatenate(joined, 1).astype(BF16)
            sum_copy(stage, half).start()

        fill(0, 0)
        gain_copy.wait()
        vec = vec_ref[...]
        row = lax.broadcasted_iota(jnp.int32, vec.shape, 0)
        for k in range(CONV_TAPS + 1):
            value = jnp.sum(chan_ref[k * seqs : (k + 1) * seqs, :], 0, keepdims=True)
            vec = jnp.where(row == k, value, vec)
        gain = jnp.sum(gain_ref[...] + gain_got[...], 0, keepdims=True)
        vec = jnp.where(row == VECTORS, gain, vec)
        tail[...] = vec.T + routing_ref[...]
        fill(0, 1)
        part_copy(0).wait_recv()
        output(0)
        for stage in range(1, stages):
            for half in range(2):
                sum_copy(stage - 1, half).wait_recv()
                fill(stage, half)
            if stage == 1:
                part_copy(1).wait()
                part_copy(2).start()
            if stage < turns - 1:
                output(stage)
        for which in range(stages, turns - 1):
            output(which)
        part_copy(2).wait_recv()
        output(turns - 1)
        for half in range(2):
            sum_copy(stages - 1, half).wait_recv()
            value = sends[stages - 1][half, high[stages - 1], 0].astype(F32)
            mine_ref[:, half * half_cols : (half + 1) * half_cols] = value + gots[stages - 1][
                half, 0
            ].astype(F32)
        width, cols = in_ref.shape[2], proj_ref.shape[1]
        in_ref[0] = mine_ref[:, :width]
        in_ref[1] = early_ref[:, :width].astype(F32)
        out_ref[...] = early_ref[:, width:].astype(F32)
        proj_ref[...] = mine_ref[:, width : width + cols]
        step_ref[...] = mine_ref[:, width + cols : width + cols + R]
        at = width + LANES
        channel_ref[...] = mine_ref[:, at : at + VECTORS - 1]
        at += VECTORS + 1
        route_ref[...] = mine_ref[:, at : at + route_ref.shape[1]]
        tail_ref[...] = mine_ref[:, width + LANES :]
        for stage in range(stages):
            for half in range(2):
                sum_copy(stage, half).wait_send()
        part_copy(2).wait_send()


def output_kernel(shape, peers, *refs):
    micros, group = shape
    early, late, refs = refs[:peers], refs[peers : 2 * peers], refs[2 * peers :]
    x_ref, dres_ref, act_own_ref, act_others_ref, gain_ref, grad_ref, act_ref, grad_tok, act_tok = refs
    x = x_ref[...].astype(F32)
    scale = lax.rsqrt(jnp.mean(x * x, -1, keepdims=True) + EPS)
    xhat = x * scale
    is_early = pl.program_id(0) < pl.num_programs(0) // 2
    d_normed = jnp.zeros_like(x)
    for first, second in zip(early, late):
        d_normed = d_normed + jnp.where(is_early, first[...], second[...]).astype(F32)
    scaled = gain_ref[...] * d_normed
    mean = jnp.mean(scaled * xhat, -1, keepdims=True)
    grad = dres_ref[...].astype(F32) + scale * (scaled - xhat * mean)
    seqs = micros * group
    rows, width = x.shape
    count = rows // seqs
    tensor = lax.axis_index("tensor")
    pieces = []
    for owner in range(peers):
        piece = act_own_ref[...].astype(F32)
        for by in range(1, peers):
            here = lax.rem(tensor + peers - by, peers) == owner
            piece = jnp.where(here, act_others_ref[by - 1].astype(F32), piece)
        pieces.append(piece)
    act = jnp.concatenate(pieces, 1)
    for k in range(width // LANES):
        grad_tok[k] = grad[:, lanes(k)]
        act_tok[k] = act[:, lanes(k)]
    for m in range(micros):
        for g in range(group):
            at = pl.ds(m * group + g, count, stride=seqs)
            for k in range(width // LANES):
                grad_ref[m, g, :, lanes(k)] = grad_tok[k, at, :]
                act_ref[m, g, :, lanes(k)] = act_tok[k, at, :].astype(BF16)


def scan_call(kernel, arrays, outs, scratch, width, chans, chunk=0, cost=None):
    def spec(shape, kind):
        def place(j, rank=len(shape)):
            at = [0] * rank
            if "t" in kind:
                at[0] = chunk
            if "c" in kind:
                at[-1] = j
            if "r" in kind:
                at[0] = j
            return tuple(at)

        return pl.BlockSpec(shape, place)

    return pl.pallas_call(
        kernel,
        grid=(chans // width,),
        in_specs=[spec(shape, kind) for _, shape, kind in arrays],
        out_specs=[spec(shape, kind) for _, shape, kind in outs],
        out_shape=[a for a, _, _ in outs],
        scratch_shapes=[
            s if not isinstance(s, tuple) else pltpu.VMEM(s, F32) for s in scratch
        ],
        compiler_params=pltpu.CompilerParams(vmem_limit_bytes=62 << 20),
        cost_estimate=cost,
    )(*[a for a, _, _ in arrays])


def per_device(
    inputs,
    out_grad,
    lengths,
    routes,
    slots,
    norm_gains,
    router_matrix,
    input_projection,
    inner_projection,
    step_projection,
    step_bias,
    channel_params,
    output_projection,
    expert_up,
    expert_down,
):
    micros, group, length, width = inputs.shape
    seqs = micros * group
    tokens = length * seqs
    owners = lax.axis_size("fsdp") * lax.axis_size("ctx")
    experts = router_matrix.shape[1]
    capacity = max(2, (25 * group * length + 32 * experts - 1) // (32 * experts))
    slots_each = micros * capacity
    rows = experts * slots_each

    def by_token(value):
        return jnp.moveaxis(value, 2, 0).reshape(tokens, *value.shape[3:])

    narrow = jnp.concatenate(
        [inner_projection, step_projection, channel_params, step_bias[:, None]], 1
    )
    x_cols = inner_projection.shape[1]
    cuts = [x_cols, x_cols + R, x_cols + R + channel_params.shape[1]]
    routing = jnp.concatenate([router_matrix, norm_gains.T], 1)
    joined = narrow.shape[0] == routing.shape[0]
    if joined:
        narrow = jnp.concatenate([narrow, routing], 1)
    narrow_cols = narrow.shape[1]
    pad = -narrow_cols % LANES
    first = jnp.concatenate([input_projection[0], jnp.pad(narrow, ((0, 0), (0, pad)))], 1)
    later = jnp.concatenate([input_projection[1], output_projection], 1)
    full = lax.all_gather(first, OWNERS, axis=0, tiled=True)
    later_full = lax.all_gather(later, OWNERS, axis=0, tiled=True)

    position = lax.axis_index("ctx") * length + jnp.arange(length)
    valid = (position[:, None] < lengths.reshape(1, seqs)).astype(F32).reshape(tokens, 1)
    route = by_token(routes)
    slot = by_token(slots)
    kept = slot >= 0
    kept_f = kept.astype(F32)
    micro_of = (jnp.arange(tokens) // group) % micros
    place = jnp.where(kept, route * slots_each + micro_of * capacity + slot, -1)
    pick = (
        jnp.arange(rows).reshape(experts, slots_each, 1) == place[None, None, :]
    ).astype(BF16)
    grad_tok = by_token(out_grad)
    grad_act = grad_tok.astype(F32) * valid

    def packed(value):
        return jnp.einsum("est,td->esd", pick, value, preferred_element_type=F32).astype(BF16)

    def unpacked(value):
        flat = value.reshape(rows, value.shape[-1])
        return lax.optimization_barrier(dot(pick.reshape(rows, tokens), flat, TN))

    def swap_owners(value):
        return lax.all_to_all(value, OWNERS, split_axis=0, concat_axis=0, tiled=True)

    full, grad_packed = lax.optimization_barrier((full, packed(grad_tok)))
    grad_rows_raw = swap_owners(grad_packed)

    w_in = full[:, :width]
    tail = full[:, width:]
    w_gate, w_out = later_full[:, :width], later_full[:, width:]
    w_x = tail[:, : cuts[0]]
    w_step = tail[:, cuts[0] : cuts[1]]
    channel_f = tail[:, cuts[1] : cuts[2]].astype(F32)
    bias_f = tail[:, cuts[2]].astype(F32)
    if joined:
        full_routing = tail[:, cuts[2] + 1 : cuts[2] + 1 + routing.shape[1]]
    else:
        full_routing = lax.all_gather(routing, OWNERS, axis=0, tiled=True)
    w_router = full_routing[:, :experts]
    gains = full_routing[:, experts:].T.astype(F32)
    chans = channel_f.shape[0]
    taps = channel_f[:, :CONV_TAPS].T
    conv_bias = channel_f[:, CONV_TAPS]
    skip = channel_f[:, CONV_TAPS + 1]
    rates = -jnp.exp(channel_f[:, CONV_TAPS + 2 :]).T

    x_tok = lax.optimization_barrier(by_token(inputs))
    x = x_tok.astype(F32)
    normed1 = (normalized(x) * gains[0]).astype(BF16)
    inner = dot(normed1, w_in, NT).astype(BF16)
    rim = (CONV_TAPS - 1) * seqs
    before = moved(inner[tokens - rim :], 1)
    gate_z = dot(normed1, w_gate, NT)
    extended = jnp.concatenate([before, inner], 0).astype(F32)
    conv = conv_bias
    for tap in range(CONV_TAPS):
        conv = conv + taps[tap] * extended[tap * seqs : tap * seqs + tokens]
    u = jax.nn.silu(conv).astype(BF16)
    u_wide = u.astype(F32)
    proj = tensor_total(dot(u, w_x), BF16)
    rank = proj[:, :R].astype(BF16)
    b_vals = proj[:, R : R + N]
    c_vals = proj[:, R + N :]
    step_pre = dot(rank, w_step, NT) + bias_f
    delta = jax.nn.softplus(step_pre)
    lane_width = 2 * LANES if chans % (2 * LANES) == 0 else LANES
    wide_rates = (N, seqs, lane_width)
    state_block = (N, seqs, lane_width)
    call = functools.partial(scan_call, width=lane_width, chans=chans)

    def both_in(value, steps=length):
        return (value, (steps * seqs, lane_width), "tc")

    def by_chan(value):
        return (value, (*value.shape[:-1], lane_width), "c")

    def by_rows(value, steps=length):
        return (value, (steps * seqs, value.shape[1]), "t")

    def cost(steps, ops):
        elements = steps * seqs * chans * N
        return pl.CostEstimate(flops=300 * ops * elements, bytes_accessed=elements, transcendentals=0)

    def out(shape, dtype=F32):
        return jax.ShapeDtypeStruct(shape, dtype)

    [end] = call(
        end_state_kernel,
        [both_in(delta), both_in(u_wide), by_rows(b_vals), by_chan(rates)],
        [by_chan(out((N + 1, seqs, chans)))],
        [wide_rates, (tokens, N * LANES)],
        cost=cost(length, 6),
    )
    end, grad_rows_raw = lax.optimization_barrier((end, grad_rows_raw))
    log_decay = end[N]
    state = carried(end, log_decay, rates, 1, 0)
    pieces = 4 if length % (4 * BLK) == 0 else 1
    steps = length // pieces
    block = steps * seqs
    groups = chans // lane_width
    peers, here = lax.axis_size("tensor"), lax.axis_index("tensor")

    def cut(value, *shape):
        return value, pl.BlockSpec(shape, lambda p, j: (p, j))

    def by_piece(value):
        return value, pl.BlockSpec((block, value.shape[1]), lambda p, j: (p, 0))

    def by_group(value):
        rank = value.ndim - 1
        return value, pl.BlockSpec(
            (*value.shape[:-1], lane_width), lambda p, j: (0,) * rank + (j,)
        )

    arrays = [
        cut(delta, block, lane_width),
        cut(u_wide, block, lane_width),
        cut(gate_z, block, lane_width),
        by_piece(b_vals),
        by_piece(c_vals),
        by_group(rates),
        by_group(skip[None]),
        (later_full, pl.BlockSpec((lane_width, width), lambda p, j: (j, 1))),
        by_group(state),
        (x_tok, pl.BlockSpec((tokens, width), lambda p, j: (0, 0))),
    ]
    results = [
        cut(out((tokens, chans)), block, lane_width),
        cut(out((tokens, chans), BF16), block, lane_width),
        (
            out((length // BLK, N, seqs, chans)),
            pl.BlockSpec((steps // BLK, N, seqs, lane_width), lambda p, j: (p, 0, 0, j)),
        ),
        (out((tokens, width)), pl.BlockSpec((tokens, width), lambda p, j: (0, 0))),
    ]
    y_vals, gated, starts, resid = pl.pallas_call(
        functools.partial(forward_kernel, peers),
        grid=(pieces, groups),
        in_specs=[spec for _, spec in arrays],
        out_specs=[spec for _, spec in results],
        out_shape=[value for value, _ in results],
        scratch_shapes=[
            pltpu.VMEM(wide_rates, F32),
            pltpu.VMEM((block, N * LANES), F32),
            pltpu.VMEM((block, N * LANES), F32),
            pltpu.VMEM((groups, *state_block), F32),
            pltpu.VMEM((block, width), F32),
            pltpu.VMEM((pieces, block, width), BF16),
            pltpu.VMEM((peers - 1, pieces, block, width), BF16),
            pltpu.SemaphoreType.DMA((peers - 1, pieces)),
            pltpu.SemaphoreType.DMA((peers - 1, pieces)),
        ],
        compiler_params=pltpu.CompilerParams(
            collective_id=2, has_side_effects=True, vmem_limit_bytes=62 << 20
        ),
        cost_estimate=cost(length, 10),
    )(*[value for value, _ in arrays])
    silu_z, gate_slope = silu_parts(gate_z)

    scale2 = lax.rsqrt(jnp.mean(resid * resid, -1, keepdims=True) + EPS)
    xhat2 = resid * scale2
    normed2 = (xhat2 * gains[1]).astype(BF16)
    probs = jax.nn.softmax(dot(normed2, w_router), -1)
    onehot = (route[:, None] == jnp.arange(experts)).astype(F32)
    gate = jnp.sum(probs * onehot, -1, keepdims=True) * kept_f[:, None]
    share = width // peers

    def half(value):
        cut = value[..., :share]
        for peer in range(1, peers):
            cut = jnp.where(here == peer, value[..., peer * share : (peer + 1) * share], cut)
        return cut

    x_rows = tensor_columns(swap_owners(packed(half(normed2))))
    gate_rows = swap_owners(
        jnp.sum(jnp.where(pick > 0, gate[:, 0], 0.0), -1)[:, None, :]
    )
    grad_rows = (jnp.swapaxes(gate_rows, 1, 2) * grad_rows_raw.astype(F32)).astype(BF16)
    up, down = expert_up[0], expert_down[0]

    def product(a, b, terms):
        return jnp.einsum(terms, a, b, preferred_element_type=F32)

    def halves(matrix, axis):
        low, high = jnp.split(matrix, 2, axis)
        return jnp.where(here == 0, low, high), jnp.where(here == 0, high, low)

    def scattered(value):
        return lax.psum_scatter(value, "tensor", scatter_dimension=2, tiled=True).astype(BF16)

    hidden = product(x_rows, up, "srd,df->srf")
    act_float, gelu_pull = jax.vjp(lambda v: jax.nn.gelu(v, approximate=True), hidden)
    act = act_float.astype(BF16)
    d_act = product(grad_rows, down, "srd,fd->srf")
    d_hidden = gelu_pull(d_act)[0].astype(BF16)
    q_rows = jnp.sum(act.astype(F32) * d_act, -1)
    if peers == 2:
        up_own, up_other = halves(up, 0)
        down_own, down_other = halves(down, 1)
        x_sent = product(d_hidden, up_other, "srf,df->srd").astype(BF16)
        x_got = swapped(x_sent)
        act_late, _ = lax.optimization_barrier((act, x_sent))
        x_own = product(d_hidden, up_own, "srf,df->srd")
        y_sent = product(act_late, down_other, "srf,fd->srd").astype(BF16)
        x_got, y_sent = lax.optimization_barrier((x_got, y_sent))
        back_x = swap_owners((x_own + x_got.astype(F32)).astype(BF16))
        y_got = swapped(y_sent)
        y_own = product(act_late, down_own, "srf,fd->srd")
        share_y = (y_own + y_got.astype(F32)).astype(BF16)
    else:
        back_x = swap_owners(scattered(product(d_hidden, up, "srf,df->srd")))
        share_y = scattered(product(act, down, "srf,fd->srd"))
    q_back = swap_owners(q_rows[:, None, :])
    grad_up = product(x_rows, d_hidden, "srd,srf->df")
    grad_down = product(act, grad_rows, "srf,srd->fd")
    back_x, grad_up, grad_down, share_y = lax.optimization_barrier(
        (back_x, grad_up, grad_down, share_y)
    )
    expert_dx = unpacked(back_x)
    q_part = jnp.sum(jnp.where(pick > 0, q_back[:, 0, :, None], 0.0), (0, 1))
    x_half = half(xhat2)
    gain_half = half(gains[1])
    grad_half = half(grad_act)
    router_half = half(w_router.T)
    sums = jnp.stack([q_part, jnp.sum(gain_half * expert_dx * x_half, -1)])
    sums = tensor_total(sums, F32)
    d_logits = (sums[0][:, None] * (onehot - probs)).astype(BF16)
    grad_router = dot(normed2, d_logits, TN)
    by_router = dot((xhat2 * gains[1]).astype(BF16), w_router)
    mean_term = (
        sums[1][:, None] + jnp.sum(d_logits.astype(F32) * by_router, -1, keepdims=True)
    ) / width
    d_normed2 = expert_dx + dot(d_logits, router_half)
    gain_grad2 = tensor_columns(jnp.sum(d_normed2 * x_half, 0, keepdims=True))[0]
    d_resid_half = grad_half + scale2 * (gain_half * d_normed2 - x_half * mean_term)

    d_mixed = tensor_columns(d_resid_half.astype(BF16))
    d_mixed, share_y = lax.optimization_barrier((d_mixed, share_y))
    expert_y = unpacked(swap_owners(share_y))
    act_half = (valid * (half(resid) + gate * expert_y)).astype(BF16)
    d_gated = dot(d_mixed, w_out, NT)
    d_y = d_gated * silu_z
    [start_grad] = call(
        start_grad_kernel,
        [both_in(delta), both_in(d_y), by_rows(c_vals), by_chan(rates)],
        [by_chan(out((N, seqs, chans)))],
        [wide_rates, (tokens, N * LANES)],
        cost=cost(length, 6),
    )
    d_gate_z = (d_gated * y_vals * gate_slope).astype(BF16)

    def owned(value):
        return lax.psum_scatter(value.astype(BF16), OWNERS, scatter_dimension=0, tiled=True)

    grad_end, act_others, early = carried(
        start_grad, log_decay, rates, -1, 1, act_half, (d_gate_z, normed1, gated, d_mixed)
    )
    mine_early = owned(early)
    w_step_wide = jnp.pad(w_step, ((0, 0), (0, LANES - R)))
    d_step, du_part, d_proj_part, rate_grad, bias_sums, skip_sums = call(
        backward_kernel,
        [
            both_in(delta),
            both_in(u_wide),
            both_in(d_y),
            (jax.nn.sigmoid(step_pre), (tokens, lane_width), "tc"),
            by_rows(b_vals),
            by_rows(c_vals),
            by_chan(rates),
            by_chan(skip[None]),
            (w_step_wide, (lane_width, LANES), "r"),
            by_chan(starts),
            by_chan(grad_end),
        ],
        [
            by_chan(out((tokens, chans), BF16)),
            by_chan(out((tokens, chans))),
            (out((tokens, LANES), BF16), (tokens, LANES), ""),
            by_chan(out((N, seqs, chans))),
            by_chan(out((seqs, chans))),
            by_chan(out((seqs, chans))),
        ],
        [
            wide_rates,
            (tokens, N * LANES),
            (tokens, N * LANES),
            (BLK + 1, N, seqs, lane_width),
            (BLK, N, seqs, lane_width),
            (BLK * seqs, N * LANES),
            (BLK * seqs, N * LANES),
            (BLK * seqs, lane_width),
            (tokens, LANES),
            pltpu.VMEM((2 * N * LANES, LANES), BF16),
        ],
        cost=cost(length, 24),
    )
    d_proj = tensor_total(d_proj_part, BF16).astype(BF16)
    step_bias_grad = jnp.sum(bias_sums, 0)
    skip_grad = jnp.sum(skip_sums, 0)
    w_x_wide = jnp.pad(w_x, ((0, 0), (0, LANES - x_cols)))
    rim_u = du_part[:rim] + dot(d_proj[:rim], w_x_wide, NT)
    after = moved(rim_u * silu_parts(conv[:rim])[1], -1)
    steps = length // 4
    block = steps * seqs
    turns = length // steps

    def from_end(value):
        return value, pl.BlockSpec((block, value.shape[1]), lambda i: (turns - 1 - i, 0))

    def whole(value):
        return value, pl.BlockSpec(value.shape, lambda i: (0, 0))

    arrays = [
        from_end(du_part),
        from_end(d_proj),
        from_end(conv),
        whole(extended),
        from_end(normed1),
        from_end(u),
        from_end(jnp.pad(rank, ((0, 0), (x_cols, LANES - x_cols - R)))),
        from_end(d_step),
        from_end(d_gate_z),
        (full, pl.BlockSpec((chans, width), lambda i: (0, 0))),
        (later_full, pl.BlockSpec((chans, width), lambda i: (0, 0))),
        whole(w_x_wide),
        whole(taps),
        whole(after),
    ]
    rows_each = narrow.shape[0]
    decay_grad = jnp.sum(rate_grad, 1) * rates
    fused = joined and peers == 2 and rows_each % 16 == 0 and owners >= 4 and VECTORS + 2 + experts <= LANES
    if fused:
        vectors = jnp.concatenate([skip_grad[None], decay_grad, step_bias_grad[None]], 0)
        vectors = jnp.pad(vectors, ((CONV_TAPS + 1, LANES - VECTORS), (0, 0)))
        routing_wide = jnp.pad(
            jnp.concatenate([grad_router, gain_grad2[:, None]], 1),
            ((0, 0), (VECTORS + 1, LANES - VECTORS - 2 - experts)),
        )

        def entire(value):
            return value, pl.BlockSpec(value.shape, lambda i: (0,) * value.ndim)

        arrays += [
            whole(x_tok),
            whole(d_mixed),
            whole(act_half),
            entire(act_others),
            whole(gains[:1]),
            whole(vectors),
            whole(routing_wide),
            whole(mine_early),
        ]
        cols = width + 2 * LANES
        results = [
            entire(out(inputs.shape)),
            entire(out(inputs.shape, BF16)),
            entire(out((2, rows_each, width))),
            *[
                whole(out((rows_each, count)))
                for count in (width, x_cols, R, VECTORS - 1, experts, LANES)
            ],
        ]
        sizes = (lax.axis_size("fsdp"), lax.axis_size("ctx"))
        stages = (owners - 1).bit_length()
        counts = [owners >> (stage + 1) for stage in range(stages)]
        (
            input_grad,
            activations,
            mine_in,
            mine_out,
            mine_x,
            mine_dt,
            mine_channel,
            mine_router,
            mine_tail,
        ) = pl.pallas_call(
            functools.partial(finish_kernel, (micros, group), sizes, turns),
            grid=(turns,),
            in_specs=[spec for _, spec in arrays],
            out_specs=[spec for _, spec in results],
            out_shape=[value for value, _ in results],
            scratch_shapes=[
                pltpu.VMEM((chans, width), F32),
                pltpu.VMEM((chans, LANES), F32),
                pltpu.VMEM(((CONV_TAPS + 1) * seqs, chans), F32),
                pltpu.VMEM((seqs, width), F32),
                pltpu.VMEM((block + rim, chans), F32),
                pltpu.VMEM((turns, block, width), BF16),
                pltpu.VMEM((turns, block, width), BF16),
                pltpu.VMEM((seqs, width), F32),
                pltpu.VMEM((chans, LANES), F32),
                pltpu.VMEM((width // LANES, block, LANES), F32),
                pltpu.VMEM((width // LANES, block, LANES), F32),
                pltpu.VMEM((rows_each, cols), F32),
                *[pltpu.VMEM((2, 2, count, rows_each, cols // 2), BF16) for count in counts],
                *[pltpu.VMEM((2, count, rows_each, cols // 2), BF16) for count in counts],
                pltpu.SemaphoreType.DMA((3,)),
                pltpu.SemaphoreType.DMA((3,)),
                pltpu.SemaphoreType.DMA((1,)),
                pltpu.SemaphoreType.DMA((1,)),
                pltpu.SemaphoreType.DMA((stages, 2)),
                pltpu.SemaphoreType.DMA((stages, 2)),
            ],
            compiler_params=pltpu.CompilerParams(
                collective_id=3, has_side_effects=True, vmem_limit_bytes=63 << 20
            ),
        )(*[value for value, _ in arrays])
        mine_bias = mine_tail[:, VECTORS - 1]
        gains_out = jnp.stack([mine_tail[:, VECTORS], mine_tail[:, VECTORS + 1 + experts]])
        return (
            activations,
            input_grad,
            gains_out,
            mine_router,
            mine_in,
            mine_x,
            mine_dt,
            mine_bias,
            mine_channel,
            mine_out,
            grad_up[None],
            grad_down[None],
        )
    arrays.append(from_end(x_tok))
    results = [
        (
            out((tokens // 2, width), BF16),
            pl.BlockSpec((block, width), lambda i: (jnp.maximum(turns // 2 - 1 - i, 0), 0)),
        ),
        (
            out((tokens // 2, width), BF16),
            pl.BlockSpec(
                (block, width), lambda i: (jnp.minimum(turns - 1 - i, turns // 2 - 1), 0)
            ),
        ),
        whole(out((chans, width))),
        whole(out((chans, LANES))),
        whole(out(((CONV_TAPS + 1) * seqs, chans))),
        whole(out((seqs, width))),
    ]
    late_part, early_part, grad_in, narrow_sums, conv_sums, gain_sums = pl.pallas_call(
        functools.partial(inner_grad_kernel, seqs),
        grid=(turns,),
        in_specs=[spec for _, spec in arrays],
        out_specs=[spec for _, spec in results],
        out_shape=[value for value, _ in results],
        scratch_shapes=[pltpu.VMEM((block + rim, chans), F32)],
        compiler_params=pltpu.CompilerParams(vmem_limit_bytes=62 << 20),
    )(*[value for value, _ in arrays])
    late_part, mine_early = lax.optimization_barrier((late_part, mine_early))
    grad_xproj, grad_dt = narrow_sums[:, :x_cols], narrow_sums[:, x_cols : x_cols + R]
    conv_sums = jnp.sum(conv_sums.reshape(CONV_TAPS + 1, seqs, chans), 1)
    gain_grad1 = jnp.sum(gain_sums, 0)

    narrow_grads = jnp.concatenate(
        [
            grad_xproj,
            grad_dt,
            conv_sums.T,
            skip_grad[:, None],
            decay_grad.T,
            step_bias_grad[:, None],
        ],
        1,
    )
    routing_grads = jnp.concatenate([grad_router, gain_grad1[:, None], gain_grad2[:, None]], 1)
    if joined:
        narrow_grads = jnp.concatenate([narrow_grads, routing_grads], 1)
    wide_grads = jnp.concatenate(
        [grad_in, jnp.pad(narrow_grads, ((0, 0), (0, pad)))], 1
    )

    halves = [late_part, early_part]
    if peers == 2:
        exchanged = [swapped(part) for part in halves]
    else:
        exchanged = [lax.all_gather(part, "tensor") for part in halves]
    mine, exchanged = halved(wide_grads, exchanged)
    normed_parts = []
    for own, others in zip(halves, exchanged):
        if peers == 2:
            normed_parts.append([own, others])
        else:
            normed_parts.append([others[k] for k in range(peers)])
    late_parts, early_parts = normed_parts

    def rows_of(value):
        return value, pl.BlockSpec((block, value.shape[1]), lambda i: (i, 0))

    def early_rows(value):
        return value, pl.BlockSpec((block, width), lambda i: (jnp.minimum(i, turns // 2 - 1), 0))

    def late_rows(value):
        return value, pl.BlockSpec((block, width), lambda i: (jnp.maximum(i - turns // 2, 0), 0))

    arrays = (
        [early_rows(part) for part in early_parts]
        + [late_rows(part) for part in late_parts]
        + [
            rows_of(x_tok),
            rows_of(d_mixed),
            rows_of(act_half),
            (act_others, pl.BlockSpec((peers - 1, block, share), lambda i: (0, i, 0))),
            whole(gains[:1]),
        ]
    )
    out_spec = pl.BlockSpec((micros, group, steps, width), lambda i: (0, 0, i, 0))
    input_grad, activations = pl.pallas_call(
        functools.partial(output_kernel, (micros, group), peers),
        grid=(turns,),
        in_specs=[spec for _, spec in arrays],
        out_specs=[out_spec, out_spec],
        out_shape=[out(inputs.shape), out(inputs.shape, BF16)],
        scratch_shapes=[pltpu.VMEM((width // LANES, block, LANES), F32)] * 2,
        compiler_params=pltpu.CompilerParams(vmem_limit_bytes=62 << 20),
    )(*[value for value, _ in arrays])
    mine_tail = mine[:, width:]
    if joined:
        mine_routing = mine_tail[:, cuts[2] + 1 : cuts[2] + 1 + routing.shape[1]]
    else:
        mine_routing, _ = halved(routing_grads)
    gains_out = jnp.stack(
        [tensor_total(mine_routing[None, :, experts], F32)[0], mine_routing[:, experts + 1]]
    )
    return (
        activations,
        input_grad,
        gains_out,
        mine_routing[:, :experts],
        jnp.stack([mine[:, :width], mine_early[:, :width].astype(F32)]),
        mine_tail[:, : cuts[0]],
        mine_tail[:, cuts[0] : cuts[1]],
        mine_tail[:, cuts[2]],
        mine_tail[:, cuts[1] : cuts[2]],
        mine_early[:, width:].astype(F32),
        grad_up[None],
        grad_down[None],
    )


def solution(mesh):
    return jax.shard_map(
        per_device,
        mesh=mesh,
        in_specs=(
            P(None, "fsdp", "ctx", None),
            P(None, "fsdp", "ctx", None),
            P(None, "fsdp"),
            P(None, "fsdp", "ctx"),
            P(None, "fsdp", "ctx"),
            P(None, ("fsdp", "ctx")),
            P(("fsdp", "ctx"), None),
            P(None, ("fsdp", "ctx", "tensor"), None),
            P(("fsdp", "ctx", "tensor"), None),
            P(("fsdp", "ctx", "tensor"), None),
            P(("fsdp", "ctx", "tensor")),
            P(("fsdp", "ctx", "tensor"), None),
            P(("fsdp", "ctx", "tensor"), None),
            P(("fsdp", "ctx"), None, "tensor"),
            P(("fsdp", "ctx"), "tensor", None),
        ),
        out_specs=(
            P(None, "fsdp", "ctx", None),
            P(None, "fsdp", "ctx", None),
            P(None, ("fsdp", "ctx")),
            P(("fsdp", "ctx"), None),
            P(None, ("fsdp", "ctx", "tensor"), None),
            P(("fsdp", "ctx", "tensor"), None),
            P(("fsdp", "ctx", "tensor"), None),
            P(("fsdp", "ctx", "tensor")),
            P(("fsdp", "ctx", "tensor"), None),
            P(("fsdp", "ctx", "tensor"), None),
            P(("fsdp", "ctx"), None, "tensor"),
            P(("fsdp", "ctx"), "tensor", None),
        ),
        check_vma=False,
    )
```
